32 devices in a mesh: dp: 8 (over y, x, core), ffn: 4 (over z).
Axes of the slice: x: 2, y: 2, z: 4, core: 2. Of those that a mesh axis runs over, the one named last changes fastest.
Arguments:
- tokens: bfloat16 [49152, 768], P(('dp', 'ffn')), may hold values from -6 to 6
- lengths: int32 [96], P(('dp', 'ffn')), may hold values from 32 to 512, as said below
- qkv_weight: bfloat16 [2304, 192], P(('dp', 'ffn')), may hold values from -0.4375 to 0.4375
- out_weight: bfloat16 [768, 768], P(('dp', 'ffn')), may hold values from -0.875 to 0.875
- ffn_in_weight: bfloat16 [4, 192, 768], P(None, 'dp', 'ffn'), may hold values from -0.4375 to 0.4375
- ffn_out_weight: bfloat16 [4, 768, 192], P(None, 'ffn', 'dp'), may hold values from -0.21875 to 0.21875
- biases: bfloat16 [10, 768], P(None, ('dp', 'ffn')), may hold values from -3 to 3
- gains: bfloat16 [2, 768], P(None, ('dp', 'ffn')), may hold values from 0.5 to 1.5
- cotangent: bfloat16 [49152, 768], P(('dp', 'ffn')), may hold values from -6 to 6
Outputs:
- output: bfloat16 [49152, 768], P(('dp', 'ffn'))
- grad_tokens: bfloat16 [49152, 768], P(('dp', 'ffn'))
- grad_qkv_weight: float32 [2304, 192], P(('dp', 'ffn'))
- grad_out_weight: float32 [768, 768], P(('dp', 'ffn'))
- grad_ffn_in_weight: float32 [4, 192, 768], P(None, 'dp', 'ffn')
- grad_ffn_out_weight: float32 [4, 768, 192], P(None, 'ffn', 'dp')
- grad_biases: float32 [10, 768], P(None, ('dp', 'ffn'))
- grad_gains: float32 [2, 768], P(None, ('dp', 'ffn'))
The draws below stay inside these ranges and needn't reach their ends.
Inputs may be any that keep to these rules, and one draw needn't show every extreme that they name: `lengths`: one slot of the whole batch holds a sequence of the full 512 positions.
All inputs are finite; a program needn't handle non-finite values.
Results may differ from the reference program's by a relative error of at most 0.017.
Values may be sent and summed in bfloat16 or wider, within the bound.
A program may use at most 320 MiB of HBM per device.

```python
import jax
import jax.numpy as jnp
from jax import lax

D = 768
HEADS = 12
HEAD_DIM = 64
GROUPS = 4
SLOT_LEN = 512
MIN_LEN = 32
GROUP_WIDTH = 192
GROUP_UNITS = 768
SLOTS = 96
TOKENS = 49152


def draw_lengths(key, part):
    key = jax.random.fold_in(key, 7)
    first_key, second_key = jax.random.split(key)
    drawn = jax.random.randint(first_key, (SLOTS,), MIN_LEN, SLOT_LEN + 1)
    chosen = jax.random.randint(second_key, (), 0, SLOTS)
    return jnp.where(jnp.arange(SLOTS) == chosen, SLOT_LEN, drawn).astype(jnp.int32)


def level_of(own_key, extent, cuts, smallest, largest):
    def one(axis_at, parts):
        steps = jax.random.uniform(jax.random.fold_in(jax.random.fold_in(own_key, 6), axis_at), (parts,), jnp.float32, smallest / len(cuts), largest / len(cuts))
        return jnp.repeat(jnp.exp(steps), extent[axis_at] // parts).reshape((-1,) + (1,) * (len(extent) - axis_at - 1))

    level = one(*cuts[0])
    for cut in cuts[1:]:
        level = level * one(*cut)
    return level


def gaussian(key, dims, spread, most, pieces=(), kind=jnp.bfloat16):
    values = spread * jax.random.normal(key, dims, jnp.float32)
    if pieces:
        values = values * level_of(key, dims, pieces, -0.22, 0.18)
    return jnp.clip(values, -most, most).astype(kind)


def setup_inputs(seed: int = 0) -> dict:
    streams_of = jax.random.split(jax.random.key(seed), 10)
    return {
        "tokens": gaussian(streams_of[0], (TOKENS, D), 1.0, 6.0, ((0, 32),)),
        "lengths": draw_lengths(jax.random.fold_in(streams_of[9], 71), 0),
        "qkv_weight": gaussian(streams_of[2], (3 * D, GROUP_WIDTH), GROUP_WIDTH ** -0.5, 0.4375, ((0, 32),)),
        "out_weight": gaussian(streams_of[3], (D, D), (D // 16) ** -0.5, 0.875, ((0, 32),)),
        "ffn_in_weight": gaussian(streams_of[4], (GROUPS, GROUP_WIDTH, GROUP_UNITS), GROUP_WIDTH ** -0.5, 0.4375, ((1, 8), (2, 4))),
        "ffn_out_weight": gaussian(streams_of[5], (GROUPS, GROUP_UNITS, GROUP_WIDTH), GROUP_UNITS ** -0.5, 0.21875, ((1, 4), (2, 8))),
        "biases": gaussian(streams_of[6], (GROUPS + 6, D), 0.5, 3.0, ((1, 32),)),
        "gains": jnp.clip(1.0 + 0.1 * jax.random.normal(streams_of[7], (2, D), jnp.float32), 0.5, 1.5).astype(jnp.bfloat16),
        "cotangent": gaussian(streams_of[8], (TOKENS, D), 1.0, 6.0, ((0, 32),)),
    }


PRECISE = lax.Precision.HIGHEST
EPSILON = 1e-12
NEGATIVE = -1e+30

@jax.custom_vjp
def low(v):
    return lax.optimization_barrier(v.astype(jnp.bfloat16)).astype(jnp.float32)

@jax.custom_vjp
def low_back(v):
    return v

def low_keep(v):
    return (low(v), None)

def low_pass(kept, grad):
    return (grad,)

def back_keep(v):
    return (v, None)

def back_low(kept, grad):
    return (low(grad),)
low.defvjp(low_keep, low_pass)
low_back.defvjp(back_keep, back_low)

def both_ways(values):
    return low(low_back(values))

def grouped(values, weight):
    count = values.shape[0]
    split = values.reshape(count, weight.shape[0], weight.shape[1])
    return jnp.einsum('ngi,gio->ngo', split, weight, precision=PRECISE).reshape(count, -1)

def normalize(residual, gain_row, offset_row):
    centre = residual - lax.optimization_barrier(jnp.mean(residual, axis=-1, keepdims=True))
    inverse = lax.rsqrt(lax.optimization_barrier(jnp.mean(centre * centre, axis=-1, keepdims=True)) + EPSILON)
    return centre * inverse * gain_row + offset_row

def layer_block(parameters, inputs, lengths):
    qkv_weight, out_weight, ffn_in_weight, ffn_out_weight, biases, gains = parameters
    model_width = inputs.shape[1]
    group_width = model_width // GROUPS
    projections = qkv_weight.reshape(3, GROUPS, group_width, group_width)
    query = both_ways(grouped(inputs, projections[0]) + biases[GROUPS])
    keys = both_ways(grouped(inputs, projections[1]))
    values = both_ways(grouped(inputs, projections[2]) + biases[GROUPS + 1])
    slot_count = lengths.shape[0]
    positions = jnp.arange(SLOT_LEN)
    score_scale = HEAD_DIM ** (-0.5)

    def split_heads(array):
        return array.reshape(slot_count, SLOT_LEN, HEADS, HEAD_DIM)

    def attend(packed):
        query_slot, key_slot, value_slot, length = packed
        raw_scores = low_back(score_scale * jnp.einsum('qhd,khd->hqk', query_slot, key_slot, precision=PRECISE))
        masked = jnp.where((positions < length)[None, None, :], raw_scores, NEGATIVE)
        probabilities = low(jax.nn.softmax(masked, axis=-1))
        mixed = jnp.einsum('hqk,khd->qhd', probabilities, value_slot, precision=PRECISE)
        return mixed.reshape(SLOT_LEN, model_width)
    context = lax.map(jax.checkpoint(attend), (split_heads(query), split_heads(keys), split_heads(values), lengths))
    context = both_ways(context.reshape(-1, model_width))
    attn_out = low_back(jnp.dot(context, out_weight, precision=PRECISE) + biases[GROUPS + 2])
    first_norm = normalize(inputs + attn_out, gains[0], biases[GROUPS + 3])
    pre_act = low_back(grouped(low(first_norm), ffn_in_weight) + biases[:GROUPS].reshape(-1))
    activation = low(jax.nn.gelu(pre_act, approximate=False))
    ffn_branch = low_back(grouped(activation, ffn_out_weight) + biases[GROUPS + 4])
    return normalize(first_norm + ffn_branch, gains[1], biases[GROUPS + 5])

def reference(tokens, lengths, qkv_weight, out_weight, ffn_in_weight, ffn_out_weight, biases, gains, cotangent):
    parameters = tuple((array.astype(jnp.float32) for array in (qkv_weight, out_weight, ffn_in_weight, ffn_out_weight, biases, gains)))
    inputs = tokens.astype(jnp.float32)
    model_width = inputs.shape[1]
    block_slots = 8
    block_count = lengths.shape[0] // block_slots
    block_lengths = lengths.reshape(block_count, block_slots)

    def whole_layer(weights_all, layer_input):
        blocked = layer_input.reshape(block_count, block_slots * SLOT_LEN, model_width)

        def scan_step(carried, packed):
            return (carried, jax.checkpoint(layer_block)(weights_all, packed[0], packed[1]))
        carried, outputs = lax.scan(scan_step, jnp.float32(0.0), (blocked, block_lengths))
        return outputs.reshape(-1, model_width)
    output, pullback = jax.vjp(whole_layer, parameters, inputs)
    grad_params, grad_inputs = pullback(cotangent.astype(jnp.float32))
    return (output.astype(jnp.bfloat16), grad_inputs.astype(jnp.bfloat16), grad_params[0], grad_params[1], grad_params[2], grad_params[3], grad_params[4], grad_params[5])
```

```python
import functools
import jax
import jax.numpy as jnp
from jax import lax
from jax.sharding import PartitionSpec as P
from jax.experimental import pallas as pl
from jax.experimental.pallas import tpu as pltpu
f32=jnp.float32; bf=jnp.bfloat16
EPS=1e-12; NEG=-1e30
SL=512; D=768
def dg(a,b,ca,cb): return lax.dot_general(a,b,(((ca,),(cb,)),((),())),preferred_element_type=f32)
def nn(a,b): return dg(a,b,1,0)
def nt(a,b): return dg(a,b,1,1)
def tn(a,b): return dg(a,b,0,0)

def gelu_pair(u):
    x=jnp.abs(u)
    d=1.0+(0.3275911*0.7071067811865476)*x
    t=pl.reciprocal(d,approx=True)
    t=t*(2.0-d*t)
    e=jnp.exp((-0.5)*(u*u))
    q=t*(0.5*0.254829592+t*(0.5*-0.284496736+t*(0.5*1.421413741+t*(0.5*-1.453152027+t*(0.5*1.061405429)))))
    h=q*e
    c=jnp.where(u>=0,1.0-h,h)
    return u*c, c+(0.3989422804014327*u)*e

def qkv_phase(tok,w,bias,Q,K,V,s):
    rows=pl.ds(pl.multiple_of(s*SL,SL),SL)
    for S in range(2):
        b=384*S
        y0=nn(tok[rows,b:b+256],w[2*S]); y1=nn(tok[rows,b+128:b+384],w[2*S+1])
        for part,(dst,brow,sc) in enumerate(((Q,4,0.125),(K,None,None),(V,5,None))):
            c=256*part
            tiles=(y0[:,c:c+128],y0[:,c+128:c+256]+y1[:,c:c+128],y1[:,c+128:c+256])
            for i,t in enumerate(tiles):
                l=b+128*i
                if brow is not None: t=t+bias[brow:brow+1,l:l+128]
                t=t.astype(bf)
                if sc is not None: t=t*jnp.asarray(sc,bf)
                dst[rows,l:l+128]=t

def halves(t):
    lane=lax.broadcasted_iota(jnp.int32,t.shape,1)
    z=jnp.zeros_like(t)
    return jnp.where(lane<64,t,z),jnp.where(lane<64,z,t)

def attn_fwd(Q,K,V,P,CTX,maskrow,s,p):
    rows=pl.ds(pl.multiple_of(s*SL,SL),SL); cols=pl.ds(pl.multiple_of(p*128,128),128)
    q,k,v=Q[rows,cols],K[rows,cols],V[rows,cols]
    qs=halves(q); vs=halves(v)
    ones=jnp.ones((SL,128),bf); on=halves(ones)
    r=None
    for h in range(2):
        sc=nt(qs[h],k)+maskrow
        m=jnp.max(sc,axis=1,keepdims=True)
        e=jnp.exp(sc-m)
        l=jnp.sum(e,axis=1,keepdims=True)
        pb=(e*(1.0/l)).astype(bf)
        P[s*12+2*p+h]=pb
        c=nn(pb,vs[h])
        r=c if r is None else r+c
    CTX[rows,cols]=r

def attn_bwd(Q,K,V,P,CTX,DC,s,p):
    rows=pl.ds(pl.multiple_of(s*SL,SL),SL); cols=pl.ds(pl.multiple_of(p*128,128),128)
    q,k,v,dc=Q[rows,cols],K[rows,cols],V[rows,cols],DC[rows,cols]
    dcs=halves(dc); ks=halves(k)
    prod=dc.astype(f32)*CTX[rows,cols]
    prods=halves(prod)
    dq=None; dkT=[]; dvT=[]
    for h in range(2):
        delta=jnp.sum(prods[h],axis=1,keepdims=True)
        pb=P[s*12+2*p+h]
        dp=nt(dcs[h],v)-delta
        ds=(pb.astype(f32)*dp).astype(bf)
        c=nn(ds,ks[h])
        dq=c if dq is None else dq+c
        dkT.append(tn(q,ds)[64*h:64*h+64]); dvT.append(tn(dc,pb)[64*h:64*h+64])
    Q[rows,cols]=(dq*0.125).astype(bf)
    K[rows,cols]=jnp.concatenate(dkT,0).T.astype(bf)
    V[rows,cols]=jnp.concatenate(dvT,0).T.astype(bf)

def ln_fwd(r):
    mean=jnp.sum(r,axis=1,keepdims=True)*(1.0/D)
    c=r-mean
    var=jnp.sum(c*c,axis=1,keepdims=True)*(1.0/D)
    inv=lax.rsqrt(var+EPS)
    return c*inv,inv
def ln_bwd(gy,xh,inv,gamma):
    e=gy*gamma
    me=jnp.sum(e,axis=1,keepdims=True)*(1.0/D)
    mx=jnp.sum(e*xh,axis=1,keepdims=True)*(1.0/D)
    return inv*(e-me-xh*mx)
def win(g): return 128*((192*g)//128)

def mid_phase(R,i,tok,cot,wo,win_,wout,bias,gain,CTX,DC,DR,out,gin,gout,gwo,gb,gg,AB,SLP,XH,H1B,F):
    rows=pl.ds(pl.multiple_of(i*R,R),R)
    ctxb=CTX[rows,:].astype(bf)
    r1=nn(ctxb,wo[...])+bias[6:7,:]+tok[rows,:].astype(f32)
    xh1,inv1=ln_fwd(r1)
    XH[...]=xh1
    h1=xh1*gain[0:1,:]+bias[7:8,:]
    H1B[...]=h1.astype(bf)
    F[...]=h1+bias[8:9,:]
    def fwd_g(g):
        w0=win(g)
        u=nn(H1B[:,w0:w0+256],win_[g])+bias[g:g+1,:]
        a,sl=gelu_pair(u)
        ab=a.astype(bf)
        AB[g]=ab; SLP[g]=sl.astype(bf)
        F[:,w0:w0+256]+=nt(ab,wout[g])
    for g in range(4): fwd_g(g)
    xh2,inv2=ln_fwd(F[...])
    out[rows,:]=(xh2*gain[1:2,:]+bias[9:10,:]).astype(bf)
    gy=cot[rows,:].astype(f32)
    gg[1:2,:]+=jnp.sum(gy*xh2,axis=0,keepdims=True)
    gb[9:10,:]+=jnp.sum(gy,axis=0,keepdims=True)
    dr2=ln_bwd(gy,xh2,inv2,gain[1:2,:])
    dfb=dr2.astype(bf)
    gb[8:9,:]+=jnp.sum(dfb.astype(f32),axis=0,keepdims=True)
    F[...]=dr2
    for g in range(4):
        w0=win(g); off=64*(g%2)
        dfw=dfb[:,w0:w0+256]
        dact=nn(dfw,wout[g])
        dub=(dact*SLP[g].astype(f32)).astype(bf)
        F[:,w0:w0+256]+=nt(dub,win_[g])
        gb[g:g+1,:]+=jnp.sum(dub.astype(f32),axis=0,keepdims=True)
        gin[g]+=tn(H1B[:,w0:w0+256],dub)[off:off+192]
        gout[g]+=tn(dfw,AB[g])[off:off+192]
    xh1=XH[...]
    dh1=F[...]
    gg[0:1,:]+=jnp.sum(dh1*xh1,axis=0,keepdims=True)
    gb[7:8,:]+=jnp.sum(dh1,axis=0,keepdims=True)
    dr1=ln_bwd(dh1,xh1,inv1,gain[0:1,:])
    dab=dr1.astype(bf)
    DR[rows,:]=dab
    gb[6:7,:]+=jnp.sum(dab.astype(f32),axis=0,keepdims=True)
    gwo[...]+=tn(ctxb,dab)
    DC[rows,:]=nt(dab,wo[...]).astype(bf)

def tail_phase(tok,w,Q,K,V,DR,gx,gqkv,gb,s):
    rows=pl.ds(pl.multiple_of(s*SL,SL),SL)
    for S in range(2):
        b=384*S; ys=[]
        for j in range(2):
            g=2*S+j; w0=win(g); off=64*j
            dcat=jnp.concatenate([Q[rows,w0:w0+256],K[rows,w0:w0+256],V[rows,w0:w0+256]],axis=1)
            gqkv[g]+=tn(tok[rows,w0:w0+256],dcat)[off:off+192]
            ys.append(nt(dcat,w[g]))
        for i in range(3):
            t=(ys[0][:,:128],ys[0][:,128:]+ys[1][:,:128],ys[1][:,128:])[i]
            l=b+128*i
            gx[rows,l:l+128]=(t+DR[rows,l:l+128].astype(f32)).astype(bf)
    gb[4:5,:]+=jnp.sum(Q[rows,:].astype(f32),axis=0,keepdims=True)
    gb[5:6,:]+=jnp.sum(V[rows,:].astype(f32),axis=0,keepdims=True)

def kernel(R,phases,len_ref,tok,cot_hbm,wqkv,wo,win_,wout,bias,gain,out,gx,gqkv,gwo,gin,gout,gb,gg,Q,K,V,P,CTX,DC,sem,AB,SLP,XH,H1B,F):
    n=tok.shape[0]//SL
    DR=gx; cot=DC
    cp=pltpu.make_async_copy(cot_hbm,DC,sem); cp.start(); cp.wait()
    if 0 in phases:
        for r in (gqkv,gwo,gin,gout,gb,gg): r[...]=jnp.zeros_like(r)
        lax.fori_loop(0,n,lambda s,c:(qkv_phase(tok,wqkv,bias,Q,K,V,s),c)[1],0)
    if 1 in phases:
        def f(i,c):
            s=i//6
            lane=lax.broadcasted_iota(jnp.int32,(1,SL),1)
            mrow=jnp.where(lane<len_ref[s],0.0,NEG)
            attn_fwd(Q,K,V,P,CTX,mrow,s,i%6); return c
        lax.fori_loop(0,n*6,f,0)
    if 2 in phases:
        lax.fori_loop(0,tok.shape[0]//R,lambda i,c:(mid_phase(R,i,tok,cot,wo,win_,wout,bias,gain,CTX,DC,DR,out,gin,gout,gwo,gb,gg,AB,SLP,XH,H1B,F),c)[1],0)
    if 3 in phases:
        lax.fori_loop(0,n*6,lambda i,c:(attn_bwd(Q,K,V,P,CTX,DC,i//6,i%6),c)[1],0)
    if 4 in phases:
        lax.fori_loop(0,n,lambda s,c:(tail_phase(tok,wqkv,Q,K,V,DR,gx,gqkv,gb,s),c)[1],0)

def main_call(lengths,tok,cot,wqkv,wo,win_,wout,bias,gain,R=256,phases=(0,1,2,3,4)):
    n=tok.shape[0]; s=n//SL
    vm=pl.BlockSpec(memory_space=pltpu.VMEM)
    sd=jax.ShapeDtypeStruct
    return pl.pallas_call(functools.partial(kernel,R,phases),
      out_shape=(sd((n,D),bf),sd((n,D),bf),sd((4,192,768),f32),sd((D,D),f32),sd((4,192,768),f32),sd((4,192,768),f32),sd((16,D),f32),sd((8,D),f32)),
      in_specs=[pl.BlockSpec(memory_space=pltpu.SMEM),vm,pl.BlockSpec(memory_space=pl.ANY)]+[vm]*6,out_specs=(vm,)*8,
      scratch_shapes=[pltpu.VMEM((n,D),bf)]*3+[pltpu.VMEM((s*12,SL,SL),bf),pltpu.VMEM((n,D),f32),pltpu.VMEM((n,D),bf),pltpu.SemaphoreType.DMA,
        pltpu.VMEM((4,R,768),bf),pltpu.VMEM((4,R,768),bf),pltpu.VMEM((R,D),f32),pltpu.VMEM((R,D),bf),pltpu.VMEM((R,D),f32)],
      compiler_params=pltpu.CompilerParams(vmem_limit_bytes=63<<20))(lengths,tok,cot,wqkv,wo,win_,wout,bias,gain)


MESH = pl.DeviceIdType.MESH


def place():
    dp = lax.axis_index("dp")
    return lax.rem(dp, 2), lax.div(dp, 2), lax.axis_index("ffn")


def peers(nq, nf):
    c, q, f = place()
    by_f = [(2 * q + c, lax.rem(f + k, nf)) for k in range(1, nf)]
    by_q = [(2 * lax.rem(q + k, nq) + c, f) for k in range(1, nq)]
    return by_f, by_q, (2 * q + 1 - c, f)


def greet(nq, nf):
    by_f, by_q, twin = peers(nq, nf)
    everyone = by_f + by_q + [twin]
    barrier = pltpu.get_barrier_semaphore()
    for peer in everyone:
        pl.semaphore_signal(barrier, inc=1, device_id=peer, device_id_type=MESH)
    pl.semaphore_wait(barrier, len(everyone))


def send(src, dst, send_sem, recv_sem, peer):
    copy = pltpu.make_async_remote_copy(
        src_ref=src, dst_ref=dst, send_sem=send_sem, recv_sem=recv_sem,
        device_id=peer, device_id_type=MESH)
    copy.start()
    return copy


def gather_kernel(nq, nf, count, *refs):
    mine, full = refs[:count], refs[count:2 * count]
    send_sem, recv_sem = refs[2 * count:]
    c, q, f = place()
    by_f, by_q, twin = peers(nq, nf)
    for m, g in zip(mine, full):
        g[c, q, f] = m[...]
    greet(nq, nf)
    started = []
    slot = 0

    def stage(at, targets):
        nonlocal slot
        copies = []
        for g in full:
            for peer in targets:
                copies.append(send(at(g), at(g), send_sem.at[slot], recv_sem.at[slot], peer))
                slot += 1
        for copy in copies:
            copy.wait_recv()
        started.extend(copies)

    stage(lambda g: g.at[c, q, f], by_f)
    stage(lambda g: g.at[c, q], by_q)
    stage(lambda g: g.at[c], [twin])
    for copy in started:
        copy.wait_send()


def gather_all(pieces, nq, nf):
    vm = pl.BlockSpec(memory_space=pltpu.VMEM)
    copies = len(pieces) * (nf + nq - 1)
    return pl.pallas_call(
        functools.partial(gather_kernel, nq, nf, len(pieces)),
        out_shape=tuple(jax.ShapeDtypeStruct((2, nq, nf) + p.shape, p.dtype) for p in pieces),
        in_specs=[vm] * len(pieces), out_specs=(vm,) * len(pieces),
        scratch_shapes=[pltpu.SemaphoreType.DMA((copies,)), pltpu.SemaphoreType.DMA((copies,))],
        compiler_params=pltpu.CompilerParams(
            collective_id=0, has_side_effects=True, vmem_limit_bytes=40 << 20),
    )(*pieces)


def scatter_kernel(nq, nf, count, *refs):
    x = refs[:count]
    out = refs[count:2 * count]
    rc, y, rp, z, rf = (refs[(2 + i) * count:(3 + i) * count] for i in range(5))
    send_sem, recv_sem = refs[7 * count:]
    c, q, f = place()
    by_f, by_q, twin = peers(nq, nf)
    greet(nq, nf)
    started = []
    slot = 0

    def go(src, dst, peer):
        nonlocal slot
        copy = send(src, dst, send_sem.at[slot], recv_sem.at[slot], peer)
        slot += 1
        started.append(copy)
        return copy

    first = [go(x[i].at[1 - c], rc[i], twin) for i in range(count)]
    second = []
    for i in range(count):
        first[i].wait_recv()
        y[i][...] = (x[i][c].astype(f32) + rc[i][...].astype(f32)).astype(bf)
        second.append([go(y[i].at[lax.rem(q + k, nq)], rp[i].at[k - 1], by_q[k - 1]) for k in range(1, nq)])
    third = []
    for i in range(count):
        total = y[i][q].astype(f32)
        for k in range(1, nq):
            second[i][k - 1].wait_recv()
            total = total + rp[i][k - 1].astype(f32)
        z[i][...] = total.astype(bf)
        third.append([go(z[i].at[lax.rem(f + k, nf)], rf[i].at[k - 1], by_f[k - 1]) for k in range(1, nf)])
    for i in range(count):
        total = z[i][f].astype(f32)
        for k in range(1, nf):
            third[i][k - 1].wait_recv()
            total = total + rf[i][k - 1].astype(f32)
        out[i][...] = total
    for copy in started:
        copy.wait_send()


def scatter_sum(arrays, nq, nf):
    vm = pl.BlockSpec(memory_space=pltpu.VMEM)
    count = len(arrays)
    tails = [a.shape[3:] for a in arrays]
    copies = count * (nf + nq - 1)
    scratch = []
    for lead in ((nq, nf), (nq, nf), (nq - 1, nf), (nf,), (nf - 1,)):
        scratch += [pltpu.VMEM(lead + t, bf) for t in tails]
    return pl.pallas_call(
        functools.partial(scatter_kernel, nq, nf, count),
        out_shape=tuple(jax.ShapeDtypeStruct(t, f32) for t in tails),
        in_specs=[vm] * count, out_specs=(vm,) * count,
        scratch_shapes=scratch + [pltpu.SemaphoreType.DMA((copies,)), pltpu.SemaphoreType.DMA((copies,))],
        compiler_params=pltpu.CompilerParams(
            collective_id=1, has_side_effects=True, vmem_limit_bytes=60 << 20),
    )(*arrays)


def on_device(nq, nf, tokens, lengths, qkv_weight, out_weight, ffn_in_weight, ffn_out_weight, biases, gains, cotangent):
    n = 2 * nq * nf
    r = D // n
    a, b = ffn_in_weight.shape[1:]
    q_piece = jnp.concatenate(
        [qkv_weight.reshape(3, r, 192).transpose(1, 0, 2).reshape(r, 576),
         biases.T, gains.T, jnp.zeros((r, 52), bf)], axis=1)
    i_piece = ffn_in_weight.transpose(1, 0, 2).reshape(a, 4 * b)
    t_piece = ffn_out_weight.transpose(2, 0, 1).reshape(a, 4 * b)
    gq, go, gi = gather_all((q_piece, out_weight, jnp.stack([i_piece, t_piece])), nq, nf)

    def by_device(g):
        return jnp.swapaxes(g, 0, 1).reshape((n,) + g.shape[3:])

    gq = by_device(gq)
    qkv = gq[:, :, :576].reshape(n, r, 3, 192).transpose(0, 2, 1, 3).reshape(3 * D, 192)
    small = gq[:, :, 576:588].reshape(D, 12).T
    wo = by_device(go).reshape(D, D)
    gi = jnp.swapaxes(gi, 0, 1).reshape(2 * nq, nf, 2, a, 4, b).transpose(2, 4, 0, 3, 1, 5).reshape(2, 4, 192, 768)
    zero = jnp.zeros((4, 256, 768), bf)
    we, wi, wt = zero, zero, zero
    pr = qkv.reshape(3, 4, 192, 192)
    for g in range(4):
        o = 64 * (g % 2)
        for p in range(3):
            we = we.at[g, o:o + 192, 256 * p + o:256 * p + o + 192].set(pr[p, g])
        wi = wi.at[g, o:o + 192].set(gi[0, g])
        wt = wt.at[g, o:o + 192].set(gi[1, g])
    bias = jnp.pad(small[:10].astype(f32), ((0, 6), (0, 0)))
    gain = jnp.pad(small[10:].astype(f32), ((0, 6), (0, 0)))
    out, gx, gqkv, gwo, gin, gout, gb, gg = main_call(lengths, tokens, cotangent, we, wo, wi, wt, bias, gain)
    gq = jnp.stack([jnp.stack([gqkv[g][:, 256 * p + 64 * (g % 2):256 * p + 64 * (g % 2) + 192] for g in range(4)]) for p in range(3)])
    gq = gq.reshape(n, 3, r, 192).transpose(0, 2, 1, 3).reshape(n, r, 576)
    rows = jnp.concatenate([gb[:10], gg[:2]]).T.reshape(n, r, 12)
    gq = jnp.concatenate([gq, rows, jnp.zeros((n, r, 52), f32)], axis=2).astype(bf)

    def to_chunks(x):
        return jnp.swapaxes(x.reshape((nq, 2, nf) + x.shape[1:]), 0, 1)

    go = gwo.astype(bf).reshape(n, r, D)
    gi = jnp.stack([gin, gout]).astype(bf).reshape(2, 4, 2 * nq, a, nf, b).transpose(2, 4, 0, 3, 1, 5).reshape(n, 2, a, 4 * b)
    sq, so, si = scatter_sum((to_chunks(gq), to_chunks(go), to_chunks(gi)), nq, nf)
    g_qkv = sq[:, :576].reshape(r, 3, 192).transpose(1, 0, 2).reshape(3 * r, 192)
    g_in = si[0].reshape(a, 4, b).transpose(1, 0, 2)
    g_out = si[1].reshape(a, 4, b).transpose(1, 2, 0)
    return out, gx, g_qkv, so, g_in, g_out, sq[:, 576:586].T, sq[:, 586:588].T


def solution(mesh):
    both = ("dp", "ffn")
    nq, nf = mesh.shape["dp"] // 2, mesh.shape["ffn"]
    return jax.shard_map(
        functools.partial(on_device, nq, nf),
        mesh=mesh,
        in_specs=(P(both, None), P(both), P(both, None), P(both, None), P(None, "dp", "ffn"),
                  P(None, "ffn", "dp"), P(None, both), P(None, both), P(both, None)),
        out_specs=(P(both, None), P(both, None), P(both, None), P(both, None), P(None, "dp", "ffn"),
                   P(None, "ffn", "dp"), P(None, both), P(None, both)),
        check_vma=False,
    )
```

```python
import functools

import jax
import jax.numpy as jnp
from jax import lax
from jax.experimental import pallas as pl
from jax.experimental.pallas import tpu as pltpu
from jax.sharding import PartitionSpec

f32, bf = jnp.float32, jnp.bfloat16
EPS, NEG = 1e-12, -1e30
SL, D, HEADS, GROUPS, GW, GU = 512, 768, 12, 4, 192, 768
PAIRS = D // 128
R = 256
MESH = pl.DeviceIdType.MESH


def dg(a, b, ca, cb):
    return lax.dot_general(a, b, (((ca,), (cb,)), ((), ())), preferred_element_type=f32)


def nn(a, b):
    return dg(a, b, 1, 0)


def nt(a, b):
    return dg(a, b, 1, 1)


def tn(a, b):
    return dg(a, b, 0, 0)


def win(g):
    return 128 * ((GW * g) // 128)


def off(g):
    return 64 * (g % 2)


def halves(t):
    lane = lax.broadcasted_iota(jnp.int32, t.shape, 1)
    z = jnp.zeros_like(t)
    return jnp.where(lane < 64, t, z), jnp.where(lane < 64, z, t)


def colsum(x):
    return jnp.sum(x, axis=0, keepdims=True)


def rowsum(x):
    return jnp.sum(x, axis=1, keepdims=True)


def gelu_pair(u):
    c = 0.5 + 0.5 * lax.erf(u * 0.7071067811865476)
    return u * c, c + (0.3989422804014327 * u) * jnp.exp((-0.5) * (u * u))


def ln_fwd(r):
    c = r - rowsum(r) * (1.0 / D)
    inv = lax.rsqrt(rowsum(c * c) * (1.0 / D) + EPS)
    return c * inv, inv


def ln_bwd(gy, xh, inv, gamma):
    e = gy * gamma
    return inv * (e - rowsum(e) * (1.0 / D) - xh * (rowsum(e * xh) * (1.0 / D)))


def rows_of(i, size):
    return pl.ds(pl.multiple_of(i * size, size), size)


def project(tok, wq, bias, Q, K, V, s):
    rows = rows_of(s, SL)
    for S in range(2):
        b = 384 * S
        y0, y1 = nn(tok[rows, b:b + 256], wq[2 * S]), nn(tok[rows, b + 128:b + 384], wq[2 * S + 1])
        for part, (dst, brow) in enumerate(((Q, 4), (K, None), (V, 5))):
            c = 256 * part
            tiles = (y0[:, c:c + 128], y0[:, c + 128:c + 256] + y1[:, c:c + 128], y1[:, c + 128:c + 256])
            for i, t in enumerate(tiles):
                cols = slice(b + 128 * i, b + 128 * i + 128)
                if brow is not None:
                    t = t + bias[brow:brow + 1, cols]
                t = t.astype(bf)
                if part == 0:
                    t = t * jnp.asarray(0.125, bf)
                dst[rows, cols] = t


def attend(Q, K, V, P, CTX, LI, maskrow, s, p, T=256):
    r0 = pl.multiple_of(s * SL, SL)
    rows, cols = pl.ds(r0, SL), rows_of(p, 128)
    k = K[rows, cols]
    vcat = jnp.concatenate([jnp.concatenate([a, b], 1) for a, b in
                            zip(halves(V[rows, cols]), halves(jnp.ones((SL, 128), bf)))], 0)
    for t in range(SL // T):
        rt = pl.ds(r0 + t * T, T)
        pbs = []
        for h, q in enumerate(halves(Q[rt, cols])):
            sc = nt(q, k) + maskrow
            pb = jnp.exp(sc - jnp.max(sc, axis=1, keepdims=True)).astype(bf)
            P[h, t * T:(t + 1) * T] = pb
            pbs.append(pb)
        r = nn(jnp.concatenate(pbs, 1), vcat)
        li = 1.0 / r[:, 128:]
        CTX[rt, cols] = r[:, :128] * li
        LI[rt, cols] = li.astype(bf)


def attend_back(Q, K, V, P, CTX, DC, s, p, T=256):
    r0 = pl.multiple_of(s * SL, SL)
    rows, cols = pl.ds(r0, SL), rows_of(p, 128)
    q, k, v, dc = Q[rows, cols], K[rows, cols], V[rows, cols], DC[rows, cols]
    kcat = jnp.concatenate(halves(k), 0)
    dss = [[], []]
    for t in range(SL // T):
        rt = pl.ds(r0 + t * T, T)
        dct = dc[t * T:(t + 1) * T]
        dcs, prods = halves(dct), halves(dct.astype(f32) * CTX[rt, cols])
        row = []
        for h in range(2):
            dp = nt(dcs[h], v) - rowsum(prods[h])
            ds = (P[h, t * T:(t + 1) * T].astype(f32) * dp).astype(bf)
            dss[h].append(ds)
            row.append(ds)
        Q[rt, cols] = (nn(jnp.concatenate(row, 1), kcat) * 0.125).astype(bf)
    dk, dv = [], []
    for h in range(2):
        dk.append(tn(q, jnp.concatenate(dss[h], 0))[64 * h:64 * h + 64])
        dv.append(tn(dc, P[h])[64 * h:64 * h + 64])
    K[rows, cols] = jnp.concatenate(dk, 0).T.astype(bf)
    V[rows, cols] = jnp.concatenate(dv, 0).T.astype(bf)


def middle(i, tok, WO, WI, WT, bias, CTX, DC, DR, OB, G1, G2, G3, GB, AB, SLP, XH, H1B, F):
    rows = rows_of(i, R)
    ctxb = CTX[rows, :].astype(bf)
    xh1, inv1 = ln_fwd(nn(ctxb, WO[...]) + bias[6:7, :] + tok[rows, :].astype(f32))
    XH[...] = xh1
    h1 = xh1 * bias[10:11, :] + bias[7:8, :]
    H1B[...] = h1.astype(bf)
    F[...] = h1 + bias[8:9, :]
    for g in range(GROUPS):
        w = slice(win(g), win(g) + 256)
        a, slope = gelu_pair(nn(H1B[:, w], WI[g]) + bias[g:g + 1, :])
        ab = a.astype(bf)
        AB[g] = ab
        SLP[g] = slope.astype(bf)
        F[:, w] += nt(ab, WT[g])
    xh2, inv2 = ln_fwd(F[...])
    OB[...] = (xh2 * bias[11:12, :] + bias[9:10, :]).astype(bf)
    gy = DC[rows, :].astype(f32)
    GB[11:12, :] += colsum(gy * xh2)
    GB[9:10, :] += colsum(gy)
    dr2 = ln_bwd(gy, xh2, inv2, bias[11:12, :])
    dfb = dr2.astype(bf)
    GB[8:9, :] += colsum(dfb.astype(f32))
    F[...] = dr2
    for g in range(GROUPS):
        w = slice(win(g), win(g) + 256)
        o = off(g)
        dub = (nn(dfb[:, w], WT[g]) * SLP[g].astype(f32)).astype(bf)
        F[:, w] += nt(dub, WI[g])
        GB[g:g + 1, :] += colsum(dub.astype(f32))
        G1[g] += tn(H1B[:, w], dub)[o:o + GW]
        G2[g] += tn(dfb[:, w], AB[g])[o:o + GW]
    xh1, dh1 = XH[...], F[...]
    GB[10:11, :] += colsum(dh1 * xh1)
    GB[7:8, :] += colsum(dh1)
    dab = ln_bwd(dh1, xh1, inv1, bias[10:11, :]).astype(bf)
    GB[6:7, :] += colsum(dab.astype(f32))
    G3[...] += tn(ctxb, dab)
    DC[rows, :] = (nt(dab, WO[...]) * DR[rows, :].astype(f32)).astype(bf)
    DR[rows, :] = dab


def qkv_grads(tok, Q, K, V, G1, GB, s):
    rows = rows_of(s, SL)
    for g in range(GROUPS):
        w = slice(win(g), win(g) + 256)
        d3 = jnp.concatenate([Q[rows, w], K[rows, w], V[rows, w]], axis=1)
        G1[g] += tn(tok[rows, w], d3)[off(g):off(g) + GW]
    GB[4:5, :] += colsum(Q[rows, :].astype(f32))
    GB[5:6, :] += colsum(V[rows, :].astype(f32))


def token_grads(wq, Q, K, V, DR, s):
    rows = rows_of(s, SL)
    for S in range(2):
        b, ys = 384 * S, []
        for g in (2 * S, 2 * S + 1):
            w = slice(win(g), win(g) + 256)
            ys.append(nt(jnp.concatenate([Q[rows, w], K[rows, w], V[rows, w]], axis=1), wq[g]))
        tiles = (ys[0][:, :128], ys[0][:, 128:] + ys[1][:, :128], ys[1][:, 128:])
        for i, t in enumerate(tiles):
            cols = slice(b + 128 * i, b + 128 * i + 128)
            DR[rows, cols] = (t + DR[rows, cols].astype(f32)).astype(bf)


class Cut:
    def __init__(self, nc, nq, nf):
        self.nc, self.nq, self.nf = nc, nq, nf
        self.n = nc * nq * nf
        self.r = D // self.n
        self.a, self.b = GW // (nc * nq), GU // nf
        self.shapes = ((self.r, 640), (self.r, D), (2, self.a, GROUPS * self.b))

    def at(self, d):
        dp, f = divmod(d, self.nf)
        return dp % self.nc, dp // self.nc, f


def unpack_q(cut, GQ, WQ, SM):
    WQ[...] = jnp.zeros_like(WQ)
    r = cut.r
    for p in range(3):
        for g in range(GROUPS):
            parts = []
            for i in range(GW // r):
                d, j = divmod((D * p + GW * g) // r + i, 3)
                parts.append(GQ[cut.at(d)].astype(f32)[:, GW * j:GW * (j + 1)])
            o = off(g)
            WQ[g, o:o + GW, 256 * p + o:256 * p + o + GW] = jnp.concatenate(parts, 0).astype(bf)
    small = jnp.concatenate([GQ[cut.at(d)][:, 512:].astype(f32) for d in range(cut.n)], 0)
    SM[...] = small.T[64:80]


def unpack_o(cut, GO, WO):
    per = GW // cut.r
    for i in range(D // GW):
        rows = [GO[cut.at(d)].astype(f32) for d in range(per * i, per * i + per)]
        WO[GW * i:GW * (i + 1), :] = jnp.concatenate(rows, 0).astype(bf)


def unpack_i(cut, GI, WI, WT):
    b = cut.b
    for k, W in enumerate((WI, WT)):
        for g in range(GROUPS):
            o = off(g)
            z = 0 if o else GW
            W[g, z:z + 64] = jnp.zeros((64, GU), bf)
            cols = []
            for f in range(cut.nf):
                cols.append(jnp.concatenate(
                    [GI[cut.at(dp * cut.nf + f)][k].astype(f32)[:, g * b:(g + 1) * b]
                     for dp in range(cut.nc * cut.nq)], 0))
            W[g, o:o + GW] = jnp.concatenate(cols, 1).astype(bf)


def pack_o(cut, G3, GO):
    for d in range(cut.n):
        GO[cut.at(d)] = G3[cut.r * d:cut.r * (d + 1), :].astype(bf)


def pack_i(cut, G1, G2, GI):
    a, b = cut.a, cut.b
    for k, G in enumerate((G1, G2)):
        for dp in range(cut.nc * cut.nq):
            for f in range(cut.nf):
                GI[cut.at(dp * cut.nf + f) + (k,)] = jnp.concatenate(
                    [G[g, a * dp:a * (dp + 1), b * f:b * (f + 1)] for g in range(GROUPS)], 1).astype(bf)


def pack_q(cut, G1, GB, GQ):
    r = cut.r
    small = jnp.concatenate([jnp.zeros((64, D), f32), GB[...], jnp.zeros((48, D), f32)], 0).T
    for d in range(cut.n):
        parts = []
        for j in range(3):
            p, rest = divmod(r * (3 * d + j), D)
            g, i = divmod(rest, GW)
            c = 256 * p + off(g)
            parts.append(G1[g, i:i + r, c:c + GW])
        parts.append(small[r * d:r * (d + 1), 64:])
        GQ[cut.at(d)] = jnp.concatenate(parts, 1).astype(bf)


class Links:
    def __init__(self, cut, send_sem, recv_sem):
        self.cut, self.sems = cut, (send_sem, recv_sem)
        dp, self.f = lax.axis_index("dp"), lax.axis_index("ffn")
        self.c, self.q = lax.rem(dp, 2), lax.div(dp, 2)
        nq, nf = cut.nq, cut.nf
        self.fs = [lax.rem(self.f + k, nf) for k in range(1, nf)]
        self.qs = [lax.rem(self.q + k, nq) for k in range(1, nq)]
        self.per = nf - 1 + nq - 1 + 1

    def to_f(self, k):
        return (2 * self.q + self.c, self.fs[k])

    def to_q(self, k):
        return (2 * self.qs[k] + self.c, self.f)

    def twin(self):
        return (2 * self.q + 1 - self.c, self.f)

    def greet(self):
        everyone = [self.to_f(k) for k in range(len(self.fs))] + [self.to_q(k) for k in range(len(self.qs))] + [self.twin()]
        barrier = pltpu.get_barrier_semaphore()
        for peer in everyone:
            pl.semaphore_signal(barrier, inc=1, device_id=peer, device_id_type=MESH)
        pl.semaphore_wait(barrier, len(everyone))

    def copy(self, src, dst, slot, peer):
        return pltpu.make_async_remote_copy(
            src_ref=src, dst_ref=dst, send_sem=self.sems[0].at[slot], recv_sem=self.sems[1].at[slot],
            device_id=peer, device_id_type=MESH)

    def gather(self, stage, i, G):
        base = i * self.per
        c, q, f = self.c, self.q, self.f
        if stage == 0:
            return [self.copy(G.at[c, q, f], G.at[c, q, f], base + k, self.to_f(k)) for k in range(len(self.fs))]
        base += len(self.fs)
        if stage == 1:
            return [self.copy(G.at[c, q], G.at[c, q], base + k, self.to_q(k)) for k in range(len(self.qs))]
        return [self.copy(G.at[c], G.at[c], base + len(self.qs), self.twin())]

    def scatter(self, stage, i, G, RC, RP, Z, RF):
        base = (3 + i) * self.per
        c = self.c
        if stage == 0:
            return [self.copy(G.at[1 - c], RC, base, self.twin())]
        base += 1
        if stage == 1:
            return [self.copy(G.at[c, self.qs[k]], RP.at[k], base + k, self.to_q(k)) for k in range(len(self.qs))]
        base += len(self.qs)
        return [self.copy(Z.at[self.fs[k]], RF.at[k], base + k, self.to_f(k)) for k in range(len(self.fs))]

    def add_twin(self, G, RC):
        for q in range(self.cut.nq):
            G[self.c, q] = (G[self.c, q].astype(f32) + RC[q].astype(f32)).astype(bf)

    def add_q(self, G, RP, Z):
        total = G[self.c, self.q].astype(f32)
        for k in range(len(self.qs)):
            total = total + RP[k].astype(f32)
        Z[...] = total.astype(bf)

    def add_f(self, Z, RF):
        total = Z[self.f].astype(f32)
        for k in range(len(self.fs)):
            total = total + RF[k].astype(f32)
        return total


def start(copies):
    for copy in copies:
        copy.start()


def arrive(copies):
    for copy in copies:
        copy.wait_recv()


def sent(copies):
    for copy in copies:
        copy.wait_send()


def layer(cut, remote, length, qp, op, ip, tok_in, cot_in,
          out, gx, phbm, sq, so, si,
          tok, DC, Q, K, V, CTX, DR, WQ, WO, WI, WT, SM, GQ, GO, GI,
          RCq, RCo, RCi, RPq, RPo, RPi, Zq, Zo, Zi, RFq, RFo, RFi,
          G1, G2, G3, GB, AB, SLP, XH, H1B, F, OB, PB, in_sem, p_sem, o_sem, x_sem, *sems):
    slots = tok.shape[0] // SL
    nmid = tok.shape[0] // R
    links = Links(cut, *sems) if remote else None
    loads = [pltpu.make_async_copy(tok_in, tok, in_sem.at[0]), pltpu.make_async_copy(cot_in, DC, in_sem.at[1])]
    start(loads)
    if remote:
        at = links.c, links.q, links.f
        GQ[at] = qp[...]
        GO[at] = op[...]
        GI[at] = ip[...]
    else:
        for src, dst in ((qp, GQ), (op, GO), (ip, GI)):
            pltpu.sync_copy(src, dst)
    gq = lambda stage: links.gather(stage, 0, GQ)
    gr = lambda stage: links.gather(stage, 1, GO) + links.gather(stage, 2, GI)
    sq_args, so_args, si_args = (0, GQ, RCq, RPq, Zq, RFq), (1, GO, RCo, RPo, Zo, RFo), (2, GI, RCi, RPi, Zi, RFi)
    rq = lambda stage: links.scatter(stage, *sq_args)
    rr = lambda stage: links.scatter(stage, *so_args) + links.scatter(stage, *si_args)

    if remote:
        links.greet()
        start(gq(0))
        start(gr(0))
    for G in (G1, G2, G3, GB):
        G[...] = jnp.zeros_like(G)
    if remote:
        arrive(gq(0))
        start(gq(1))
        arrive(gq(1))
        start(gq(2))
        arrive(gr(0))
        start(gr(1))
        arrive(gq(2))
    unpack_q(cut, GQ, WQ, SM)
    loads[0].wait()
    lax.fori_loop(0, slots, lambda s, x: (project(tok, WQ, SM, Q, K, V, s), x)[1], 0)

    steps = slots * PAIRS // 2

    def to_hbm(i, slot):
        return pltpu.make_async_copy(PB.at[slot], phbm.at[i], p_sem.at[slot])

    def forward(i, x):
        half = lax.rem(i, 2)

        @pl.when(i >= 2)
        def _():
            for u in range(2):
                to_hbm(2 * i + u, 2 * half + u).wait()

        if remote:
            @pl.when(i == 4)
            def _():
                arrive(gr(1))
                start(gr(2))

        for u in range(2):
            pair = 2 * i + u
            s = lax.div(pair, PAIRS)
            lane = lax.broadcasted_iota(jnp.int32, (1, SL), 1)
            maskrow = jnp.where(lane < length[s], 0.0, NEG)
            attend(Q, K, V, PB.at[2 * half + u], CTX, DR, maskrow, s, lax.rem(pair, PAIRS))
        for u in range(2):
            to_hbm(2 * i + u, 2 * half + u).start()
        return x

    lax.fori_loop(0, steps, forward, 0)
    if remote:
        arrive(gr(2))
    unpack_o(cut, GO, WO)
    unpack_i(cut, GI, WI, WT)
    loads[1].wait()
    for i in range(max(0, steps - 2), steps):
        for u in range(2):
            to_hbm(2 * i + u, 2 * (i % 2) + u).wait()

    def from_hbm(i, slot):
        return pltpu.make_async_copy(phbm.at[i], PB.at[slot], p_sem.at[slot])

    for u in range(2):
        from_hbm(u, u).start()

    def out_copy(i, slot):
        return pltpu.make_async_copy(OB.at[slot], out.at[rows_of(i, R), :], o_sem.at[slot])

    def mid(i, x):
        slot = lax.rem(i, 2)

        @pl.when(i >= 2)
        def _():
            out_copy(i, slot).wait()

        middle(i, tok, WO, WI, WT, SM, CTX, DC, DR, OB.at[slot], G1, G2, G3, GB, AB, SLP, XH, H1B, F)
        out_copy(i, slot).start()
        return x

    lax.fori_loop(0, nmid, mid, 0)
    if remote:
        sent(gq(0) + gq(1) + gq(2) + gr(0) + gr(1) + gr(2))
    pack_o(cut, G3, GO)
    pack_i(cut, G1, G2, GI)
    if remote:
        start(rr(0))
    G1[...] = jnp.zeros_like(G1)

    def backward(i, x):
        half = lax.rem(i, 2)

        @pl.when(i + 1 < steps)
        def _():
            for u in range(2):
                from_hbm(2 * i + 2 + u, 2 - 2 * half + u).start()

        if remote:
            @pl.when(i == 1)
            def _():
                arrive(rr(0))
                links.add_twin(GO, RCo)
                links.add_twin(GI, RCi)
                start(rr(1))

            @pl.when(i == steps - 2)
            def _():
                arrive(rr(1))
                links.add_q(GO, RPo, Zo)
                links.add_q(GI, RPi, Zi)
                start(rr(2))

        for u in range(2):
            from_hbm(2 * i + u, 2 * half + u).wait()
        for u in range(2):
            pair = 2 * i + u
            attend_back(Q, K, V, PB.at[2 * half + u], CTX, DC, lax.div(pair, PAIRS), lax.rem(pair, PAIRS))
        return x

    lax.fori_loop(0, steps, backward, 0)
    lax.fori_loop(0, slots, lambda s, x: (qkv_grads(tok, Q, K, V, G1, GB, s), x)[1], 0)
    pack_q(cut, G1, GB, GQ)
    if remote:
        start(rq(0))

    def gx_copy(s):
        return pltpu.make_async_copy(DR.at[rows_of(s, SL), :], gx.at[rows_of(s, SL), :], x_sem.at[s])

    def last(s, x):
        if remote:
            @pl.when(s == 1)
            def _():
                arrive(rq(0))
                links.add_twin(GQ, RCq)
                start(rq(1))
        token_grads(WQ, Q, K, V, DR, s)
        gx_copy(s).start()
        return x

    lax.fori_loop(0, slots, last, 0)
    if remote:
        arrive(rr(2))
        so[...] = links.add_f(Zo, RFo)
        si[...] = links.add_f(Zi, RFi)
        arrive(rq(1))
        links.add_q(GQ, RPq, Zq)
        start(rq(2))
        arrive(rq(2))
        sq[...] = links.add_f(Zq, RFq)
        sent(rr(0) + rr(1) + rr(2) + rq(0) + rq(1) + rq(2))
    else:
        for src, dst in ((GQ, sq), (GO, so), (GI, si)):
            pltpu.sync_copy(src, dst)
    for i in range(max(0, nmid - 2), nmid):
        out_copy(i, i % 2).wait()
    for s in range(slots):
        gx_copy(s).wait()


def run_layer(cut, remote, lengths, pieces, tokens, cotangent):
    rows = tokens.shape[0]
    slots = rows // SL
    vm, hbm = pl.BlockSpec(memory_space=pltpu.VMEM), pl.BlockSpec(memory_space=pl.ANY)
    sd, vmem, dma = jax.ShapeDtypeStruct, pltpu.VMEM, pltpu.SemaphoreType.DMA
    nq, nf, shapes = cut.nq, cut.nf, cut.shapes
    scratch = [vmem((rows, D), bf)] * 5 + [vmem((rows, D), f32), vmem((rows, D), bf)]
    scratch += [vmem((GROUPS, 256, 768), bf), vmem((D, D), bf), vmem((GROUPS, 256, GU), bf), vmem((GROUPS, 256, GU), bf), vmem((16, D), f32)]
    scratch += [vmem((cut.nc, nq, nf) + s, bf) for s in shapes]
    if remote:
        for lead in ((nq, nf), (nq - 1, nf), (nf,), (nf - 1,)):
            scratch += [vmem(lead + s, bf) for s in shapes]
    else:
        scratch += [vmem((8, 128), bf)] * 12
    scratch += [vmem((GROUPS, GW, GU), f32)] * 2 + [vmem((D, D), f32), vmem((16, D), f32)]
    scratch += [vmem((GROUPS, R, GU), bf)] * 2 + [vmem((R, D), f32), vmem((R, D), bf), vmem((R, D), f32), vmem((2, R, D), bf)]
    scratch += [vmem((4, 2, SL, SL), bf), dma((2,)), dma((4,)), dma((2,)), dma((slots,))]
    params = dict(vmem_limit_bytes=64 * 1024 * 1024 - 65536)
    if remote:
        count = 6 * (nf + nq - 1)
        scratch += [dma((count,)), dma((count,))]
        params.update(collective_id=0, has_side_effects=True)
    return pl.pallas_call(
        functools.partial(layer, cut, remote),
        out_shape=(sd((rows, D), bf), sd((rows, D), bf), sd((slots * PAIRS, 2, SL, SL), bf)) + tuple(sd(s, f32) if remote else sd((cut.nc, nq, nf) + s, bf) for s in shapes),
        in_specs=[pl.BlockSpec(memory_space=pltpu.SMEM)] + [vm if remote else hbm] * 3 + [hbm, hbm],
        out_specs=(hbm, hbm, hbm) + (vm if remote else hbm,) * 3,
        scratch_shapes=scratch,
        compiler_params=pltpu.CompilerParams(**params),
    )(lengths, *pieces, tokens, cotangent)


def on_device(cut, remote, tokens, lengths, qkv_weight, out_weight, ffn_in_weight, ffn_out_weight, biases, gains, cotangent):
    r, a, b = cut.r, cut.a, cut.b
    q_piece = jnp.concatenate(
        [qkv_weight.reshape(3, r, GW).transpose(1, 0, 2).reshape(r, 3 * GW), biases.T, gains.T, jnp.zeros((r, 52), bf)], axis=1)
    i_piece = jnp.stack([ffn_in_weight.transpose(1, 0, 2).reshape(a, GROUPS * b), ffn_out_weight.transpose(2, 0, 1).reshape(a, GROUPS * b)])
    out, gx, _, sq, so, si = run_layer(cut, remote, lengths, (q_piece, out_weight, i_piece), tokens, cotangent)
    g_qkv = sq[:, :3 * GW].reshape(r, 3, GW).transpose(1, 0, 2).reshape(3 * r, GW)
    g_in = si[0].reshape(a, GROUPS, b).transpose(1, 0, 2)
    g_out = si[1].reshape(a, GROUPS, b).transpose(1, 2, 0)
    return out, gx, g_qkv, so, g_in, g_out, sq[:, 576:586].T, sq[:, 586:588].T


def solution(mesh):
    both = ("dp", "ffn")
    P = PartitionSpec
    return jax.shard_map(
        functools.partial(on_device, Cut(2, mesh.shape["dp"] // 2, mesh.shape["ffn"]), True),
        mesh=mesh,
        in_specs=(P(both, None), P(both), P(both, None), P(both, None), P(None, "dp", "ffn"),
                  P(None, "ffn", "dp"), P(None, both), P(None, both), P(both, None)),
        out_specs=(P(both, None), P(both, None), P(both, None), P(both, None), P(None, "dp", "ffn"),
                   P(None, "ffn", "dp"), P(None, both), P(None, both)),
        check_vma=False,
    )
```

```python
import functools

import jax
import jax.numpy as jnp
from jax import lax
from jax.experimental import pallas as pl
from jax.experimental.pallas import tpu as pltpu
from jax.sharding import PartitionSpec

f32, bf = jnp.float32, jnp.bfloat16
EPS, NEG = 1e-12, -1e30
SL, D, HEADS, GROUPS, GW, GU = 512, 768, 12, 4, 192, 768
PAIRS = D // 128
R = 256
MESH = pl.DeviceIdType.MESH


def dg(a, b, ca, cb):
    return lax.dot_general(a, b, (((ca,), (cb,)), ((), ())), preferred_element_type=f32)


def nn(a, b):
    return dg(a, b, 1, 0)


def nt(a, b):
    return dg(a, b, 1, 1)


def tn(a, b):
    return dg(a, b, 0, 0)


def win(g):
    return 128 * ((GW * g) // 128)


def off(g):
    return 64 * (g % 2)


def halves(t):
    lane = lax.broadcasted_iota(jnp.int32, t.shape, 1)
    z = jnp.zeros_like(t)
    return jnp.where(lane < 64, t, z), jnp.where(lane < 64, z, t)


def colsum(x):
    return jnp.sum(x, axis=0, keepdims=True)


def rowsum(x):
    return jnp.sum(x, axis=1, keepdims=True)


def gelu_pair(u):
    c = 0.5 + 0.5 * lax.erf(u * 0.7071067811865476)
    return u * c, c + (0.3989422804014327 * u) * jnp.exp((-0.5) * (u * u))


def ln_fwd(r):
    c = r - rowsum(r) * (1.0 / D)
    inv = lax.rsqrt(rowsum(c * c) * (1.0 / D) + EPS)
    return c * inv, inv


def ln_bwd(gy, xh, inv, gamma):
    e = gy * gamma
    return inv * (e - rowsum(e) * (1.0 / D) - xh * (rowsum(e * xh) * (1.0 / D)))


def rows_of(i, size):
    return pl.ds(pl.multiple_of(i * size, size), size)


def project(tok, wq, bias, Q, K, V, s):
    rows = rows_of(s, SL)
    for S in range(2):
        b = 384 * S
        y0, y1 = nn(tok[rows, b:b + 256], wq[2 * S]), nn(tok[rows, b + 128:b + 384], wq[2 * S + 1])
        for part, (dst, brow) in enumerate(((Q, 4), (K, None), (V, 5))):
            c = 256 * part
            tiles = (y0[:, c:c + 128], y0[:, c + 128:c + 256] + y1[:, c:c + 128], y1[:, c + 128:c + 256])
            for i, t in enumerate(tiles):
                cols = slice(b + 128 * i, b + 128 * i + 128)
                if brow is not None:
                    t = t + bias[brow:brow + 1, cols]
                t = t.astype(bf)
                if part == 0:
                    t = t * jnp.asarray(0.125, bf)
                dst[rows, cols] = t


def attend(Q, K, V, P, CTX, LI, maskrow, s, p, T=256):
    r0 = pl.multiple_of(s * SL, SL)
    rows, cols = pl.ds(r0, SL), rows_of(p, 128)
    k = K[rows, cols]
    vcat = jnp.concatenate([jnp.concatenate([a, b], 1) for a, b in
                            zip(halves(V[rows, cols]), halves(jnp.ones((SL, 128), bf)))], 0)
    for t in range(SL // T):
        rt = pl.ds(r0 + t * T, T)
        pbs = []
        for h, q in enumerate(halves(Q[rt, cols])):
            sc = nt(q, k) + maskrow
            pb = jnp.exp(sc - jnp.max(sc, axis=1, keepdims=True)).astype(bf)
            P[h, t * T:(t + 1) * T] = pb
            pbs.append(pb)
        r = nn(jnp.concatenate(pbs, 1), vcat)
        li = 1.0 / r[:, 128:]
        CTX[rt, cols] = r[:, :128] * li
        LI[rt, cols] = li.astype(bf)


def attend_back(Q, K, V, P, CTX, DC, s, p, T=256):
    r0 = pl.multiple_of(s * SL, SL)
    rows, cols = pl.ds(r0, SL), rows_of(p, 128)
    q, k, v, dc = Q[rows, cols], K[rows, cols], V[rows, cols], DC[rows, cols]
    kcat = jnp.concatenate(halves(k), 0)
    dss = [[], []]
    for t in range(SL // T):
        rt = pl.ds(r0 + t * T, T)
        dct = dc[t * T:(t + 1) * T]
        dcs, prods = halves(dct), halves(dct.astype(f32) * CTX[rt, cols])
        row = []
        for h in range(2):
            dp = nt(dcs[h], v) - rowsum(prods[h])
            ds = (P[h, t * T:(t + 1) * T].astype(f32) * dp).astype(bf)
            dss[h].append(ds)
            row.append(ds)
        Q[rt, cols] = (nn(jnp.concatenate(row, 1), kcat) * 0.125).astype(bf)
    dk, dv = [], []
    for h in range(2):
        dk.append(tn(q, jnp.concatenate(dss[h], 0))[64 * h:64 * h + 64])
        dv.append(tn(dc, P[h])[64 * h:64 * h + 64])
    K[rows, cols] = jnp.concatenate(dk, 0).T.astype(bf)
    V[rows, cols] = jnp.concatenate(dv, 0).T.astype(bf)


def middle(i, tok, WO, WI, WT, bias, CTX, DC, DR, OB, G1, G2, G3, GB, AB, SLP, XH, H1B, F):
    rows = rows_of(i, R)
    ctxb = CTX[rows, :].astype(bf)
    xh1, inv1 = ln_fwd(nn(ctxb, WO[...]) + bias[6:7, :] + tok[rows, :].astype(f32))
    XH[...] = xh1
    h1 = xh1 * bias[10:11, :] + bias[7:8, :]
    H1B[...] = h1.astype(bf)
    F[...] = h1 + bias[8:9, :]
    for g in range(GROUPS):
        w = slice(win(g), win(g) + 256)
        a, slope = gelu_pair(nn(H1B[:, w], WI[g]) + bias[g:g + 1, :])
        ab = a.astype(bf)
        AB[g] = ab
        SLP[g] = slope.astype(bf)
        F[:, w] += nt(ab, WT[g])
    xh2, inv2 = ln_fwd(F[...])
    OB[...] = (xh2 * bias[11:12, :] + bias[9:10, :]).astype(bf)
    gy = DC[rows, :].astype(f32)
    GB[11:12, :] += colsum(gy * xh2)
    GB[9:10, :] += colsum(gy)
    dr2 = ln_bwd(gy, xh2, inv2, bias[11:12, :])
    dfb = dr2.astype(bf)
    GB[8:9, :] += colsum(dfb.astype(f32))
    F[...] = dr2
    for g in range(GROUPS):
        w = slice(win(g), win(g) + 256)
        o = off(g)
        dub = (nn(dfb[:, w], WT[g]) * SLP[g].astype(f32)).astype(bf)
        F[:, w] += nt(dub, WI[g])
        GB[g:g + 1, :] += colsum(dub.astype(f32))
        G1[g] += tn(H1B[:, w], dub)[o:o + GW]
        G2[g] += tn(dfb[:, w], AB[g])[o:o + GW]
    xh1, dh1 = XH[...], F[...]
    GB[10:11, :] += colsum(dh1 * xh1)
    GB[7:8, :] += colsum(dh1)
    dab = ln_bwd(dh1, xh1, inv1, bias[10:11, :]).astype(bf)
    GB[6:7, :] += colsum(dab.astype(f32))
    G3[...] += tn(ctxb, dab)
    DC[rows, :] = (nt(dab, WO[...]) * DR[rows, :].astype(f32)).astype(bf)
    DR[rows, :] = dab


def qkv_grads(tok, Q, K, V, G1, GB, s):
    rows = rows_of(s, SL)
    for g in range(GROUPS):
        w = slice(win(g), win(g) + 256)
        d3 = jnp.concatenate([Q[rows, w], K[rows, w], V[rows, w]], axis=1)
        G1[g] += tn(tok[rows, w], d3)[off(g):off(g) + GW]
    GB[4:5, :] += colsum(Q[rows, :].astype(f32))
    GB[5:6, :] += colsum(V[rows, :].astype(f32))


def token_grads(wq, Q, K, V, DR, s):
    rows = rows_of(s, SL)
    for S in range(2):
        b, ys = 384 * S, []
        for g in (2 * S, 2 * S + 1):
            w = slice(win(g), win(g) + 256)
            ys.append(nt(jnp.concatenate([Q[rows, w], K[rows, w], V[rows, w]], axis=1), wq[g]))
        tiles = (ys[0][:, :128], ys[0][:, 128:] + ys[1][:, :128], ys[1][:, 128:])
        for i, t in enumerate(tiles):
            cols = slice(b + 128 * i, b + 128 * i + 128)
            DR[rows, cols] = (t + DR[rows, cols].astype(f32)).astype(bf)


QA, QB, OW, FW = range(4)
ORDER = ("qf", "fq", "fq", "qf")


class Cut:
    def __init__(self, nq, nf):
        self.nq, self.nf = nq, nf
        self.n = 2 * nq * nf
        self.r = D // self.n
        self.a, self.b = GW // (2 * nq), GU // nf
        self.shapes = ((self.r, 2 * GW), (self.r, 256), (self.r, D), (2, self.a, GROUPS * self.b))

    def lead(self, i):
        return (self.nq, self.nf) if ORDER[i] == "qf" else (self.nf, self.nq)

    def at(self, i, d):
        dp, f = divmod(d, self.nf)
        c, q = dp % 2, dp // 2
        return (c, q, f) if ORDER[i] == "qf" else (c, f, q)


def put_pieces(cut, at, qkv, wo, wi, wt, biases, gains, SC, G):
    r = cut.r
    SC[...] = jnp.zeros_like(SC)
    SC[0:10, 0:r] = biases[...].astype(f32)
    SC[10:12, 0:r] = gains[...].astype(f32)
    rows = qkv[...].astype(f32)
    G[QA][at[QA]] = jnp.concatenate([rows[:r], rows[r:2 * r]], 1).astype(bf)
    G[QB][at[QB]] = jnp.concatenate([rows[2 * r:], SC[...].T[:r, :64]], 1).astype(bf)
    G[OW][at[OW]] = wo[...]
    for k, w in enumerate((wi, wt)):
        G[FW][at[FW] + (k,)] = jnp.concatenate([w[g].astype(f32) for g in range(GROUPS)], 1).astype(bf)


def unpack_q(cut, G, WQ, SM):
    WQ[...] = jnp.zeros_like(WQ)
    r = cut.r
    for p in range(3):
        for g in range(GROUPS):
            parts = []
            for i in range(GW // r):
                d, j = divmod((D * p + GW * g) // r + i, 3)
                if j < 2:
                    parts.append(G[QA][cut.at(QA, d)].astype(f32)[:, GW * j:GW * (j + 1)])
                else:
                    parts.append(G[QB][cut.at(QB, d)].astype(f32)[:, :GW])
            o = off(g)
            WQ[g, o:o + GW, 256 * p + o:256 * p + o + GW] = jnp.concatenate(parts, 0).astype(bf)
    small = jnp.concatenate([G[QB][cut.at(QB, d)][:, 128:].astype(f32) for d in range(cut.n)], 0)
    SM[...] = small.T[64:80]


def unpack_o(cut, G, WO):
    per = GW // cut.r
    for i in range(D // GW):
        rows = [G[OW][cut.at(OW, d)].astype(f32) for d in range(per * i, per * i + per)]
        WO[GW * i:GW * (i + 1), :] = jnp.concatenate(rows, 0).astype(bf)


def unpack_f(cut, G, WI, WT):
    b = cut.b
    for k, W in enumerate((WI, WT)):
        for g in range(GROUPS):
            o = off(g)
            z = 0 if o else GW
            W[g, z:z + 64] = jnp.zeros((64, GU), bf)
            cols = []
            for f in range(cut.nf):
                cols.append(jnp.concatenate(
                    [G[FW][cut.at(FW, dp * cut.nf + f)][k].astype(f32)[:, g * b:(g + 1) * b] for dp in range(2 * cut.nq)], 0))
            W[g, o:o + GW] = jnp.concatenate(cols, 1).astype(bf)


def pack_o(cut, G3, G):
    for d in range(cut.n):
        G[OW][cut.at(OW, d)] = G3[cut.r * d:cut.r * (d + 1), :].astype(bf)


def pack_f(cut, G1, G2, G):
    a, b = cut.a, cut.b
    for k, grad in enumerate((G1, G2)):
        for dp in range(2 * cut.nq):
            for f in range(cut.nf):
                G[FW][cut.at(FW, dp * cut.nf + f) + (k,)] = jnp.concatenate(
                    [grad[g, a * dp:a * (dp + 1), b * f:b * (f + 1)] for g in range(GROUPS)], 1).astype(bf)


def pack_q(cut, G1, GB, G):
    r = cut.r
    small = jnp.concatenate([jnp.zeros((64, D), f32), GB[...], jnp.zeros((48, D), f32)], 0).T
    for d in range(cut.n):
        parts = []
        for j in range(3):
            p, rest = divmod(r * (3 * d + j), D)
            g, i = divmod(rest, GW)
            c = 256 * p + off(g)
            parts.append(G1[g, i:i + r, c:c + GW])
        G[QA][cut.at(QA, d)] = jnp.concatenate(parts[:2], 1).astype(bf)
        G[QB][cut.at(QB, d)] = jnp.concatenate([parts[2], small[r * d:r * (d + 1), 64:]], 1).astype(bf)


class Links:
    def __init__(self, cut, send_sem, recv_sem):
        self.cut, self.sems = cut, (send_sem, recv_sem)
        dp, self.f = lax.axis_index("dp"), lax.axis_index("ffn")
        self.c, self.q = lax.rem(dp, 2), lax.div(dp, 2)
        nq, nf = cut.nq, cut.nf
        fs = [lax.rem(self.f + k, nf) for k in range(1, nf)]
        qs = [lax.rem(self.q + k, nq) for k in range(1, nq)]
        to_f = [(2 * self.q + self.c, f) for f in fs]
        to_q = [(2 * q + self.c, self.f) for q in qs]
        self.twin = (2 * self.q + 1 - self.c, self.f)
        self.axis = {"q": (self.q, qs, to_q), "f": (self.f, fs, to_f)}
        self.per = nf + nq - 1

    def at(self, i):
        return (self.c, self.q, self.f) if ORDER[i] == "qf" else (self.c, self.f, self.q)

    def greet(self):
        barrier = pltpu.get_barrier_semaphore()
        everyone = self.axis["q"][2] + self.axis["f"][2] + [self.twin]
        for peer in everyone:
            pl.semaphore_signal(barrier, inc=1, device_id=peer, device_id_type=MESH)
        return lambda: pl.semaphore_wait(barrier, len(everyone))

    def copy(self, src, dst, slot, peer):
        return pltpu.make_async_remote_copy(
            src_ref=src, dst_ref=dst, send_sem=self.sems[0].at[slot], recv_sem=self.sems[1].at[slot],
            device_id=peer, device_id_type=MESH)

    def gather(self, stage, i, G):
        base, c = i * self.per, self.c
        (u, us, to_u), (v, vs, to_v) = (self.axis[x] for x in ORDER[i])
        if stage == 0:
            return [self.copy(G.at[c, u, v], G.at[c, u, v], base + k, to_v[k]) for k in range(len(vs))]
        base += len(vs)
        if stage == 1:
            return [self.copy(G.at[c, u], G.at[c, u], base + k, to_u[k]) for k in range(len(us))]
        return [self.copy(G.at[c], G.at[c], base + len(us), self.twin)]

    def scatter(self, stage, i, G, RC, RU, Z, RV):
        base, c = (4 + i) * self.per, self.c
        (u, us, to_u), (v, vs, to_v) = (self.axis[x] for x in ORDER[i])
        if stage == 0:
            return [self.copy(G.at[1 - c], RC, base, self.twin)]
        base += 1
        if stage == 1:
            return [self.copy(G.at[c, us[k]], RU.at[k], base + k, to_u[k]) for k in range(len(us))]
        base += len(us)
        return [self.copy(Z.at[vs[k]], RV.at[k], base + k, to_v[k]) for k in range(len(vs))]

    def add_twin(self, i, G, RC, RU, Z, RV):
        for u in range(G.shape[1]):
            G[self.c, u] = (G[self.c, u].astype(f32) + RC[u].astype(f32)).astype(bf)

    def add_u(self, i, G, RC, RU, Z, RV):
        total = G[self.c, self.axis[ORDER[i][0]][0]].astype(f32)
        for k in range(RU.shape[0]):
            total = total + RU[k].astype(f32)
        Z[...] = total.astype(bf)

    def add_v(self, i, G, RC, RU, Z, RV):
        total = Z[self.axis[ORDER[i][1]][0]].astype(f32)
        for k in range(RV.shape[0]):
            total = total + RV[k].astype(f32)
        return total


def start(copies):
    for copy in copies:
        copy.start()


def arrive(copies):
    for copy in copies:
        copy.wait_recv()


def sent(copies):
    for copy in copies:
        copy.wait_send()


def layer(cut, remote, length, *refs):
    count = 6 if remote else 4
    pieces, refs = refs[:count], refs[count:]
    tok_in, cot_in, out, gx, phbm = refs[:5]
    results, refs = refs[5:9], refs[9:]
    tok, DC, Q, K, V, CTX, DR, WQ, WO, WI, WT, SM = refs[:12]
    G, refs = refs[12:16], refs[16:]
    if remote:
        parts, refs = [refs[4 * k:4 * k + 4] for k in range(4)], refs[16:]
        RC, RU, Z, RV = parts
    G1, G2, G3, GB, SC, AB, SLP, XH, H1B, F, OB, PB, in_sem, p_sem, o_sem, x_sem = refs[:16]
    slots = tok.shape[0] // SL
    nmid = tok.shape[0] // R
    links = Links(cut, *refs[16:]) if remote else None

    def gather(stage, which):
        return sum((links.gather(stage, i, G[i]) for i in which), [])

    def scatter(stage, which):
        return sum((links.scatter(stage, i, G[i], RC[i], RU[i], Z[i], RV[i]) for i in which), [])

    def add(step, which):
        return [step(i, G[i], RC[i], RU[i], Z[i], RV[i]) for i in which]

    early, late = (QA, QB), (OW, FW)
    if remote:
        met = links.greet()
    loads = [pltpu.make_async_copy(tok_in, tok, in_sem.at[0]), pltpu.make_async_copy(cot_in, DC, in_sem.at[1])]
    start(loads)
    if remote:
        put_pieces(cut, [links.at(i) for i in range(4)], *pieces, SC, G)
        met()
        start(gather(0, early))
    else:
        for src, dst in zip(pieces, G):
            pltpu.sync_copy(src, dst)
    for g in (G1, G2, G3, GB):
        g[...] = jnp.zeros_like(g)
    if remote:
        arrive(gather(0, early))
        start(gather(1, early))
        arrive(gather(1, early))
        start(gather(2, early))
        start(gather(0, late))
        arrive(gather(2, early))
    unpack_q(cut, G, WQ, SM)
    loads[0].wait()
    lax.fori_loop(0, slots, lambda s, x: (project(tok, WQ, SM, Q, K, V, s), x)[1], 0)

    steps = slots * PAIRS // 2

    def to_hbm(i, slot):
        return pltpu.make_async_copy(PB.at[slot], phbm.at[i], p_sem.at[slot])

    def forward(i, x):
        half = lax.rem(i, 2)

        @pl.when(i >= 2)
        def _():
            for u in range(2):
                to_hbm(2 * i + u, 2 * half + u).wait()

        if remote:
            @pl.when(i == 1)
            def _():
                arrive(gather(0, late))
                start(gather(1, late))

        for u in range(2):
            pair = 2 * i + u
            s = lax.div(pair, PAIRS)
            lane = lax.broadcasted_iota(jnp.int32, (1, SL), 1)
            maskrow = jnp.where(lane < length[s], 0.0, NEG)
            attend(Q, K, V, PB.at[2 * half + u], CTX, DR, maskrow, s, lax.rem(pair, PAIRS))
        for u in range(2):
            to_hbm(2 * i + u, 2 * half + u).start()
        return x

    lax.fori_loop(0, steps, forward, 0)
    if remote:
        arrive(gather(1, late))
        start(gather(2, late))
        arrive(gather(2, late))
    unpack_o(cut, G, WO)
    unpack_f(cut, G, WI, WT)
    loads[1].wait()
    for i in range(max(0, steps - 2), steps):
        for u in range(2):
            to_hbm(2 * i + u, 2 * (i % 2) + u).wait()

    def from_hbm(i, slot):
        return pltpu.make_async_copy(phbm.at[i], PB.at[slot], p_sem.at[slot])

    for u in range(2):
        from_hbm(u, u).start()

    def out_copy(i, slot):
        return pltpu.make_async_copy(OB.at[slot], out.at[rows_of(i, R), :], o_sem.at[slot])

    def mid(i, x):
        slot = lax.rem(i, 2)

        @pl.when(i >= 2)
        def _():
            out_copy(i, slot).wait()

        middle(i, tok, WO, WI, WT, SM, CTX, DC, DR, OB.at[slot], G1, G2, G3, GB, AB, SLP, XH, H1B, F)
        out_copy(i, slot).start()
        return x

    lax.fori_loop(0, nmid, mid, 0)
    if remote:
        sent(sum((gather(stage, early + late) for stage in range(3)), []))
    pack_o(cut, G3, G)
    pack_f(cut, G1, G2, G)
    if remote:
        start(scatter(0, late))
    G1[...] = jnp.zeros_like(G1)

    def backward(i, x):
        half = lax.rem(i, 2)

        @pl.when(i + 1 < steps)
        def _():
            for u in range(2):
                from_hbm(2 * i + 2 + u, 2 - 2 * half + u).start()

        if remote:
            @pl.when(i == 1)
            def _():
                arrive(scatter(0, late))
                add(links.add_twin, late)
                start(scatter(1, late))

            @pl.when(i == steps - 1)
            def _():
                arrive(scatter(1, late))
                add(links.add_u, late)
                start(scatter(2, late))

        for u in range(2):
            from_hbm(2 * i + u, 2 * half + u).wait()
        for u in range(2):
            pair = 2 * i + u
            attend_back(Q, K, V, PB.at[2 * half + u], CTX, DC, lax.div(pair, PAIRS), lax.rem(pair, PAIRS))
        return x

    lax.fori_loop(0, steps, backward, 0)
    lax.fori_loop(0, slots, lambda s, x: (qkv_grads(tok, Q, K, V, G1, GB, s), x)[1], 0)
    pack_q(cut, G1, GB, G)
    if remote:
        start(scatter(0, early))

    def gx_copy(s):
        return pltpu.make_async_copy(DR.at[rows_of(s, SL), :], gx.at[rows_of(s, SL), :], x_sem.at[s])

    def last(s, x):
        if remote:
            @pl.when(s == 1)
            def _():
                arrive(scatter(0, early))
                add(links.add_twin, early)
                start(scatter(1, early))
        token_grads(WQ, Q, K, V, DR, s)
        gx_copy(s).start()
        return x

    lax.fori_loop(0, slots, last, 0)
    if remote:
        arrive(scatter(2, late))
        for i, total in zip(late, add(links.add_v, late)):
            results[i][...] = total
        arrive(scatter(1, early))
        add(links.add_u, early)
        start(scatter(2, early))
        arrive(scatter(2, early))
        for i, total in zip(early, add(links.add_v, early)):
            results[i][...] = total
        sent(sum((scatter(stage, early + late) for stage in range(3)), []))
    else:
        for src, dst in zip(G, results):
            pltpu.sync_copy(src, dst)
    for i in range(max(0, nmid - 2), nmid):
        out_copy(i, i % 2).wait()
    for s in range(slots):
        gx_copy(s).wait()


def run_layer(cut, remote, lengths, pieces, tokens, cotangent):
    rows = tokens.shape[0]
    slots = rows // SL
    vm, hbm = pl.BlockSpec(memory_space=pltpu.VMEM), pl.BlockSpec(memory_space=pl.ANY)
    sd, vmem, dma = jax.ShapeDtypeStruct, pltpu.VMEM, pltpu.SemaphoreType.DMA
    shapes, leads = cut.shapes, [cut.lead(i) for i in range(4)]
    scratch = [vmem((rows, D), bf)] * 5 + [vmem((rows, D), f32), vmem((rows, D), bf)]
    scratch += [vmem((GROUPS, 256, 768), bf), vmem((D, D), bf), vmem((GROUPS, 256, GU), bf), vmem((GROUPS, 256, GU), bf), vmem((16, D), f32)]
    scratch += [vmem((2,) + u + s, bf) for u, s in zip(leads, shapes)]
    if remote:
        scratch += [vmem(u + s, bf) for u, s in zip(leads, shapes)]
        scratch += [vmem((u[0] - 1, u[1]) + s, bf) for u, s in zip(leads, shapes)]
        scratch += [vmem(u[1:] + s, bf) for u, s in zip(leads, shapes)]
        scratch += [vmem((u[1] - 1,) + s, bf) for u, s in zip(leads, shapes)]
    scratch += [vmem((GROUPS, GW, GU), f32)] * 2 + [vmem((D, D), f32), vmem((16, D), f32), vmem((128, 128), f32)]
    scratch += [vmem((GROUPS, R, GU), bf)] * 2 + [vmem((R, D), f32), vmem((R, D), bf), vmem((R, D), f32), vmem((2, R, D), bf)]
    scratch += [vmem((4, 2, SL, SL), bf), dma((2,)), dma((4,)), dma((2,)), dma((slots,))]
    params = dict(vmem_limit_bytes=64 * 1024 * 1024 - 65536)
    if remote:
        count = 8 * (cut.nf + cut.nq - 1)
        scratch += [dma((count,)), dma((count,))]
        params.update(collective_id=0, has_side_effects=True)
    return pl.pallas_call(
        functools.partial(layer, cut, remote),
        out_shape=(sd((rows, D), bf), sd((rows, D), bf), sd((slots * PAIRS, 2, SL, SL), bf))
        + tuple(sd(s, f32) if remote else sd((2,) + u + s, bf) for u, s in zip(leads, shapes)),
        in_specs=[pl.BlockSpec(memory_space=pltpu.SMEM)] + [vm if remote else hbm] * len(pieces) + [hbm, hbm],
        out_specs=(hbm, hbm, hbm) + (vm if remote else hbm,) * 4,
        scratch_shapes=scratch,
        compiler_params=pltpu.CompilerParams(**params),
    )(lengths, *pieces, tokens, cotangent)


def finish(cut, qa, qb, ow, fw, out, gx, g_qkv, g_in, g_out, g_bias, g_gain, g_wo, out2, gx2, SC):
    r, b = cut.r, cut.b
    out2[...] = out[...]
    gx2[...] = gx[...]

    @pl.when(pl.program_id(0) == 0)
    def _():
        g_qkv[...] = jnp.concatenate([qa[:, :GW], qa[:, GW:], qb[:, :GW]], 0)
        g_wo[...] = ow[...]
        for g in range(GROUPS):
            g_in[g] = fw[0, :, g * b:(g + 1) * b]
            g_out[g] = fw[1, :, g * b:(g + 1) * b]
        SC[...] = jnp.zeros_like(SC)
        SC[0:r, :] = qb[:, 128:]
        small = SC[...].T
        g_bias[...] = small[64:74, 0:r]
        g_gain[...] = small[74:76, 0:r]


def run_finish(cut, parts, out, gx):
    rows = out.shape[0]
    r, a, b = cut.r, cut.a, cut.b
    steps = 2
    sd = jax.ShapeDtypeStruct
    tile = pl.BlockSpec((rows // steps, D), lambda i: (i, 0))

    def whole(shape):
        return pl.BlockSpec(shape, lambda i: (0,) * len(shape))

    small = ((3 * r, GW), (GROUPS, a, b), (GROUPS, a, b), (10, r), (2, r), (r, D))
    return pl.pallas_call(
        functools.partial(finish, cut),
        grid=(steps,),
        out_shape=tuple(sd(s, f32) for s in small) + (sd((rows, D), bf),) * 2,
        in_specs=[whole(p.shape) for p in parts] + [tile, tile],
        out_specs=tuple(whole(s) for s in small) + (tile, tile),
        scratch_shapes=[pltpu.VMEM((128, 128), f32)],
    )(*parts, out, gx)


def on_device(cut, tokens, lengths, qkv_weight, out_weight, ffn_in_weight, ffn_out_weight, biases, gains, cotangent):
    pieces = (qkv_weight, out_weight, ffn_in_weight, jnp.swapaxes(ffn_out_weight, 1, 2), biases, gains)
    out, gx, _, *parts = run_layer(cut, True, lengths, pieces, tokens, cotangent)
    g_qkv, g_in, g_out, g_bias, g_gain, g_wo, out, gx = run_finish(cut, parts, out, gx)
    return out, gx, g_qkv, g_wo, g_in, jnp.swapaxes(g_out, 1, 2), g_bias, g_gain


def solution(mesh):
    both = ("dp", "ffn")
    P = PartitionSpec
    return jax.shard_map(
        functools.partial(on_device, Cut(mesh.shape["dp"] // 2, mesh.shape["ffn"])),
        mesh=mesh,
        in_specs=(P(both, None), P(both), P(both, None), P(both, None), P(None, "dp", "ffn"),
                  P(None, "ffn", "dp"), P(None, both), P(None, both), P(both, None)),
        out_specs=(P(both, None), P(both, None), P(both, None), P(both, None), P(None, "dp", "ffn"),
                   P(None, "ffn", "dp"), P(None, both), P(None, both)),
        check_vma=False,
    )
```

```python
import functools

import jax
import jax.numpy as jnp
from jax import lax
from jax.experimental import pallas as pl
from jax.experimental.pallas import tpu as pltpu
from jax.sharding import PartitionSpec

f32, bf = jnp.float32, jnp.bfloat16
EPS, NEG = 1e-12, -1e30
SL, D, HEADS, GROUPS, GW, GU = 512, 768, 12, 4, 192, 768
PAIRS = D // 128
R = 256
UP = 2
MESH = pl.DeviceIdType.MESH


def dg(a, b, ca, cb):
    return lax.dot_general(a, b, (((ca,), (cb,)), ((), ())), preferred_element_type=f32)


def nn(a, b):
    return dg(a, b, 1, 0)


def nt(a, b):
    return dg(a, b, 1, 1)


def tn(a, b):
    return dg(a, b, 0, 0)


def win(g):
    return 128 * ((GW * g) // 128)


def off(g):
    return 64 * (g % 2)


def halves(t):
    lane = lax.broadcasted_iota(jnp.int32, t.shape, 1)
    z = jnp.zeros_like(t)
    return jnp.where(lane < 64, t, z), jnp.where(lane < 64, z, t)


def rowsum(x):
    return jnp.sum(x, axis=1, keepdims=True)


def ln_fwd(r):
    c = r - rowsum(r) * (1.0 / D)
    inv = lax.rsqrt(rowsum(c * c) * (1.0 / D) + EPS)
    return c * inv, inv


def ln_bwd(gy, xh, inv, gamma):
    e = gy * gamma
    return inv * (e - rowsum(e) * (1.0 / D) - xh * (rowsum(e * xh) * (1.0 / D)))


def rows_of(i, size):
    return pl.ds(pl.multiple_of(i * size, size), size)


def project(tok, wq, bias, Q, K, V, s):
    rows = rows_of(s, SL)
    for S in range(2):
        b = 384 * S
        y0, y1 = nn(tok[rows, b:b + 256], wq[2 * S]), nn(tok[rows, b + 128:b + 384], wq[2 * S + 1])
        for part, (dst, brow) in enumerate(((Q, 4), (K, None), (V, 5))):
            c = 256 * part
            tiles = (y0[:, c:c + 128], y0[:, c + 128:c + 256] + y1[:, c:c + 128], y1[:, c + 128:c + 256])
            for i, t in enumerate(tiles):
                cols = slice(b + 128 * i, b + 128 * i + 128)
                if brow is not None:
                    t = t + bias[brow:brow + 1, cols]
                t = t.astype(bf)
                if part == 0:
                    t = t * jnp.asarray(0.125, bf)
                dst[rows, cols] = t


def attend(Q, K, V, P, CTX, LI, maskrow, s, p, T=256):
    r0 = pl.multiple_of(s * SL, SL)
    rows, cols = pl.ds(r0, SL), rows_of(p, 128)
    k = K[rows, cols]
    vcat = jnp.concatenate([jnp.concatenate([a, b], 1) for a, b in
                            zip(halves(V[rows, cols]), halves(jnp.ones((SL, 128), bf)))], 0)
    for t in range(SL // T):
        rt = pl.ds(r0 + t * T, T)
        pbs = []
        for h, q in enumerate(halves(Q[rt, cols])):
            sc = nt(q, k) + maskrow
            pb = jnp.exp(sc - jnp.max(sc, axis=1, keepdims=True)).astype(bf)
            P[h, t * T:(t + 1) * T] = pb
            pbs.append(pb)
        r = nn(jnp.concatenate(pbs, 1), vcat)
        li = 1.0 / r[:, 128:]
        CTX[rt, cols] = r[:, :128] * li
        LI[rt, cols] = li.astype(bf)


def attend_back(Q, K, V, P, CTX, DC, s, p, T=256):
    r0 = pl.multiple_of(s * SL, SL)
    rows, cols = pl.ds(r0, SL), rows_of(p, 128)
    q, k, v, dc = Q[rows, cols], K[rows, cols], V[rows, cols], DC[rows, cols]
    kcat = jnp.concatenate(halves(k), 0)
    dss = [[], []]
    for t in range(SL // T):
        rt = pl.ds(r0 + t * T, T)
        dct = dc[t * T:(t + 1) * T]
        dcs, prods = halves(dct), halves(dct.astype(f32) * CTX[rt, cols])
        row = []
        for h in range(2):
            dp = nt(dcs[h], v) - rowsum(prods[h])
            ds = (P[h, t * T:(t + 1) * T].astype(f32) * dp).astype(bf)
            dss[h].append(ds)
            row.append(ds)
        Q[rt, cols] = (nn(jnp.concatenate(row, 1), kcat) * 0.125).astype(bf)
    dk, dv = [], []
    for h in range(2):
        dk.append(tn(q, jnp.concatenate(dss[h], 0))[64 * h:64 * h + 64])
        dv.append(tn(dc, P[h])[64 * h:64 * h + 64])
    K[rows, cols] = jnp.concatenate(dk, 0).T.astype(bf)
    V[rows, cols] = jnp.concatenate(dv, 0).T.astype(bf)


CH = 32


def fold(x):
    return jnp.sum(x.reshape(-1, 8, x.shape[-1]), axis=0)


def gelu_pair(u):
    c = 1.0 + lax.erf(u * 0.7071067811865476)
    return u * c, c + (0.7978845608028654 * u) * jnp.exp2((-0.7213475204444817 * u) * u)


def tile(i, tok, WO, WI, WT, bias, CTX, DC, DR, OB, GB, AB, SLP, H1B, DB, DA, XH, F, INV):
    r0 = pl.multiple_of(i * R, R)
    rows = pl.ds(r0, R)
    parts = [(slice(k, k + CH), pl.ds(r0 + k, CH)) for k in range(0, R, CH)]
    y = nn(CTX[rows, :].astype(bf), WO[...])
    for here, there in parts:
        xh1, inv1 = ln_fwd(y[here] + bias[6:7, :] + tok[there, :].astype(f32))
        XH[here, :] = xh1
        INV[here, :] = jnp.broadcast_to(inv1, (CH, 128))
        h1 = xh1 * bias[10:11, :] + bias[7:8, :]
        H1B[here, :] = h1.astype(bf)
        F[here, :] = h1 + bias[8:9, :]
        yield 1
    for g in range(GROUPS):
        w = slice(win(g), win(g) + 256)
        AB[g], SLP[g] = gelu_pair((nn(H1B[:, w], WI[g]) + bias[g:g + 1, :]).astype(bf))
        F[:, w] += nt(AB[g], WT[g])
        yield 0
    sums = [0.0, 0.0, 0.0]
    for here, there in parts:
        xh2, inv2 = ln_fwd(F[here, :])
        OB[here, :] = (xh2 * bias[11:12, :] + bias[9:10, :]).astype(bf)
        gy = DC[there, :].astype(f32)
        dr2 = ln_bwd(gy, xh2, inv2, bias[11:12, :])
        F[here, :] = dr2
        DB[here, :] = dr2.astype(bf)
        sums = [s + fold(x) for s, x in zip(sums, (gy * xh2, gy, dr2))]
        yield 1
    for k, s in zip((11, 9, 8), sums):
        GB[k] += s
    for g in range(GROUPS):
        w = slice(win(g), win(g) + 256)
        SLP[g] = nn(DB[:, w], WT[g]).astype(bf) * SLP[g]
        F[:, w] += nt(SLP[g], WI[g])
        yield 0
    sums = [0.0, 0.0, 0.0]
    for here, there in parts:
        xh1, dh1 = XH[here, :], F[here, :]
        dr1 = ln_bwd(dh1, xh1, INV[here, 0:1], bias[10:11, :])
        DA[here, :] = dr1.astype(bf)
        sums = [s + fold(x) for s, x in zip(sums, (dh1 * xh1, dh1, dr1))]
        yield 1
    for k, s in zip((10, 7, 6), sums):
        GB[k] += s
    y = nt(DA[...], WO[...])
    for here, there in parts:
        DC[there, :] = (y[here] * DR[there, :].astype(f32)).astype(bf)
    DR[rows, :] = DA[...]
    yield 0


def weights(i, CTX, G1, G2, G3, GB, AB, SLP, H1B, DB, DA):
    lane = lax.broadcasted_iota(jnp.int32, (R, 256), 1)
    rows = rows_of(i, R)
    for k in range(0, D, 256):
        G3[k:k + 256, :] += tn(CTX[rows, k:k + 256].astype(bf), DA[...])
        yield
    for g in range(GROUPS):
        w = slice(win(g), win(g) + 256)
        o, z = off(g), 0 if off(g) else GW
        mine = jnp.where((lane >= o) & (lane < o + GW), H1B[:, w], jnp.ones((R, 256), bf))
        t = tn(mine, SLP[g])
        G1[g] += t[o:o + GW]
        GB[g, 0:1, :] += t[z:z + 1]
        yield
        G2[g] += tn(DB[:, w], AB[g])[o:o + GW]
        yield


PER = 0.5


def weave(main, side):
    credit = 0.0
    for kind in main:
        credit += PER * kind
        while credit >= 1:
            credit -= 1
            next(side, None)
    for _ in side:
        pass


def middle(i, tok, WO, WI, WT, bias, CTX, DC, DR, OB, G1, G2, G3, GB, AB, SLP, H1B, DB, DA, XH, F, INV):
    for u in range(2):
        now, last = 2 * i + u, jnp.maximum(2 * i + u - 1, 0)
        v = 1 - u
        weave(tile(now, tok, WO, WI, WT, bias, CTX, DC, DR, OB.at[u * R:(u + 1) * R], GB, AB.at[u], SLP.at[u], H1B.at[u], DB.at[u], DA.at[u], XH, F, INV),
              weights(last, CTX, G1, G2, G3, GB, AB.at[v], SLP.at[v], H1B.at[v], DB.at[v], DA.at[v]))


def qkv_grads(tok, Q, K, V, G1, GB, s):
    rows = rows_of(s, SL)
    for g in range(GROUPS):
        w = slice(win(g), win(g) + 256)
        d3 = jnp.concatenate([Q[rows, w], K[rows, w], V[rows, w]], axis=1)
        G1[g] += tn(tok[rows, w], d3)[off(g):off(g) + GW]
    GB[4] += fold(Q[rows, :].astype(f32))
    GB[5] += fold(V[rows, :].astype(f32))


def token_grads(wq, Q, K, V, DR, s):
    rows = rows_of(s, SL)
    for S in range(2):
        b, ys = 384 * S, []
        for g in (2 * S, 2 * S + 1):
            w = slice(win(g), win(g) + 256)
            ys.append(nt(jnp.concatenate([Q[rows, w], K[rows, w], V[rows, w]], axis=1), wq[g]))
        tiles = (ys[0][:, :128], ys[0][:, 128:] + ys[1][:, :128], ys[1][:, 128:])
        for i, t in enumerate(tiles):
            cols = slice(b + 128 * i, b + 128 * i + 128)
            DR[rows, cols] = (t + DR[rows, cols].astype(f32)).astype(bf)


QA, QB, OW, FW = range(4)
GATHER = ("qf", "qf", "fq", "qf")
SCATTER = ("qf", "fq", "fq", "qf")


class Cut:
    def __init__(self, nq, nf):
        self.nq, self.nf = nq, nf
        self.n = 2 * nq * nf
        self.r = D // self.n
        self.a, self.b = GW // (2 * nq), GU // nf
        self.shapes = ((self.r, 2 * GW), (self.r, 256), (self.r, D), (2, self.a, GROUPS * self.b))

    def lead(self, i):
        return (self.nq, self.nf) if SCATTER[i] == "qf" else (self.nf, self.nq)

    def place(self, order, q, f):
        return q * self.nf + f if order == "qf" else f * self.nq + q

    def at(self, order, d):
        dp, f = divmod(d, self.nf)
        return dp % 2, self.place(order, dp // 2, f)


def put_pieces(cut, at, qkv, wo, wi, wt, biases, gains, SC, G):
    r = cut.r
    SC[...] = jnp.zeros_like(SC)
    SC[0:10, 0:r] = biases[...].astype(f32)
    SC[10:12, 0:r] = gains[...].astype(f32)
    rows = qkv[...].astype(f32)
    G[QA][at[QA]] = jnp.concatenate([rows[:r], rows[r:2 * r]], 1).astype(bf)
    G[QB][at[QB]] = jnp.concatenate([rows[2 * r:], SC[...].T[:r, :64]], 1).astype(bf)
    G[OW][at[OW]] = wo[...]
    for k, w in enumerate((wi, wt)):
        G[FW][at[FW] + (k,)] = jnp.concatenate([w[g].astype(f32) for g in range(GROUPS)], 1).astype(bf)


def unpack_q(cut, G, WQ, SM):
    WQ[...] = jnp.zeros_like(WQ)
    r = cut.r
    for p in range(3):
        for g in range(GROUPS):
            parts = []
            for i in range(GW // r):
                d, j = divmod((D * p + GW * g) // r + i, 3)
                if j < 2:
                    parts.append(G[QA][cut.at(GATHER[QA], d)].astype(f32)[:, GW * j:GW * (j + 1)])
                else:
                    parts.append(G[QB][cut.at(GATHER[QB], d)].astype(f32)[:, :GW])
            o = off(g)
            WQ[g, o:o + GW, 256 * p + o:256 * p + o + GW] = jnp.concatenate(parts, 0).astype(bf)
    small = jnp.concatenate([G[QB][cut.at(GATHER[QB], d)][:, 128:].astype(f32) for d in range(cut.n)], 0)
    SM[...] = small.T[64:80]


def unpack_o(cut, G, WO):
    per = GW // cut.r
    for i in range(D // GW):
        rows = [G[OW][cut.at(GATHER[OW], d)].astype(f32) for d in range(per * i, per * i + per)]
        WO[GW * i:GW * (i + 1), :] = jnp.concatenate(rows, 0).astype(bf)


def unpack_f(cut, G, WI, WT):
    b = cut.b
    for k, W in enumerate((WI, WT)):
        for g in range(GROUPS):
            o = off(g)
            z = 0 if o else GW
            W[g, z:z + 64] = jnp.zeros((64, GU), bf)
            cols = []
            for f in range(cut.nf):
                cols.append(jnp.concatenate(
                    [G[FW][cut.at(GATHER[FW], dp * cut.nf + f)][k].astype(f32)[:, g * b:(g + 1) * b] for dp in range(2 * cut.nq)], 0))
            w = jnp.concatenate(cols, 1)
            W[g, o:o + GW] = (0.5 * w if k else w).astype(bf)


def pack_o(cut, G3, G):
    for d in range(cut.n):
        G[OW][cut.at(SCATTER[OW], d)] = G3[cut.r * d:cut.r * (d + 1), :].astype(bf)


def pack_f(cut, G1, G2, G):
    a, b = cut.a, cut.b
    for k, grad in enumerate((G1, G2)):
        for dp in range(2 * cut.nq):
            for f in range(cut.nf):
                t = jnp.concatenate([grad[g, a * dp:a * (dp + 1), b * f:b * (f + 1)] for g in range(GROUPS)], 1)
                G[FW][cut.at(SCATTER[FW], dp * cut.nf + f) + (k,)] = (0.5 * t if k else t).astype(bf)


def pack_q(cut, G1, GB, G):
    r = cut.r
    small = jnp.concatenate([jnp.zeros((64, D), f32), jnp.sum(GB[...], axis=1), jnp.zeros((48, D), f32)], 0).T
    for d in range(cut.n):
        parts = []
        for j in range(3):
            p, rest = divmod(r * (3 * d + j), D)
            g, i = divmod(rest, GW)
            c = 256 * p + off(g)
            parts.append(G1[g, i:i + r, c:c + GW])
        G[QA][cut.at(SCATTER[QA], d)] = jnp.concatenate(parts[:2], 1).astype(bf)
        G[QB][cut.at(SCATTER[QB], d)] = jnp.concatenate([parts[2], small[r * d:r * (d + 1), 64:]], 1).astype(bf)


class Links:
    def __init__(self, cut, send_sem, recv_sem):
        self.cut, self.sems = cut, (send_sem, recv_sem)
        dp, self.f = lax.axis_index("dp"), lax.axis_index("ffn")
        self.c, self.q = lax.rem(dp, 2), lax.div(dp, 2)
        nq, nf = cut.nq, cut.nf
        fs = [lax.rem(self.f + k, nf) for k in range(1, nf)]
        qs = [lax.rem(self.q + k, nq) for k in range(1, nq)]
        to_f = [(2 * self.q + self.c, f) for f in fs]
        to_q = [(2 * q + self.c, self.f) for q in qs]
        self.twin = (2 * self.q + 1 - self.c, self.f)
        self.axis = {"q": (self.q, qs, to_q), "f": (self.f, fs, to_f)}
        self.per = nf + nq - 1

    def at(self, i):
        return self.c, self.cut.place(GATHER[i], self.q, self.f)

    def greet(self):
        barrier = pltpu.get_barrier_semaphore()
        everyone = self.axis["q"][2] + self.axis["f"][2] + [self.twin]
        for peer in everyone:
            pl.semaphore_signal(barrier, inc=1, device_id=peer, device_id_type=MESH)
        return lambda: pl.semaphore_wait(barrier, len(everyone))

    def copy(self, src, dst, slot, peer):
        return pltpu.make_async_remote_copy(
            src_ref=src, dst_ref=dst, send_sem=self.sems[0].at[slot], recv_sem=self.sems[1].at[slot],
            device_id=peer, device_id_type=MESH)

    def gather(self, stage, i, G):
        base, c = i * self.per, self.c
        (u, us, to_u), (v, vs, to_v) = (self.axis[x] for x in GATHER[i])
        size = len(vs) + 1
        if stage == 0:
            mine = G.at[c, u * size + v]
            return [self.copy(mine, mine, base + k, to_v[k]) for k in range(len(vs))]
        base += len(vs)
        if stage == 1:
            mine = G.at[c, pl.ds(u * size, size)]
            return [self.copy(mine, mine, base + k, to_u[k]) for k in range(len(us))]
        return [self.copy(G.at[c], G.at[c], base + len(us), self.twin)]

    def scatter(self, stage, i, G, RC, RU, Z, RV):
        base, c = (4 + i) * self.per, self.c
        (u, us, to_u), (v, vs, to_v) = (self.axis[x] for x in SCATTER[i])
        size = len(vs) + 1
        if stage == 0:
            return [self.copy(G.at[1 - c], RC, base, self.twin)]
        base += 1
        if stage == 1:
            return [self.copy(G.at[c, pl.ds(us[k] * size, size)], RU.at[k], base + k, to_u[k]) for k in range(len(us))]
        base += len(us)
        return [self.copy(Z.at[vs[k]], RV.at[k], base + k, to_v[k]) for k in range(len(vs))]

    def add_twin(self, i, G, RC, RU, Z, RV):
        for k in range(RC.shape[0]):
            G[self.c, k] = (G[self.c, k].astype(f32) + RC[k].astype(f32)).astype(bf)

    def add_u(self, i, G, RC, RU, Z, RV):
        size = Z.shape[0]
        total = G[self.c, pl.ds(self.axis[SCATTER[i][0]][0] * size, size)].astype(f32)
        for k in range(RU.shape[0]):
            total = total + RU[k].astype(f32)
        Z[...] = total.astype(bf)

    def add_v(self, i, G, RC, RU, Z, RV):
        total = Z[self.axis[SCATTER[i][1]][0]].astype(f32)
        for k in range(RV.shape[0]):
            total = total + RV[k].astype(f32)
        return total


def start(copies):
    for copy in copies:
        copy.start()


def arrive(copies):
    for copy in copies:
        copy.wait_recv()


def sent(copies):
    for copy in copies:
        copy.wait_send()


def layer(cut, remote, length, *refs):
    count = 6 if remote else 4
    pieces, refs = refs[:count], refs[count:]
    tok_in, cot_in, out, gx, phbm = refs[:5]
    results, refs = refs[5:9], refs[9:]
    tok, DC, Q, K, V, CTX, DR, WQ, WO, WI, WT, SM = refs[:12]
    G, refs = refs[12:16], refs[16:]
    if remote:
        parts, refs = [refs[4 * k:4 * k + 4] for k in range(4)], refs[16:]
        RC, RU, Z, RV = parts
    G1, G2, G3, GB, SC, AB, SLP, H1B, DB, DA, XH, F, INV, OB, PB, in_sem, p_sem, o_sem, x_sem = refs[:19]
    slots = tok.shape[0] // SL
    nmid = tok.shape[0] // (2 * R)
    links = Links(cut, *refs[19:]) if remote else None

    def gather(stage, which):
        return sum((links.gather(stage, i, G[i]) for i in which), [])

    def scatter(stage, which):
        return sum((links.scatter(stage, i, G[i], RC[i], RU[i], Z[i], RV[i]) for i in which), [])

    def add(step, which):
        return [step(i, G[i], RC[i], RU[i], Z[i], RV[i]) for i in which]

    early, late = (QA, QB), (OW, FW)
    if remote:
        met = links.greet()
    loads = [pltpu.make_async_copy(tok_in, tok, in_sem.at[0]), pltpu.make_async_copy(cot_in, DC, in_sem.at[1])]
    start(loads)
    if remote:
        put_pieces(cut, [links.at(i) for i in range(4)], *pieces, SC, G)
        met()
        start(gather(0, early))
    else:
        for src, dst in zip(pieces, G):
            pltpu.sync_copy(src, dst)
    for g in (G1, G2, G3, GB):
        g[...] = jnp.zeros_like(g)
    if remote:
        arrive(gather(0, early))
        start(gather(1, early))
        start(gather(0, (FW,)))
        arrive(gather(1, early))
        start(gather(2, early))
        start(gather(0, (OW,)))
        arrive(gather(2, early))
    unpack_q(cut, G, WQ, SM)
    if remote:
        arrive(gather(0, late))
        start(gather(1, late))
    loads[0].wait()
    lax.fori_loop(0, slots, lambda s, x: (project(tok, WQ, SM, Q, K, V, s), x)[1], 0)

    steps = slots * PAIRS // UP

    def to_hbm(i, slot):
        return pltpu.make_async_copy(PB.at[slot], phbm.at[i], p_sem.at[slot])

    def forward(i, x):
        half = lax.rem(i, 2)

        @pl.when(i >= 2)
        def _():
            for u in range(UP):
                to_hbm(UP * i + u, UP * half + u).wait()

        if remote:
            @pl.when(i == steps - 2)
            def _():
                arrive(gather(1, late))
                start(gather(2, late))

        for u in range(UP):
            pair = UP * i + u
            s = lax.div(pair, PAIRS)
            lane = lax.broadcasted_iota(jnp.int32, (1, SL), 1)
            maskrow = jnp.where(lane < length[s], 0.0, NEG)
            attend(Q, K, V, PB.at[UP * half + u], CTX, DR, maskrow, s, lax.rem(pair, PAIRS))
        for u in range(UP):
            to_hbm(UP * i + u, UP * half + u).start()
        return x

    lax.fori_loop(0, steps, forward, 0)
    if remote:
        arrive(gather(2, late))
    unpack_o(cut, G, WO)
    unpack_f(cut, G, WI, WT)
    loads[1].wait()
    for i in range(max(0, steps - 2), steps):
        for u in range(UP):
            to_hbm(UP * i + u, UP * (i % 2) + u).wait()

    def from_hbm(i, slot):
        return pltpu.make_async_copy(phbm.at[i], PB.at[slot], p_sem.at[slot])

    for u in range(UP):
        from_hbm(u, u).start()

    def out_copy(i, slot):
        return pltpu.make_async_copy(OB.at[slot], out.at[rows_of(i, 2 * R), :], o_sem.at[slot])

    def mid(i, x):
        @pl.when(i >= 1)
        def _():
            out_copy(i, 0).wait()

        middle(i, tok, WO, WI, WT, SM, CTX, DC, DR, OB.at[0], G1, G2, G3, GB, AB, SLP, H1B, DB, DA, XH, F, INV)
        out_copy(i, 0).start()
        return x

    for ref in (AB, SLP, H1B, DB, DA):
        ref[1] = jnp.zeros(ref.shape[1:], bf)
    lax.fori_loop(0, nmid, mid, 0)
    for _ in weights(2 * nmid - 1, CTX, G1, G2, G3, GB, AB.at[1], SLP.at[1], H1B.at[1], DB.at[1], DA.at[1]):
        pass
    if remote:
        sent(sum((gather(stage, early + late) for stage in range(3)), []))
    pack_o(cut, G3, G)
    pack_f(cut, G1, G2, G)
    if remote:
        start(scatter(0, late))
    G1[...] = jnp.zeros_like(G1)

    def backward(i, x):
        half = lax.rem(i, 2)

        @pl.when(i + 1 < steps)
        def _():
            for u in range(UP):
                from_hbm(UP * i + UP + u, UP - UP * half + u).start()

        if remote:
            @pl.when(i == 2)
            def _():
                arrive(scatter(0, late))
                add(links.add_twin, late)
                start(scatter(1, late))

        for u in range(UP):
            from_hbm(UP * i + u, UP * half + u).wait()
        for u in range(UP):
            pair = UP * i + u
            attend_back(Q, K, V, PB.at[UP * half + u], CTX, DC, lax.div(pair, PAIRS), lax.rem(pair, PAIRS))
        return x

    lax.fori_loop(0, steps, backward, 0)
    if remote:
        arrive(scatter(1, late))
        add(links.add_u, late)
        start(scatter(2, late))
    lax.fori_loop(0, slots, lambda s, x: (qkv_grads(tok, Q, K, V, G1, GB, s), x)[1], 0)
    pack_q(cut, G1, GB, G)
    if remote:
        start(scatter(0, early))

    def gx_copy(s):
        return pltpu.make_async_copy(DR.at[rows_of(s, SL), :], gx.at[rows_of(s, SL), :], x_sem.at[s])

    def final(s, x):
        if remote:
            @pl.when(s == 1)
            def _():
                arrive(scatter(0, early))
                add(links.add_twin, early)
                start(scatter(1, early))
        token_grads(WQ, Q, K, V, DR, s)
        gx_copy(s).start()
        return x

    lax.fori_loop(0, slots, final, 0)
    if remote:
        arrive(scatter(2, late))
        for i, total in zip(late, add(links.add_v, late)):
            results[i][...] = total
        arrive(scatter(1, early))
        add(links.add_u, early)
        start(scatter(2, early))
        arrive(scatter(2, early))
        for i, total in zip(early, add(links.add_v, early)):
            results[i][...] = total
        sent(sum((scatter(stage, late + early) for stage in range(3)), []))
    else:
        for src, dst in zip(G, results):
            pltpu.sync_copy(src, dst)
    out_copy(nmid - 1, 0).wait()
    for s in range(slots):
        gx_copy(s).wait()


def run_layer(cut, remote, lengths, pieces, tokens, cotangent):
    rows = tokens.shape[0]
    slots = rows // SL
    vm, hbm = pl.BlockSpec(memory_space=pltpu.VMEM), pl.BlockSpec(memory_space=pl.ANY)
    sd, vmem, dma = jax.ShapeDtypeStruct, pltpu.VMEM, pltpu.SemaphoreType.DMA
    shapes, leads = cut.shapes, [cut.lead(i) for i in range(4)]
    scratch = [vmem((rows, D), bf)] * 5 + [vmem((rows, D), f32), vmem((rows, D), bf)]
    scratch += [vmem((GROUPS, 256, 768), bf), vmem((D, D), bf), vmem((GROUPS, 256, GU), bf), vmem((GROUPS, 256, GU), bf), vmem((16, D), f32)]
    scratch += [vmem((2, u[0] * u[1]) + s, bf) for u, s in zip(leads, shapes)]
    if remote:
        back = list(zip(leads, shapes))
        scratch += [vmem((u[0] * u[1],) + s, bf) for u, s in back]
        scratch += [vmem((u[0] - 1, u[1]) + s, bf) for u, s in back]
        scratch += [vmem(u[1:] + s, bf) for u, s in back]
        scratch += [vmem((u[1] - 1,) + s, bf) for u, s in back]
    scratch += [vmem((GROUPS, GW, GU), f32)] * 2 + [vmem((D, D), f32), vmem((16, 8, D), f32), vmem((128, 128), f32)]
    scratch += [vmem((2, GROUPS, R, GU), bf)] * 2 + [vmem((2, R, D), bf)] * 3 + [vmem((R, D), f32)] * 2
    scratch += [vmem((R, 128), f32), vmem((1, 2 * R, D), bf)]
    scratch += [vmem((2 * UP, 2, SL, SL), bf), dma((2,)), dma((4,)), dma((2,)), dma((slots,))]
    params = dict(vmem_limit_bytes=64 * 1024 * 1024 - 65536)
    if remote:
        count = 8 * (cut.nf + cut.nq - 1)
        scratch += [dma((count,)), dma((count,))]
        params.update(collective_id=0, has_side_effects=True)
    return pl.pallas_call(
        functools.partial(layer, cut, remote),
        out_shape=(sd((rows, D), bf), sd((rows, D), bf), sd((slots * PAIRS, 2, SL, SL), bf))
        + tuple(sd(s, f32) if remote else sd((2, u[0] * u[1]) + s, bf) for u, s in zip(leads, shapes)),
        in_specs=[pl.BlockSpec(memory_space=pltpu.SMEM)] + [vm if remote else hbm] * len(pieces) + [hbm, hbm],
        out_specs=(hbm, hbm, hbm) + (vm if remote else hbm,) * 4,
        scratch_shapes=scratch,
        compiler_params=pltpu.CompilerParams(**params),
    )(lengths, *pieces, tokens, cotangent)


def finish(cut, qa, qb, ow, fw, out, gx, g_qkv, g_in, g_out, g_bias, g_gain, g_wo, out2, gx2, SC):
    r, b = cut.r, cut.b
    out2[...] = out[...]
    gx2[...] = gx[...]

    @pl.when(pl.program_id(0) == 0)
    def _():
        g_qkv[...] = jnp.concatenate([qa[:, :GW], qa[:, GW:], qb[:, :GW]], 0)
        g_wo[...] = ow[...]
        for g in range(GROUPS):
            g_in[g] = fw[0, :, g * b:(g + 1) * b]
            g_out[g] = fw[1, :, g * b:(g + 1) * b]
        SC[...] = jnp.zeros_like(SC)
        SC[0:r, :] = qb[:, 128:]
        small = SC[...].T
        g_bias[...] = small[64:74, 0:r]
        g_gain[...] = small[74:76, 0:r]


def run_finish(cut, parts, out, gx):
    rows = out.shape[0]
    r, a, b = cut.r, cut.a, cut.b
    steps = 2
    sd = jax.ShapeDtypeStruct
    tile = pl.BlockSpec((rows // steps, D), lambda i: (i, 0))

    def whole(shape):
        return pl.BlockSpec(shape, lambda i: (0,) * len(shape))

    small = ((3 * r, GW), (GROUPS, a, b), (GROUPS, a, b), (10, r), (2, r), (r, D))
    return pl.pallas_call(
        functools.partial(finish, cut),
        grid=(steps,),
        out_shape=tuple(sd(s, f32) for s in small) + (sd((rows, D), bf),) * 2,
        in_specs=[whole(p.shape) for p in parts] + [tile, tile],
        out_specs=tuple(whole(s) for s in small) + (tile, tile),
        scratch_shapes=[pltpu.VMEM((128, 128), f32)],
    )(*parts, out, gx)


def on_device(cut, tokens, lengths, qkv_weight, out_weight, ffn_in_weight, ffn_out_weight, biases, gains, cotangent):
    pieces = (qkv_weight, out_weight, ffn_in_weight, jnp.swapaxes(ffn_out_weight, 1, 2), biases, gains)
    out, gx, _, *parts = run_layer(cut, True, lengths, pieces, tokens, cotangent)
    g_qkv, g_in, g_out, g_bias, g_gain, g_wo, out, gx = run_finish(cut, parts, out, gx)
    return out, gx, g_qkv, g_wo, g_in, jnp.swapaxes(g_out, 1, 2), g_bias, g_gain


def solution(mesh):
    both = ("dp", "ffn")
    P = PartitionSpec
    return jax.shard_map(
        functools.partial(on_device, Cut(mesh.shape["dp"] // 2, mesh.shape["ffn"])),
        mesh=mesh,
        in_specs=(P(both, None), P(both), P(both, None), P(both, None), P(None, "dp", "ffn"),
                  P(None, "ffn", "dp"), P(None, both), P(None, both), P(both, None)),
        out_specs=(P(both, None), P(both, None), P(both, None), P(both, None), P(None, "dp", "ffn"),
                   P(None, "ffn", "dp"), P(None, both), P(None, both)),
        check_vma=False,
    )
```

```python
import functools

import jax
import jax.numpy as jnp
from jax import lax
from jax.experimental import pallas as pl
from jax.experimental.pallas import tpu as pltpu
from jax.sharding import PartitionSpec

f32, bf = jnp.float32, jnp.bfloat16
EPS, NEG = 1e-12, -1e30
SL, D, HEADS, GROUPS, GW, GU = 512, 768, 12, 4, 192, 768
PAIRS = D // 128
R = 256
MESH = pl.DeviceIdType.MESH


def dg(a, b, ca, cb):
    return lax.dot_general(a, b, (((ca,), (cb,)), ((), ())), preferred_element_type=f32)


def nn(a, b):
    return dg(a, b, 1, 0)


def nt(a, b):
    return dg(a, b, 1, 1)


def tn(a, b):
    return dg(a, b, 0, 0)


def win(g):
    return 128 * ((GW * g) // 128)


def off(g):
    return 64 * (g % 2)


def halves(t):
    lane = lax.broadcasted_iota(jnp.int32, t.shape, 1)
    z = jnp.zeros_like(t)
    return jnp.where(lane < 64, t, z), jnp.where(lane < 64, z, t)


def rowsum(x):
    return jnp.sum(x, axis=1, keepdims=True)


def ln_fwd(r):
    c = r - rowsum(r) * (1.0 / D)
    inv = lax.rsqrt(rowsum(c * c) * (1.0 / D) + EPS)
    return c * inv, inv


def ln_bwd(gy, xh, inv, gamma):
    e = gy * gamma
    return inv * (e - rowsum(e) * (1.0 / D) - xh * (rowsum(e * xh) * (1.0 / D)))


def rows_of(i, size):
    return pl.ds(pl.multiple_of(i * size, size), size)


def project(tok, wq, bias, Q, K, V, s):
    rows = rows_of(s, SL)
    for S in range(2):
        b = 384 * S
        y0, y1 = nn(tok[rows, b:b + 256], wq[2 * S]), nn(tok[rows, b + 128:b + 384], wq[2 * S + 1])
        for part, (dst, brow) in enumerate(((Q, 4), (K, None), (V, 5))):
            c = 256 * part
            tiles = (y0[:, c:c + 128], y0[:, c + 128:c + 256] + y1[:, c:c + 128], y1[:, c + 128:c + 256])
            for i, t in enumerate(tiles):
                cols = slice(b + 128 * i, b + 128 * i + 128)
                if brow is not None:
                    t = t + bias[brow:brow + 1, cols]
                t = t.astype(bf)
                if part == 0:
                    t = t * jnp.asarray(0.125, bf)
                dst[rows, cols] = t


def attend(Q, K, V, P, CTX, LI, maskrow, s, p, T=256):
    r0 = pl.multiple_of(s * SL, SL)
    rows, cols = pl.ds(r0, SL), rows_of(p, 128)
    k = K[rows, cols]
    vcat = jnp.concatenate([jnp.concatenate([a, b], 1) for a, b in
                            zip(halves(V[rows, cols]), halves(jnp.ones((SL, 128), bf)))], 0)
    for t in range(SL // T):
        rt = pl.ds(r0 + t * T, T)
        pbs = []
        for h, q in enumerate(halves(Q[rt, cols])):
            sc = nt(q, k) + maskrow
            pb = jnp.exp(sc - jnp.max(sc, axis=1, keepdims=True)).astype(bf)
            P[h, t * T:(t + 1) * T] = pb
            pbs.append(pb)
        r = nn(jnp.concatenate(pbs, 1), vcat)
        li = 1.0 / r[:, 128:]
        CTX[rt, cols] = r[:, :128] * li
        LI[rt, cols] = li.astype(bf)


def attend_back(Q, K, V, P, CTX, DC, s, p, T=256):
    r0 = pl.multiple_of(s * SL, SL)
    rows, cols = pl.ds(r0, SL), rows_of(p, 128)
    q, k, v, dc = Q[rows, cols], K[rows, cols], V[rows, cols], DC[rows, cols]
    kcat = jnp.concatenate(halves(k), 0)
    dss, dq = [[], []], []
    for t in range(SL // T):
        rt = pl.ds(r0 + t * T, T)
        dct = dc[t * T:(t + 1) * T]
        dcs, prods = halves(dct), halves(dct.astype(f32) * CTX[rt, cols])
        row = []
        for h in range(2):
            dp = nt(dcs[h], v) - rowsum(prods[h])
            ds = (P[h, t * T:(t + 1) * T].astype(f32) * dp).astype(bf)
            dss[h].append(ds)
            row.append(ds)
        dq.append((nn(jnp.concatenate(row, 1), kcat) * 0.125).astype(bf))
    dk, dv = [], []
    for h in range(2):
        dk.append(tn(q, jnp.concatenate(dss[h], 0))[64 * h:64 * h + 64])
        dv.append(tn(dc, P[h])[64 * h:64 * h + 64])
    dk, dv = jnp.concatenate(dk, 0).astype(bf).T, jnp.concatenate(dv, 0).astype(bf).T

    def put():
        Q[rows, cols] = jnp.concatenate(dq, 0)
        K[rows, cols] = dk
        V[rows, cols] = dv

    return put


CH = 32


def fold(x):
    return jnp.sum(x.reshape(-1, 8, x.shape[-1]), axis=0)


def gelu_pair(u):
    c = 1.0 + lax.erf(u * 0.7071067811865476)
    return u * c, c + (0.7978845608028654 * u) * jnp.exp2((-0.7213475204444817 * u) * u)


def tile(i, tok, WO, WI, WT, bias, CTX, DC, DR, OB, GB, AB, SLP, H1B, DB, DA, XH, F, INV):
    r0 = pl.multiple_of(i * R, R)
    rows = pl.ds(r0, R)
    parts = [(slice(k, k + CH), pl.ds(r0 + k, CH)) for k in range(0, R, CH)]
    y = nn(CTX[rows, :].astype(bf), WO[...])
    for here, there in parts:
        xh1, inv1 = ln_fwd(y[here] + bias[6:7, :] + tok[there, :].astype(f32))
        XH[here, :] = xh1
        INV[here, :] = jnp.broadcast_to(inv1, (CH, 128))
        h1 = xh1 * bias[10:11, :] + bias[7:8, :]
        H1B[here, :] = h1.astype(bf)
        F[here, :] = h1 + bias[8:9, :]
        yield 1
    for g in range(GROUPS):
        w = slice(win(g), win(g) + 256)
        AB[g], SLP[g] = gelu_pair((nn(H1B[:, w], WI[g]) + bias[g:g + 1, :]).astype(bf))
        F[:, w] += nt(AB[g], WT[g])
        yield 0
    sums = [0.0, 0.0, 0.0]
    for here, there in parts:
        xh2, inv2 = ln_fwd(F[here, :])
        y = (xh2 * bias[11:12, :] + bias[9:10, :]).astype(bf)
        OB[0, here, 0:D // 2] = y[:, :D // 2]
        OB[1, here, 0:D // 2] = y[:, D // 2:]
        gy = DC[there, :].astype(f32)
        dr2 = ln_bwd(gy, xh2, inv2, bias[11:12, :])
        F[here, :] = dr2
        DB[here, :] = dr2.astype(bf)
        sums = [s + fold(x) for s, x in zip(sums, (gy * xh2, gy, dr2))]
        yield 1
    for k, s in zip((11, 9, 8), sums):
        GB[k] += s
    for g in range(GROUPS):
        w = slice(win(g), win(g) + 256)
        SLP[g] = nn(DB[:, w], WT[g]).astype(bf) * SLP[g]
        F[:, w] += nt(SLP[g], WI[g])
        yield 0
    sums = [0.0, 0.0, 0.0]
    for here, there in parts:
        xh1, dh1 = XH[here, :], F[here, :]
        dr1 = ln_bwd(dh1, xh1, INV[here, 0:1], bias[10:11, :])
        DA[here, :] = dr1.astype(bf)
        sums = [s + fold(x) for s, x in zip(sums, (dh1 * xh1, dh1, dr1))]
        yield 1
    for k, s in zip((10, 7, 6), sums):
        GB[k] += s
    y = nt(DA[...], WO[...])
    for here, there in parts:
        DC[there, :] = (y[here] * DR[there, :].astype(f32)).astype(bf)
    DR[rows, :] = DA[...]
    yield 0


def weights(i, CTX, G1, G2, G3, GB, AB, SLP, H1B, DB, DA):
    lane = lax.broadcasted_iota(jnp.int32, (R, 256), 1)
    rows = rows_of(i, R)
    for k in range(0, D, 256):
        G3[k:k + 256, :] += tn(CTX[rows, k:k + 256].astype(bf), DA[...])
        yield
    for g in range(GROUPS):
        w = slice(win(g), win(g) + 256)
        o, z = off(g), 0 if off(g) else GW
        mine = jnp.where((lane >= o) & (lane < o + GW), H1B[:, w], jnp.ones((R, 256), bf))
        t = tn(mine, SLP[g])
        G1[g] += t[o:o + GW]
        GB[g, 0:1, :] += t[z:z + 1]
        yield
        G2[g] += tn(DB[:, w], AB[g])[o:o + GW]
        yield


PER = 0.5


def weave(main, side):
    credit = 0.0
    for kind in main:
        credit += PER * kind
        while credit >= 1:
            credit -= 1
            next(side, None)
    for _ in side:
        pass


def middle(i, tok, WO, WI, WT, bias, CTX, DC, DR, OB, G1, G2, G3, GB, AB, SLP, H1B, DB, DA, XH, F, INV):
    for u in range(2):
        now, last = 2 * i + u, jnp.maximum(2 * i + u - 1, 0)
        v = 1 - u
        weave(tile(now, tok, WO, WI, WT, bias, CTX, DC, DR, OB.at[:, u * R:(u + 1) * R], GB, AB.at[u], SLP.at[u], H1B.at[u], DB.at[u], DA.at[u], XH, F, INV),
              weights(last, CTX, G1, G2, G3, GB, AB.at[v], SLP.at[v], H1B.at[v], DB.at[v], DA.at[v]))


def qkv_grads(tok, Q, K, V, G1, GB):
    lane = lax.broadcasted_iota(jnp.int32, (tok.shape[0], 256), 1)
    for g in range(GROUPS):
        w = slice(win(g), win(g) + 256)
        o, z = off(g), 0 if off(g) else GW
        mine = jnp.where((lane >= o) & (lane < o + GW), tok[:, w], jnp.ones_like(tok[:, w]))
        t = tn(mine, jnp.concatenate([Q[:, w], K[:, w], V[:, w]], axis=1))
        G1[g] = t[o:o + GW]
        for k, c in ((4, o), (5, 512 + o)):
            GB[k, 0:1, GW * g:GW * (g + 1)] = t[z:z + 1, c:c + GW]


def token_grads(wq, Q, K, V, DR, s):
    rows = rows_of(s, SL)
    for S in range(2):
        b, ys = 384 * S, []
        for g in (2 * S, 2 * S + 1):
            w = slice(win(g), win(g) + 256)
            ys.append(nt(jnp.concatenate([Q[rows, w], K[rows, w], V[rows, w]], axis=1), wq[g]))
        tiles = (ys[0][:, :128], ys[0][:, 128:] + ys[1][:, :128], ys[1][:, 128:])
        for i, t in enumerate(tiles):
            cols = slice(b + 128 * i, b + 128 * i + 128)
            DR[rows, cols] = (t + DR[rows, cols].astype(f32)).astype(bf)


QA, QB, OW, FW = range(4)
GATHER = ("qf", "qf", "fq", "qf")
SCATTER = ("qf", "fq", "fq", "qf")


class Cut:
    def __init__(self, nq, nf):
        self.nq, self.nf = nq, nf
        self.n = 2 * nq * nf
        self.r = D // self.n
        self.a, self.b = GW // (2 * nq), GU // nf
        self.pairs = 3 if self.r % 8 == 0 else 2
        self.shapes = ((self.r, 2 * GW), (self.r, 256), (self.r, D), (2, self.a, GROUPS * self.b))

    def lead(self, i):
        return (self.nq, self.nf) if SCATTER[i] == "qf" else (self.nf, self.nq)

    def place(self, order, q, f):
        return q * self.nf + f if order == "qf" else f * self.nq + q

    def at(self, order, d):
        dp, f = divmod(d, self.nf)
        return dp % 2, self.place(order, dp // 2, f)


def put_pieces(cut, at, qkv, wo, wi, wt, biases, gains, SC, G):
    r = cut.r
    SC[...] = jnp.zeros_like(SC)
    SC[0:10, 0:r] = biases[...].astype(f32)
    SC[10:12, 0:r] = gains[...].astype(f32)
    rows = qkv[...].astype(f32)
    G[QA][at[QA]] = jnp.concatenate([rows[:r], rows[r:2 * r]], 1).astype(bf)
    G[QB][at[QB]] = jnp.concatenate([rows[2 * r:], SC[...].T[:r, :64]], 1).astype(bf)
    G[OW][at[OW]] = wo[...]
    for k, w in enumerate((wi, wt)):
        G[FW][at[FW] + (k,)] = jnp.concatenate([w[g].astype(f32) for g in range(GROUPS)], 1).astype(bf)


def unpack_q(cut, G, WQ, SM):
    WQ[...] = jnp.zeros_like(WQ)
    r = cut.r
    for p in range(3):
        for g in range(GROUPS):
            parts = []
            for i in range(GW // r):
                d, j = divmod((D * p + GW * g) // r + i, 3)
                if j < 2:
                    parts.append(G[QA][cut.at(GATHER[QA], d)].astype(f32)[:, GW * j:GW * (j + 1)])
                else:
                    parts.append(G[QB][cut.at(GATHER[QB], d)].astype(f32)[:, :GW])
            o = off(g)
            WQ[g, o:o + GW, 256 * p + o:256 * p + o + GW] = jnp.concatenate(parts, 0).astype(bf)
    small = jnp.concatenate([G[QB][cut.at(GATHER[QB], d)][:, 128:].astype(f32) for d in range(cut.n)], 0)
    SM[...] = small.T[64:80]


def unpack_o(cut, G, WO):
    per = GW // cut.r
    for i in range(D // GW):
        rows = [G[OW][cut.at(GATHER[OW], d)].astype(f32) for d in range(per * i, per * i + per)]
        WO[GW * i:GW * (i + 1), :] = jnp.concatenate(rows, 0).astype(bf)


def unpack_f(cut, G, WI, WT):
    b = cut.b
    for k, W in enumerate((WI, WT)):
        for g in range(GROUPS):
            o = off(g)
            z = 0 if o else GW
            W[g, z:z + 64] = jnp.zeros((64, GU), bf)
            cols = []
            for f in range(cut.nf):
                cols.append(jnp.concatenate(
                    [G[FW][cut.at(GATHER[FW], dp * cut.nf + f)][k].astype(f32)[:, g * b:(g + 1) * b] for dp in range(2 * cut.nq)], 0))
            w = jnp.concatenate(cols, 1)
            W[g, o:o + GW] = (0.5 * w if k else w).astype(bf)


def pack_o(cut, G3, G):
    for d in range(cut.n):
        G[OW][cut.at(SCATTER[OW], d)] = G3[cut.r * d:cut.r * (d + 1), :].astype(bf)


def pack_f(cut, G1, G2, G):
    a, b = cut.a, cut.b
    for k, grad in enumerate((G1, G2)):
        for dp in range(2 * cut.nq):
            for f in range(cut.nf):
                t = jnp.concatenate([grad[g, a * dp:a * (dp + 1), b * f:b * (f + 1)] for g in range(GROUPS)], 1)
                G[FW][cut.at(SCATTER[FW], dp * cut.nf + f) + (k,)] = (0.5 * t if k else t).astype(bf)


def pack_q(cut, G1, GB, G):
    r = cut.r
    small = jnp.concatenate([jnp.zeros((64, D), f32), jnp.sum(GB[...], axis=1), jnp.zeros((48, D), f32)], 0).T
    for d in range(cut.n):
        parts = []
        for j in range(3):
            p, rest = divmod(r * (3 * d + j), D)
            g, i = divmod(rest, GW)
            c = 256 * p + off(g)
            parts.append(G1[g, i:i + r, c:c + GW])
        G[QA][cut.at(SCATTER[QA], d)] = jnp.concatenate(parts[:2], 1).astype(bf)
        G[QB][cut.at(SCATTER[QB], d)] = jnp.concatenate([parts[2], small[r * d:r * (d + 1), 64:]], 1).astype(bf)


class Links:
    def __init__(self, cut, send_sem, recv_sem):
        self.cut, self.sems = cut, (send_sem, recv_sem)
        dp, self.f = lax.axis_index("dp"), lax.axis_index("ffn")
        self.c, self.q = lax.rem(dp, 2), lax.div(dp, 2)
        nq, nf = cut.nq, cut.nf
        fs = [lax.rem(self.f + k, nf) for k in range(1, nf)]
        qs = [lax.rem(self.q + k, nq) for k in range(1, nq)]
        to_f = [(2 * self.q + self.c, f) for f in fs]
        to_q = [(2 * q + self.c, self.f) for q in qs]
        self.twin = (2 * self.q + 1 - self.c, self.f)
        self.axis = {"q": (self.q, qs, to_q), "f": (self.f, fs, to_f)}
        self.per = nf + nq - 1

    def at(self, i):
        return self.c, self.cut.place(GATHER[i], self.q, self.f)

    def greet(self):
        barrier = pltpu.get_barrier_semaphore()
        everyone = self.axis["q"][2] + self.axis["f"][2] + [self.twin]
        for peer in everyone:
            pl.semaphore_signal(barrier, inc=1, device_id=peer, device_id_type=MESH)
        return lambda: pl.semaphore_wait(barrier, len(everyone))

    def copy(self, src, dst, slot, peer):
        return pltpu.make_async_remote_copy(
            src_ref=src, dst_ref=dst, send_sem=self.sems[0].at[slot], recv_sem=self.sems[1].at[slot],
            device_id=peer, device_id_type=MESH)

    def gather(self, stage, i, G):
        base, c = i * self.per, self.c
        (u, us, to_u), (v, vs, to_v) = (self.axis[x] for x in GATHER[i])
        size = len(vs) + 1
        if stage == 0:
            mine = G.at[c, u * size + v]
            return [self.copy(mine, mine, base + k, to_v[k]) for k in range(len(vs))]
        base += len(vs)
        if stage == 1:
            mine = G.at[c, pl.ds(u * size, size)]
            return [self.copy(mine, mine, base + k, to_u[k]) for k in range(len(us))]
        return [self.copy(G.at[c], G.at[c], base + len(us), self.twin)]

    def scatter(self, stage, i, G, RC, RU, Z, RV):
        base, c = (4 + i) * self.per, self.c
        (u, us, to_u), (v, vs, to_v) = (self.axis[x] for x in SCATTER[i])
        size = len(vs) + 1
        if stage == 0:
            return [self.copy(G.at[1 - c], RC, base, self.twin)]
        base += 1
        if stage == 1:
            return [self.copy(G.at[c, pl.ds(us[k] * size, size)], RU.at[k], base + k, to_u[k]) for k in range(len(us))]
        base += len(us)
        return [self.copy(Z.at[vs[k]], RV.at[k], base + k, to_v[k]) for k in range(len(vs))]

    def add_twin(self, i, G, RC, RU, Z, RV):
        for k in range(RC.shape[0]):
            G[self.c, k] = (G[self.c, k].astype(f32) + RC[k].astype(f32)).astype(bf)

    def add_u(self, i, G, RC, RU, Z, RV):
        size = Z.shape[0]
        total = G[self.c, pl.ds(self.axis[SCATTER[i][0]][0] * size, size)].astype(f32)
        for k in range(RU.shape[0]):
            total = total + RU[k].astype(f32)
        Z[...] = total.astype(bf)

    def add_v(self, i, G, RC, RU, Z, RV):
        total = Z[self.axis[SCATTER[i][1]][0]].astype(f32)
        for k in range(RV.shape[0]):
            total = total + RV[k].astype(f32)
        return total


def start(copies):
    for copy in copies:
        copy.start()


def arrive(copies):
    for copy in copies:
        copy.wait_recv()


def sent(copies):
    for copy in copies:
        copy.wait_send()


def layer(cut, remote, length, *refs):
    count = 6 if remote else 4
    pieces, refs = refs[:count], refs[count:]
    tok_in, cot_in, out, gx, phbm = refs[:5]
    results, refs = refs[5:9], refs[9:]
    tok, DC, Q, K, V, CTX, DR, WQ, WO, WI, WT, SM = refs[:12]
    G, refs = refs[12:16], refs[16:]
    if remote:
        parts, refs = [refs[4 * k:4 * k + 4] for k in range(4)], refs[16:]
        RC, RU, Z, RV = parts
    G1, G2, G3, GB, SC, AB, SLP, H1B, DB, DA, XH, F, INV, PB, in_sem, p_sem, o_sem, x_sem = refs[:18]
    slots = tok.shape[0] // SL
    nmid = tok.shape[0] // (2 * R)
    links = Links(cut, *refs[18:]) if remote else None

    def gather(stage, which):
        return sum((links.gather(stage, i, G[i]) for i in which), [])

    def scatter(stage, which):
        return sum((links.scatter(stage, i, G[i], RC[i], RU[i], Z[i], RV[i]) for i in which), [])

    def add(step, which):
        return [step(i, G[i], RC[i], RU[i], Z[i], RV[i]) for i in which]

    early, late = (QA, QB), (OW, FW)
    if remote:
        met = links.greet()
    loads = [pltpu.make_async_copy(tok_in, tok, in_sem.at[0]), pltpu.make_async_copy(cot_in, DC, in_sem.at[1])]
    start(loads)
    if remote:
        put_pieces(cut, [links.at(i) for i in range(4)], *pieces, SC, G)
        met()
        start(gather(0, early))
    else:
        for src, dst in zip(pieces, G):
            pltpu.sync_copy(src, dst)
    for g in (G1, G2, G3, GB):
        g[...] = jnp.zeros_like(g)
    if remote:
        arrive(gather(0, early))
        start(gather(1, early))
        start(gather(0, (FW,)))
        arrive(gather(1, early))
        start(gather(2, early))
        start(gather(0, (OW,)))
        arrive(gather(2, early))
    unpack_q(cut, G, WQ, SM)
    if remote:
        arrive(gather(0, late))
        start(gather(1, late))
    loads[0].wait()
    lax.fori_loop(0, slots, lambda s, x: (project(tok, WQ, SM, Q, K, V, s), x)[1], 0)

    UP = cut.pairs
    steps = slots * PAIRS // UP

    def to_hbm(i, slot):
        return pltpu.make_async_copy(PB.at[slot], phbm.at[i], p_sem.at[slot])

    def forward(i, x):
        half = lax.rem(i, 2)

        @pl.when(i >= 2)
        def _():
            for u in range(UP):
                to_hbm(UP * i + u, UP * half + u).wait()

        if remote:
            @pl.when(i == steps * 5 // 6)
            def _():
                arrive(gather(1, late))
                start(gather(2, late))

        for u in range(UP):
            pair = UP * i + u
            s = lax.div(pair, PAIRS)
            lane = lax.broadcasted_iota(jnp.int32, (1, SL), 1)
            maskrow = jnp.where(lane < length[s], 0.0, NEG)
            attend(Q, K, V, PB.at[UP * half + u], CTX, DR, maskrow, s, lax.rem(pair, PAIRS))
        for u in range(UP):
            to_hbm(UP * i + u, UP * half + u).start()
        return x

    lax.fori_loop(0, steps, forward, 0)
    if remote:
        arrive(gather(2, late))
    unpack_o(cut, G, WO)
    unpack_f(cut, G, WI, WT)
    loads[1].wait()
    for i in range(max(0, steps - 2), steps):
        for u in range(UP):
            to_hbm(UP * i + u, UP * (i % 2) + u).wait()

    def from_hbm(i, slot):
        return pltpu.make_async_copy(phbm.at[i], PB.at[slot], p_sem.at[slot])

    for u in range(UP):
        from_hbm(u, u).start()

    OB = PB.at[2 * UP - 1]

    def out_copy(i):
        return [pltpu.make_async_copy(OB.at[h, :, 0:D // 2], out.at[rows_of(i, 2 * R), h * (D // 2):(h + 1) * (D // 2)], o_sem.at[h])
                for h in range(2)]

    def mid(i, x):
        @pl.when(i >= 1)
        def _():
            for copy in out_copy(i):
                copy.wait()

        middle(i, tok, WO, WI, WT, SM, CTX, DC, DR, OB, G1, G2, G3, GB, AB, SLP, H1B, DB, DA, XH, F, INV)
        start(out_copy(i))
        return x

    for ref in (AB, SLP, H1B, DB, DA):
        ref[1] = jnp.zeros(ref.shape[1:], bf)
    lax.fori_loop(0, nmid, mid, 0)
    for _ in weights(2 * nmid - 1, CTX, G1, G2, G3, GB, AB.at[1], SLP.at[1], H1B.at[1], DB.at[1], DA.at[1]):
        pass
    if remote:
        sent(sum((gather(stage, early + late) for stage in range(3)), []))
    pack_o(cut, G3, G)
    pack_f(cut, G1, G2, G)
    if remote:
        start(scatter(0, late))

    for copy in out_copy(nmid - 1):
        copy.wait()

    def backward(i, x):
        half = lax.rem(i, 2)

        @pl.when(i + 1 < steps)
        def _():
            for u in range(UP):
                from_hbm(UP * i + UP + u, UP - UP * half + u).start()

        if remote:
            @pl.when(i == steps // 4)
            def _():
                arrive(scatter(0, late))
                add(links.add_twin, late)
                start(scatter(1, late))

        for u in range(UP):
            from_hbm(UP * i + u, UP * half + u).wait()
        puts = []
        for u in range(UP):
            pair = UP * i + u
            puts.append(attend_back(Q, K, V, PB.at[UP * half + u], CTX, DC, lax.div(pair, PAIRS), lax.rem(pair, PAIRS)))
        for put in puts:
            put()
        return x

    lax.fori_loop(0, steps, backward, 0)
    if remote:
        arrive(scatter(1, late))
        add(links.add_u, late)
        start(scatter(2, late))
    qkv_grads(tok, Q, K, V, G1, GB)
    pack_q(cut, G1, GB, G)
    if remote:
        start(scatter(0, early))

    def gx_copy(s):
        return pltpu.make_async_copy(DR.at[rows_of(s, SL), :], gx.at[rows_of(s, SL), :], x_sem.at[s])

    def final(s, x):
        if remote:
            @pl.when(s == 1)
            def _():
                arrive(scatter(0, early))
                add(links.add_twin, early)
                start(scatter(1, early))
        token_grads(WQ, Q, K, V, DR, s)
        gx_copy(s).start()
        return x

    lax.fori_loop(0, slots, final, 0)
    if remote:
        arrive(scatter(2, late))
        for i, total in zip(late, add(links.add_v, late)):
            results[i][...] = total
        arrive(scatter(1, early))
        add(links.add_u, early)
        start(scatter(2, early))
        arrive(scatter(2, early))
        for i, total in zip(early, add(links.add_v, early)):
            results[i][...] = total
        sent(sum((scatter(stage, late + early) for stage in range(3)), []))
    else:
        for src, dst in zip(G, results):
            pltpu.sync_copy(src, dst)
    for s in range(slots):
        gx_copy(s).wait()


def run_layer(cut, remote, lengths, pieces, tokens, cotangent):
    rows = tokens.shape[0]
    slots = rows // SL
    vm, hbm = pl.BlockSpec(memory_space=pltpu.VMEM), pl.BlockSpec(memory_space=pl.ANY)
    sd, vmem, dma = jax.ShapeDtypeStruct, pltpu.VMEM, pltpu.SemaphoreType.DMA
    shapes, leads = cut.shapes, [cut.lead(i) for i in range(4)]
    scratch = [vmem((rows, D), bf)] * 5 + [vmem((rows, D), f32), vmem((rows, D), bf)]
    scratch += [vmem((GROUPS, 256, 768), bf), vmem((D, D), bf), vmem((GROUPS, 256, GU), bf), vmem((GROUPS, 256, GU), bf), vmem((16, D), f32)]
    scratch += [vmem((2, u[0] * u[1]) + s, bf) for u, s in zip(leads, shapes)]
    if remote:
        back = list(zip(leads, shapes))
        scratch += [vmem((u[0] * u[1],) + s, bf) for u, s in back]
        scratch += [vmem((u[0] - 1, u[1]) + s, bf) for u, s in back]
        scratch += [vmem(u[1:] + s, bf) for u, s in back]
        scratch += [vmem((u[1] - 1,) + s, bf) for u, s in back]
    scratch += [vmem((GROUPS, GW, GU), f32)] * 2 + [vmem((D, D), f32), vmem((16, 8, D), f32), vmem((128, 128), f32)]
    scratch += [vmem((2, GROUPS, R, GU), bf)] * 2 + [vmem((2, R, D), bf)] * 3 + [vmem((R, D), f32)] * 2
    scratch += [vmem((R, 128), f32)]
    scratch += [vmem((2 * cut.pairs, 2, SL, SL), bf), dma((2,)), dma((2 * cut.pairs,)), dma((2,)), dma((slots,))]
    params = dict(vmem_limit_bytes=64 * 1024 * 1024 - 65536)
    if remote:
        count = 8 * (cut.nf + cut.nq - 1)
        scratch += [dma((count,)), dma((count,))]
        params.update(collective_id=0, has_side_effects=True)
    return pl.pallas_call(
        functools.partial(layer, cut, remote),
        out_shape=(sd((rows, D), bf), sd((rows, D), bf), sd((slots * PAIRS, 2, SL, SL), bf))
        + tuple(sd(s, f32) if remote else sd((2, u[0] * u[1]) + s, bf) for u, s in zip(leads, shapes)),
        in_specs=[pl.BlockSpec(memory_space=pltpu.SMEM)] + [vm if remote else hbm] * len(pieces) + [hbm, hbm],
        out_specs=(hbm, hbm, hbm) + (vm if remote else hbm,) * 4,
        scratch_shapes=scratch,
        compiler_params=pltpu.CompilerParams(**params),
    )(lengths, *pieces, tokens, cotangent)


def finish(cut, qa, qb, ow, fw, out, gx, g_qkv, g_in, g_out, g_bias, g_gain, g_wo, out2, gx2, SC):
    r, b = cut.r, cut.b
    out2[...] = out[...]
    gx2[...] = gx[...]

    @pl.when(pl.program_id(0) == 0)
    def _():
        g_qkv[...] = jnp.concatenate([qa[:, :GW], qa[:, GW:], qb[:, :GW]], 0)
        g_wo[...] = ow[...]
        for g in range(GROUPS):
            g_in[g] = fw[0, :, g * b:(g + 1) * b]
            g_out[g] = fw[1, :, g * b:(g + 1) * b]
        SC[...] = jnp.zeros_like(SC)
        SC[0:r, :] = qb[:, 128:]
        small = SC[...].T
        g_bias[...] = small[64:74, 0:r]
        g_gain[...] = small[74:76, 0:r]


def run_finish(cut, parts, out, gx):
    rows = out.shape[0]
    r, a, b = cut.r, cut.a, cut.b
    steps = 2
    sd = jax.ShapeDtypeStruct
    tile = pl.BlockSpec((rows // steps, D), lambda i: (i, 0))

    def whole(shape):
        return pl.BlockSpec(shape, lambda i: (0,) * len(shape))

    small = ((3 * r, GW), (GROUPS, a, b), (GROUPS, a, b), (10, r), (2, r), (r, D))
    return pl.pallas_call(
        functools.partial(finish, cut),
        grid=(steps,),
        out_shape=tuple(sd(s, f32) for s in small) + (sd((rows, D), bf),) * 2,
        in_specs=[whole(p.shape) for p in parts] + [tile, tile],
        out_specs=tuple(whole(s) for s in small) + (tile, tile),
        scratch_shapes=[pltpu.VMEM((128, 128), f32)],
    )(*parts, out, gx)


def on_device(cut, tokens, lengths, qkv_weight, out_weight, ffn_in_weight, ffn_out_weight, biases, gains, cotangent):
    pieces = (qkv_weight, out_weight, ffn_in_weight, jnp.swapaxes(ffn_out_weight, 1, 2), biases, gains)
    out, gx, _, *parts = run_layer(cut, True, lengths, pieces, tokens, cotangent)
    g_qkv, g_in, g_out, g_bias, g_gain, g_wo, out, gx = run_finish(cut, parts, out, gx)
    return out, gx, g_qkv, g_wo, g_in, jnp.swapaxes(g_out, 1, 2), g_bias, g_gain


def solution(mesh):
    both = ("dp", "ffn")
    P = PartitionSpec
    return jax.shard_map(
        functools.partial(on_device, Cut(mesh.shape["dp"] // 2, mesh.shape["ffn"])),
        mesh=mesh,
        in_specs=(P(both, None), P(both), P(both, None), P(both, None), P(None, "dp", "ffn"),
                  P(None, "ffn", "dp"), P(None, both), P(None, both), P(both, None)),
        out_specs=(P(both, None), P(both, None), P(both, None), P(both, None), P(None, "dp", "ffn"),
                   P(None, "ffn", "dp"), P(None, both), P(None, both)),
        check_vma=False,
    )
```

```python
import functools

import jax
import jax.numpy as jnp
from jax import lax
from jax.experimental import pallas as pl
from jax.experimental.pallas import tpu as pltpu
from jax.sharding import PartitionSpec

f32, bf = jnp.float32, jnp.bfloat16
EPS, NEG = 1e-12, -1e30
SL, D, HEADS, GROUPS, GW, GU = 512, 768, 12, 4, 192, 768
PAIRS = D // 128
R = 256
MESH = pl.DeviceIdType.MESH


def dg(a, b, ca, cb):
    return lax.dot_general(a, b, (((ca,), (cb,)), ((), ())), preferred_element_type=f32)


def nn(a, b):
    return dg(a, b, 1, 0)


def nt(a, b):
    return dg(a, b, 1, 1)


def tn(a, b):
    return dg(a, b, 0, 0)


def win(g):
    return 128 * ((GW * g) // 128)


def off(g):
    return 64 * (g % 2)


def halves(t):
    lane = lax.broadcasted_iota(jnp.int32, t.shape, 1)
    z = jnp.zeros_like(t)
    return jnp.where(lane < 64, t, z), jnp.where(lane < 64, z, t)


def rowsum(x):
    return jnp.sum(x, axis=1, keepdims=True)


def ln_fwd(r):
    c = r - rowsum(r) * (1.0 / D)
    inv = lax.rsqrt(rowsum(c * c) * (1.0 / D) + EPS)
    return c * inv, inv


def ln_bwd(gy, xh, inv, gamma):
    e = gy * gamma
    return inv * (e - rowsum(e) * (1.0 / D) - xh * (rowsum(e * xh) * (1.0 / D)))


def rows_of(i, size):
    return pl.ds(pl.multiple_of(i * size, size), size)


def project(tok, wq, bias, Q, K, V, s):
    rows = rows_of(s, SL)
    for S in range(2):
        b = 384 * S
        y0, y1 = nn(tok[rows, b:b + 256], wq[2 * S]), nn(tok[rows, b + 128:b + 384], wq[2 * S + 1])
        for part, (dst, brow) in enumerate(((Q, 4), (K, None), (V, 5))):
            c = 256 * part
            tiles = (y0[:, c:c + 128], y0[:, c + 128:c + 256] + y1[:, c:c + 128], y1[:, c + 128:c + 256])
            for i, t in enumerate(tiles):
                cols = slice(b + 128 * i, b + 128 * i + 128)
                if brow is not None:
                    t = t + bias[brow:brow + 1, cols]
                t = t.astype(bf)
                if part == 0:
                    t = t * jnp.asarray(0.125, bf)
                dst[rows, cols] = t


def attend(Q, K, V, P, CTX, LI, maskrow, s, p, T=256):
    r0 = pl.multiple_of(s * SL, SL)
    rows, cols = pl.ds(r0, SL), rows_of(p, 128)
    k = K[rows, cols]
    vcat = jnp.concatenate([jnp.concatenate([a, b], 1) for a, b in
                            zip(halves(V[rows, cols]), halves(jnp.ones((SL, 128), bf)))], 0)
    for t in range(SL // T):
        rt = pl.ds(r0 + t * T, T)
        pbs = []
        for h, q in enumerate(halves(Q[rt, cols])):
            sc = nt(q, k) + maskrow
            pb = jnp.exp(sc - jnp.max(sc, axis=1, keepdims=True)).astype(bf)
            P[h, t * T:(t + 1) * T] = pb
            pbs.append(pb)
        r = nn(jnp.concatenate(pbs, 1), vcat)
        li = 1.0 / r[:, 128:]
        CTX[rt, cols] = r[:, :128] * li
        LI[rt, cols] = li.astype(bf)


def attend_back(Q, K, V, P, CTX, DC, s, p, T=256):
    r0 = pl.multiple_of(s * SL, SL)
    rows, cols = pl.ds(r0, SL), rows_of(p, 128)
    q, k, v, dc = Q[rows, cols], K[rows, cols], V[rows, cols], DC[rows, cols]
    kcat = jnp.concatenate(halves(k), 0)
    dss, dq = [[], []], []
    for t in range(SL // T):
        rt = pl.ds(r0 + t * T, T)
        dct = dc[t * T:(t + 1) * T]
        dcs, prods = halves(dct), halves(dct.astype(f32) * CTX[rt, cols])
        row = []
        for h in range(2):
            dp = nt(dcs[h], v) - rowsum(prods[h])
            ds = (P[h, t * T:(t + 1) * T].astype(f32) * dp).astype(bf)
            dss[h].append(ds)
            row.append(ds)
        dq.append((nn(jnp.concatenate(row, 1), kcat) * 0.125).astype(bf))
    dk, dv = [], []
    for h in range(2):
        dk.append(tn(q, jnp.concatenate(dss[h], 0))[64 * h:64 * h + 64])
        dv.append(tn(dc, P[h])[64 * h:64 * h + 64])
    dk, dv = jnp.concatenate(dk, 0).astype(bf).T, jnp.concatenate(dv, 0).astype(bf).T

    def put():
        Q[rows, cols] = jnp.concatenate(dq, 0)
        K[rows, cols] = dk
        V[rows, cols] = dv

    return put


CH = 32


def fold(x):
    return jnp.sum(x.reshape(-1, 8, x.shape[-1]), axis=0)


def gelu_pair(u):
    c = 1.0 + lax.erf(u * 0.7071067811865476)
    return u * c, c + (0.7978845608028654 * u) * jnp.exp2((-0.7213475204444817 * u) * u)


def tile(i, tok, WO, WI, WT, bias, CTX, DC, DR, OB, GB, AB, SLP, H1B, DB, DA, XH, F, INV):
    r0 = pl.multiple_of(i * R, R)
    rows = pl.ds(r0, R)
    parts = [(slice(k, k + CH), pl.ds(r0 + k, CH)) for k in range(0, R, CH)]
    y = nn(CTX[rows, :].astype(bf), WO[...])
    for here, there in parts:
        xh1, inv1 = ln_fwd(y[here] + bias[6:7, :] + tok[there, :].astype(f32))
        XH[0, here, 0:D // 2] = xh1[:, :D // 2].astype(bf)
        XH[1, here, 0:D // 2] = xh1[:, D // 2:].astype(bf)
        INV[here, :] = jnp.broadcast_to(inv1, (CH, 128))
        h1 = xh1 * bias[10:11, :] + bias[7:8, :]
        H1B[here, :] = h1.astype(bf)
        F[here, :] = h1 + bias[8:9, :]
        yield 1
    for g in range(GROUPS):
        w = slice(win(g), win(g) + 256)
        AB[g], SLP[g] = gelu_pair((nn(H1B[:, w], WI[g]) + bias[g:g + 1, :]).astype(bf))
        F[:, w] += nt(AB[g], WT[g])
        yield 0
    sums = [0.0, 0.0, 0.0]
    for here, there in parts:
        xh2, inv2 = ln_fwd(F[here, :])
        y = (xh2 * bias[11:12, :] + bias[9:10, :]).astype(bf)
        OB[0, here, 0:D // 2] = y[:, :D // 2]
        OB[1, here, 0:D // 2] = y[:, D // 2:]
        gy = DC[there, :].astype(f32)
        dr2 = ln_bwd(gy, xh2, inv2, bias[11:12, :])
        F[here, :] = dr2
        DB[here, :] = dr2.astype(bf)
        sums = [s + fold(x) for s, x in zip(sums, (gy * xh2, gy, dr2))]
        yield 1
    for k, s in zip((11, 9, 8), sums):
        GB[k] += s
    for g in range(GROUPS):
        w = slice(win(g), win(g) + 256)
        SLP[g] = nn(DB[:, w], WT[g]).astype(bf) * SLP[g]
        F[:, w] += nt(SLP[g], WI[g])
        yield 0
    sums = [0.0, 0.0, 0.0]
    for here, there in parts:
        xh1 = jnp.concatenate([XH[0, here, 0:D // 2], XH[1, here, 0:D // 2]], 1).astype(f32)
        dh1 = F[here, :]
        dr1 = ln_bwd(dh1, xh1, INV[here, 0:1], bias[10:11, :])
        DA[here, :] = dr1.astype(bf)
        sums = [s + fold(x) for s, x in zip(sums, (dh1 * xh1, dh1, dr1))]
        yield 1
    for k, s in zip((10, 7, 6), sums):
        GB[k] += s
    y = nt(DA[...], WO[...])
    for here, there in parts:
        DC[there, :] = (y[here] * DR[there, :].astype(f32)).astype(bf)
    DR[rows, :] = DA[...]
    yield 0


def weights(i, CTX, G1, G2, G3, GB, AB, SLP, H1B, DB, DA):
    lane = lax.broadcasted_iota(jnp.int32, (R, 256), 1)
    rows = rows_of(i, R)
    for k in range(0, D, 256):
        G3[k:k + 256, :] += tn(CTX[rows, k:k + 256].astype(bf), DA[...])
        yield
    for g in range(GROUPS):
        w = slice(win(g), win(g) + 256)
        o, z = off(g), 0 if off(g) else GW
        mine = jnp.where((lane >= o) & (lane < o + GW), H1B[:, w], jnp.ones((R, 256), bf))
        t = tn(mine, SLP[g])
        G1[g] += t[o:o + GW]
        GB[g, 0:1, :] += t[z:z + 1]
        yield
        G2[g] += tn(DB[:, w], AB[g])[o:o + GW]
        yield


def beside(main, side, count):
    credit = 0.0
    for _ in range(8):
        next(main)
        credit += count / 8
        while credit >= 1:
            credit -= 1
            next(side, None)


def middle(i, tok, WO, WI, WT, bias, CTX, DC, DR, OB, G1, G2, G3, GB, AB, SLP, H1B, DB, DA, XH, F, INV):
    tiles, sides = [], []
    for u in range(2):
        v = 1 - u
        part = slice(u * R, (u + 1) * R)
        tiles.append(tile(2 * i + u, tok, WO, WI, WT, bias, CTX, DC, DR, OB.at[:, part], GB, AB.at[u], SLP.at[u], H1B.at[u],
                          DB.at[u], DA.at[u], XH.at[:, part], F.at[u], INV.at[u]))
        sides.append(weights(jnp.maximum(2 * i + u - 1, 0), CTX, G1, G2, G3, GB, AB.at[v], SLP.at[v], H1B.at[v], DB.at[v], DA.at[v]))
    (a, b), (before, between) = tiles, sides
    beside(a, before, SPLIT)
    for _ in range(4):
        next(a)
    beside(a, before, 11 - SPLIT)
    for _ in before:
        pass
    for _ in range(4):
        next(b)
        next(a)
        next(b)
    for _ in range(4):
        next(a)
        next(b)
        next(a)
    for _ in a:
        pass
    beside(b, between, SPLIT)
    for _ in range(4):
        next(b)
    beside(b, between, 11 - SPLIT)
    for _ in between:
        pass
    for _ in b:
        pass


SPLIT = 5


def qkv_grads(tok, Q, K, V, G1, GB):
    lane = lax.broadcasted_iota(jnp.int32, (tok.shape[0], 256), 1)
    for g in range(GROUPS):
        w = slice(win(g), win(g) + 256)
        o, z = off(g), 0 if off(g) else GW
        mine = jnp.where((lane >= o) & (lane < o + GW), tok[:, w], jnp.ones_like(tok[:, w]))
        t = tn(mine, jnp.concatenate([Q[:, w], K[:, w], V[:, w]], axis=1))
        G1[g] = t[o:o + GW]
        for k, c in ((4, o), (5, 512 + o)):
            GB[k, 0:1, GW * g:GW * (g + 1)] = t[z:z + 1, c:c + GW]


def token_grads(wq, Q, K, V, DR, s):
    rows = rows_of(s, SL)
    for S in range(2):
        b, ys = 384 * S, []
        for g in (2 * S, 2 * S + 1):
            w = slice(win(g), win(g) + 256)
            ys.append(nt(jnp.concatenate([Q[rows, w], K[rows, w], V[rows, w]], axis=1), wq[g]))
        tiles = (ys[0][:, :128], ys[0][:, 128:] + ys[1][:, :128], ys[1][:, 128:])
        for i, t in enumerate(tiles):
            cols = slice(b + 128 * i, b + 128 * i + 128)
            DR[rows, cols] = (t + DR[rows, cols].astype(f32)).astype(bf)


QA, QB, OW, FW = range(4)
GATHER = ("qf", "qf", "fq", "qf")
SCATTER = ("qf", "fq", "fq", "qf")


class Cut:
    def __init__(self, nq, nf):
        self.nq, self.nf = nq, nf
        self.n = 2 * nq * nf
        self.r = D // self.n
        self.a, self.b = GW // (2 * nq), GU // nf
        self.pairs = 3 if self.r % 8 == 0 else 2
        self.shapes = ((self.r, 2 * GW), (self.r, 256), (self.r, D), (2, self.a, GROUPS * self.b))

    def lead(self, i):
        return (self.nq, self.nf) if SCATTER[i] == "qf" else (self.nf, self.nq)

    def place(self, order, q, f):
        return q * self.nf + f if order == "qf" else f * self.nq + q

    def at(self, order, d):
        dp, f = divmod(d, self.nf)
        return dp % 2, self.place(order, dp // 2, f)


def put_pieces(cut, at, qkv, wo, wi, wt, biases, gains, SC, G):
    r = cut.r
    SC[...] = jnp.zeros_like(SC)
    SC[0:10, 0:r] = biases[...].astype(f32)
    SC[10:12, 0:r] = gains[...].astype(f32)
    rows = qkv[...].astype(f32)
    G[QA][at[QA]] = jnp.concatenate([rows[:r], rows[r:2 * r]], 1).astype(bf)
    G[QB][at[QB]] = jnp.concatenate([rows[2 * r:], SC[...].T[:r, :64]], 1).astype(bf)
    G[OW][at[OW]] = wo[...]
    for k, w in enumerate((wi, wt)):
        G[FW][at[FW] + (k,)] = jnp.concatenate([w[g].astype(f32) for g in range(GROUPS)], 1).astype(bf)


def unpack_q(cut, G, WQ, SM):
    WQ[...] = jnp.zeros_like(WQ)
    r = cut.r
    for p in range(3):
        for g in range(GROUPS):
            parts = []
            for i in range(GW // r):
                d, j = divmod((D * p + GW * g) // r + i, 3)
                if j < 2:
                    parts.append(G[QA][cut.at(GATHER[QA], d)].astype(f32)[:, GW * j:GW * (j + 1)])
                else:
                    parts.append(G[QB][cut.at(GATHER[QB], d)].astype(f32)[:, :GW])
            o = off(g)
            WQ[g, o:o + GW, 256 * p + o:256 * p + o + GW] = jnp.concatenate(parts, 0).astype(bf)
    small = jnp.concatenate([G[QB][cut.at(GATHER[QB], d)][:, 128:].astype(f32) for d in range(cut.n)], 0)
    SM[...] = small.T[64:80]


def unpack_o(cut, G, WO):
    per = GW // cut.r
    for i in range(D // GW):
        rows = [G[OW][cut.at(GATHER[OW], d)].astype(f32) for d in range(per * i, per * i + per)]
        WO[GW * i:GW * (i + 1), :] = jnp.concatenate(rows, 0).astype(bf)


def unpack_f(cut, G, WI, WT):
    b = cut.b
    for k, W in enumerate((WI, WT)):
        for g in range(GROUPS):
            o = off(g)
            z = 0 if o else GW
            W[g, z:z + 64] = jnp.zeros((64, GU), bf)
            cols = []
            for f in range(cut.nf):
                cols.append(jnp.concatenate(
                    [G[FW][cut.at(GATHER[FW], dp * cut.nf + f)][k].astype(f32)[:, g * b:(g + 1) * b] for dp in range(2 * cut.nq)], 0))
            w = jnp.concatenate(cols, 1)
            W[g, o:o + GW] = (0.5 * w if k else w).astype(bf)


def pack_o(cut, G3, G):
    for d in range(cut.n):
        G[OW][cut.at(SCATTER[OW], d)] = G3[cut.r * d:cut.r * (d + 1), :].astype(bf)


def pack_f(cut, G1, G2, G):
    a, b = cut.a, cut.b
    for k, grad in enumerate((G1, G2)):
        for dp in range(2 * cut.nq):
            for f in range(cut.nf):
                t = jnp.concatenate([grad[g, a * dp:a * (dp + 1), b * f:b * (f + 1)] for g in range(GROUPS)], 1)
                G[FW][cut.at(SCATTER[FW], dp * cut.nf + f) + (k,)] = (0.5 * t if k else t).astype(bf)


def pack_q(cut, G1, GB, G):
    r = cut.r
    small = jnp.concatenate([jnp.zeros((64, D), f32), jnp.sum(GB[...], axis=1), jnp.zeros((48, D), f32)], 0).T
    for d in range(cut.n):
        parts = []
        for j in range(3):
            p, rest = divmod(r * (3 * d + j), D)
            g, i = divmod(rest, GW)
            c = 256 * p + off(g)
            parts.append(G1[g, i:i + r, c:c + GW])
        G[QA][cut.at(SCATTER[QA], d)] = jnp.concatenate(parts[:2], 1).astype(bf)
        G[QB][cut.at(SCATTER[QB], d)] = jnp.concatenate([parts[2], small[r * d:r * (d + 1), 64:]], 1).astype(bf)


class Links:
    def __init__(self, cut, send_sem, recv_sem):
        self.cut, self.sems = cut, (send_sem, recv_sem)
        dp, self.f = lax.axis_index("dp"), lax.axis_index("ffn")
        self.c, self.q = lax.rem(dp, 2), lax.div(dp, 2)
        nq, nf = cut.nq, cut.nf
        fs = [lax.rem(self.f + k, nf) for k in range(1, nf)]
        qs = [lax.rem(self.q + k, nq) for k in range(1, nq)]
        to_f = [(2 * self.q + self.c, f) for f in fs]
        to_q = [(2 * q + self.c, self.f) for q in qs]
        self.twin = (2 * self.q + 1 - self.c, self.f)
        self.axis = {"q": (self.q, qs, to_q), "f": (self.f, fs, to_f)}
        self.per = nf + nq - 1

    def at(self, i):
        return self.c, self.cut.place(GATHER[i], self.q, self.f)

    def greet(self):
        barrier = pltpu.get_barrier_semaphore()
        everyone = self.axis["q"][2] + self.axis["f"][2] + [self.twin]
        for peer in everyone:
            pl.semaphore_signal(barrier, inc=1, device_id=peer, device_id_type=MESH)
        return lambda: pl.semaphore_wait(barrier, len(everyone))

    def copy(self, src, dst, slot, peer):
        return pltpu.make_async_remote_copy(
            src_ref=src, dst_ref=dst, send_sem=self.sems[0].at[slot], recv_sem=self.sems[1].at[slot],
            device_id=peer, device_id_type=MESH)

    def gather(self, stage, i, G):
        base, c = i * self.per, self.c
        (u, us, to_u), (v, vs, to_v) = (self.axis[x] for x in GATHER[i])
        size = len(vs) + 1
        if stage == 0:
            mine = G.at[c, u * size + v]
            return [self.copy(mine, mine, base + k, to_v[k]) for k in range(len(vs))]
        base += len(vs)
        if stage == 1:
            mine = G.at[c, pl.ds(u * size, size)]
            return [self.copy(mine, mine, base + k, to_u[k]) for k in range(len(us))]
        return [self.copy(G.at[c], G.at[c], base + len(us), self.twin)]

    def scatter(self, stage, i, G, RC, RU, Z, RV):
        base, c = (4 + i) * self.per, self.c
        (u, us, to_u), (v, vs, to_v) = (self.axis[x] for x in SCATTER[i])
        size = len(vs) + 1
        if stage == 0:
            return [self.copy(G.at[1 - c], RC, base, self.twin)]
        base += 1
        if stage == 1:
            return [self.copy(G.at[c, pl.ds(us[k] * size, size)], RU.at[k], base + k, to_u[k]) for k in range(len(us))]
        base += len(us)
        return [self.copy(Z.at[vs[k]], RV.at[k], base + k, to_v[k]) for k in range(len(vs))]

    def add_twin(self, i, G, RC, RU, Z, RV):
        for k in range(RC.shape[0]):
            G[self.c, k] = (G[self.c, k].astype(f32) + RC[k].astype(f32)).astype(bf)

    def add_u(self, i, G, RC, RU, Z, RV):
        size = Z.shape[0]
        total = G[self.c, pl.ds(self.axis[SCATTER[i][0]][0] * size, size)].astype(f32)
        for k in range(RU.shape[0]):
            total = total + RU[k].astype(f32)
        Z[...] = total.astype(bf)

    def add_v(self, i, G, RC, RU, Z, RV):
        total = Z[self.axis[SCATTER[i][1]][0]].astype(f32)
        for k in range(RV.shape[0]):
            total = total + RV[k].astype(f32)
        return total


def start(copies):
    for copy in copies:
        copy.start()


def arrive(copies):
    for copy in copies:
        copy.wait_recv()


def sent(copies):
    for copy in copies:
        copy.wait_send()


def layer(cut, remote, length, *refs):
    count = 6 if remote else 4
    pieces, refs = refs[:count], refs[count:]
    tok_in, cot_in, out, gx, phbm = refs[:5]
    results, refs = refs[5:9], refs[9:]
    tok, DC, Q, K, V, CTX, DR, WQ, WO, WI, WT, SM = refs[:12]
    G, refs = refs[12:16], refs[16:]
    if remote:
        parts, refs = [refs[4 * k:4 * k + 4] for k in range(4)], refs[16:]
        RC, RU, Z, RV = parts
    G1, G2, G3, GB, SC, AB, SLP, H1B, DB, DA, F, INV, PB, in_sem, p_sem, o_sem, x_sem = refs[:17]
    slots = tok.shape[0] // SL
    nmid = tok.shape[0] // (2 * R)
    links = Links(cut, *refs[17:]) if remote else None

    def gather(stage, which):
        return sum((links.gather(stage, i, G[i]) for i in which), [])

    def scatter(stage, which):
        return sum((links.scatter(stage, i, G[i], RC[i], RU[i], Z[i], RV[i]) for i in which), [])

    def add(step, which):
        return [step(i, G[i], RC[i], RU[i], Z[i], RV[i]) for i in which]

    early, late = (QA, QB), (OW, FW)
    if remote:
        met = links.greet()
    loads = [pltpu.make_async_copy(tok_in, tok, in_sem.at[0]), pltpu.make_async_copy(cot_in, DC, in_sem.at[1])]
    start(loads)
    if remote:
        put_pieces(cut, [links.at(i) for i in range(4)], *pieces, SC, G)
        met()
        start(gather(0, early))
    else:
        for src, dst in zip(pieces, G):
            pltpu.sync_copy(src, dst)
    for g in (G1, G2, G3, GB):
        g[...] = jnp.zeros_like(g)
    if remote:
        arrive(gather(0, early))
        start(gather(1, early))
        start(gather(0, (FW,)))
        arrive(gather(1, early))
        start(gather(2, early))
        start(gather(0, (OW,)))
        arrive(gather(2, early))
    unpack_q(cut, G, WQ, SM)
    if remote:
        arrive(gather(0, late))
        start(gather(1, late))
    loads[0].wait()
    lax.fori_loop(0, slots, lambda s, x: (project(tok, WQ, SM, Q, K, V, s), x)[1], 0)

    UP = cut.pairs
    steps = slots * PAIRS // UP

    def to_hbm(i, slot):
        return pltpu.make_async_copy(PB.at[slot], phbm.at[i], p_sem.at[slot])

    def forward(i, x):
        half = lax.rem(i, 2)

        @pl.when(i >= 2)
        def _():
            for u in range(UP):
                to_hbm(UP * i + u, UP * half + u).wait()

        if remote:
            @pl.when(i == steps * 5 // 6)
            def _():
                arrive(gather(1, late))
                start(gather(2, late))

        for u in range(UP):
            pair = UP * i + u
            s = lax.div(pair, PAIRS)
            lane = lax.broadcasted_iota(jnp.int32, (1, SL), 1)
            maskrow = jnp.where(lane < length[s], 0.0, NEG)
            attend(Q, K, V, PB.at[UP * half + u], CTX, DR, maskrow, s, lax.rem(pair, PAIRS))
        for u in range(UP):
            to_hbm(UP * i + u, UP * half + u).start()
        return x

    lax.fori_loop(0, steps, forward, 0)
    if remote:
        arrive(gather(2, late))
    unpack_o(cut, G, WO)
    unpack_f(cut, G, WI, WT)
    loads[1].wait()
    for i in range(max(0, steps - 2), steps):
        for u in range(UP):
            to_hbm(UP * i + u, UP * (i % 2) + u).wait()

    def from_hbm(i, slot):
        return pltpu.make_async_copy(phbm.at[i], PB.at[slot], p_sem.at[slot])

    for u in range(UP):
        from_hbm(u, u).start()

    OB, XH = PB.at[2 * UP - 1], PB.at[2 * UP - 2]

    def out_copy(i):
        return [pltpu.make_async_copy(OB.at[h, :, 0:D // 2], out.at[rows_of(i, 2 * R), h * (D // 2):(h + 1) * (D // 2)], o_sem.at[h])
                for h in range(2)]

    def mid(i, x):
        @pl.when(i >= 1)
        def _():
            for copy in out_copy(i):
                copy.wait()

        middle(i, tok, WO, WI, WT, SM, CTX, DC, DR, OB, G1, G2, G3, GB, AB, SLP, H1B, DB, DA, XH, F, INV)
        start(out_copy(i))
        return x

    for ref in (AB, SLP, H1B, DB, DA):
        ref[1] = jnp.zeros(ref.shape[1:], bf)
    lax.fori_loop(0, nmid, mid, 0)
    for _ in weights(2 * nmid - 1, CTX, G1, G2, G3, GB, AB.at[1], SLP.at[1], H1B.at[1], DB.at[1], DA.at[1]):
        pass
    if remote:
        sent(sum((gather(stage, early + late) for stage in range(3)), []))
    pack_o(cut, G3, G)
    pack_f(cut, G1, G2, G)
    if remote:
        start(scatter(0, late))

    for copy in out_copy(nmid - 1):
        copy.wait()

    def backward(i, x):
        half = lax.rem(i, 2)

        @pl.when(i + 1 < steps)
        def _():
            for u in range(UP):
                from_hbm(UP * i + UP + u, UP - UP * half + u).start()

        if remote:
            @pl.when(i == steps // 4)
            def _():
                arrive(scatter(0, late))
                add(links.add_twin, late)
                start(scatter(1, late))

        for u in range(UP):
            from_hbm(UP * i + u, UP * half + u).wait()
        puts = []
        for u in range(UP):
            pair = UP * i + u
            puts.append(attend_back(Q, K, V, PB.at[UP * half + u], CTX, DC, lax.div(pair, PAIRS), lax.rem(pair, PAIRS)))
        for put in puts:
            put()
        return x

    lax.fori_loop(0, steps, backward, 0)
    if remote:
        arrive(scatter(1, late))
        add(links.add_u, late)
        start(scatter(2, late))
    qkv_grads(tok, Q, K, V, G1, GB)
    pack_q(cut, G1, GB, G)
    if remote:
        start(scatter(0, early))

    def gx_copy(s):
        return pltpu.make_async_copy(DR.at[rows_of(s, SL), :], gx.at[rows_of(s, SL), :], x_sem.at[s])

    def final(s, x):
        if remote:
            @pl.when(s == 1)
            def _():
                arrive(scatter(0, early))
                add(links.add_twin, early)
                start(scatter(1, early))
        token_grads(WQ, Q, K, V, DR, s)
        gx_copy(s).start()
        return x

    lax.fori_loop(0, slots, final, 0)
    if remote:
        arrive(scatter(2, late))
        for i, total in zip(late, add(links.add_v, late)):
            results[i][...] = total
        arrive(scatter(1, early))
        add(links.add_u, early)
        start(scatter(2, early))
        arrive(scatter(2, early))
        for i, total in zip(early, add(links.add_v, early)):
            results[i][...] = total
        sent(sum((scatter(stage, late + early) for stage in range(3)), []))
    else:
        for src, dst in zip(G, results):
            pltpu.sync_copy(src, dst)
    for s in range(slots):
        gx_copy(s).wait()


def run_layer(cut, remote, lengths, pieces, tokens, cotangent):
    rows = tokens.shape[0]
    slots = rows // SL
    vm, hbm = pl.BlockSpec(memory_space=pltpu.VMEM), pl.BlockSpec(memory_space=pl.ANY)
    sd, vmem, dma = jax.ShapeDtypeStruct, pltpu.VMEM, pltpu.SemaphoreType.DMA
    shapes, leads = cut.shapes, [cut.lead(i) for i in range(4)]
    scratch = [vmem((rows, D), bf)] * 5 + [vmem((rows, D), f32), vmem((rows, D), bf)]
    scratch += [vmem((GROUPS, 256, 768), bf), vmem((D, D), bf), vmem((GROUPS, 256, GU), bf), vmem((GROUPS, 256, GU), bf), vmem((16, D), f32)]
    scratch += [vmem((2, u[0] * u[1]) + s, bf) for u, s in zip(leads, shapes)]
    if remote:
        back = list(zip(leads, shapes))
        scratch += [vmem((u[0] * u[1],) + s, bf) for u, s in back]
        scratch += [vmem((u[0] - 1, u[1]) + s, bf) for u, s in back]
        scratch += [vmem(u[1:] + s, bf) for u, s in back]
        scratch += [vmem((u[1] - 1,) + s, bf) for u, s in back]
    scratch += [vmem((GROUPS, GW, GU), f32)] * 2 + [vmem((D, D), f32), vmem((16, 8, D), f32), vmem((128, 128), f32)]
    scratch += [vmem((2, GROUPS, R, GU), bf)] * 2 + [vmem((2, R, D), bf)] * 3 + [vmem((2, R, D), f32), vmem((2, R, 128), f32)]
    scratch += [vmem((2 * cut.pairs, 2, SL, SL), bf), dma((2,)), dma((2 * cut.pairs,)), dma((2,)), dma((slots,))]
    params = dict(vmem_limit_bytes=64 * 1024 * 1024 - 65536)
    if remote:
        count = 8 * (cut.nf + cut.nq - 1)
        scratch += [dma((count,)), dma((count,))]
        params.update(collective_id=0, has_side_effects=True)
    return pl.pallas_call(
        functools.partial(layer, cut, remote),
        out_shape=(sd((rows, D), bf), sd((rows, D), bf), sd((slots * PAIRS, 2, SL, SL), bf))
        + tuple(sd(s, f32) if remote else sd((2, u[0] * u[1]) + s, bf) for u, s in zip(leads, shapes)),
        in_specs=[pl.BlockSpec(memory_space=pltpu.SMEM)] + [vm if remote else hbm] * len(pieces) + [hbm, hbm],
        out_specs=(hbm, hbm, hbm) + (vm if remote else hbm,) * 4,
        scratch_shapes=scratch,
        compiler_params=pltpu.CompilerParams(**params),
    )(lengths, *pieces, tokens, cotangent)


def finish(cut, qa, qb, ow, fw, out, gx, g_qkv, g_in, g_out, g_bias, g_gain, g_wo, out2, gx2, SC):
    r, b = cut.r, cut.b
    out2[...] = out[...]
    gx2[...] = gx[...]

    @pl.when(pl.program_id(0) == 0)
    def _():
        g_qkv[...] = jnp.concatenate([qa[:, :GW], qa[:, GW:], qb[:, :GW]], 0)
        g_wo[...] = ow[...]
        for g in range(GROUPS):
            g_in[g] = fw[0, :, g * b:(g + 1) * b]
            g_out[g] = fw[1, :, g * b:(g + 1) * b]
        SC[...] = jnp.zeros_like(SC)
        SC[0:r, :] = qb[:, 128:]
        small = SC[...].T
        g_bias[...] = small[64:74, 0:r]
        g_gain[...] = small[74:76, 0:r]


def run_finish(cut, parts, out, gx):
    rows = out.shape[0]
    r, a, b = cut.r, cut.a, cut.b
    steps = 2
    sd = jax.ShapeDtypeStruct
    tile = pl.BlockSpec((rows // steps, D), lambda i: (i, 0))

    def whole(shape):
        return pl.BlockSpec(shape, lambda i: (0,) * len(shape))

    small = ((3 * r, GW), (GROUPS, a, b), (GROUPS, a, b), (10, r), (2, r), (r, D))
    return pl.pallas_call(
        functools.partial(finish, cut),
        grid=(steps,),
        out_shape=tuple(sd(s, f32) for s in small) + (sd((rows, D), bf),) * 2,
        in_specs=[whole(p.shape) for p in parts] + [tile, tile],
        out_specs=tuple(whole(s) for s in small) + (tile, tile),
        scratch_shapes=[pltpu.VMEM((128, 128), f32)],
    )(*parts, out, gx)


def on_device(cut, tokens, lengths, qkv_weight, out_weight, ffn_in_weight, ffn_out_weight, biases, gains, cotangent):
    pieces = (qkv_weight, out_weight, ffn_in_weight, jnp.swapaxes(ffn_out_weight, 1, 2), biases, gains)
    out, gx, _, *parts = run_layer(cut, True, lengths, pieces, tokens, cotangent)
    g_qkv, g_in, g_out, g_bias, g_gain, g_wo, out, gx = run_finish(cut, parts, out, gx)
    return out, gx, g_qkv, g_wo, g_in, jnp.swapaxes(g_out, 1, 2), g_bias, g_gain


def solution(mesh):
    both = ("dp", "ffn")
    P = PartitionSpec
    return jax.shard_map(
        functools.partial(on_device, Cut(mesh.shape["dp"] // 2, mesh.shape["ffn"])),
        mesh=mesh,
        in_specs=(P(both, None), P(both), P(both, None), P(both, None), P(None, "dp", "ffn"),
                  P(None, "ffn", "dp"), P(None, both), P(None, both), P(both, None)),
        out_specs=(P(both, None), P(both, None), P(both, None), P(both, None), P(None, "dp", "ffn"),
                   P(None, "ffn", "dp"), P(None, both), P(None, both)),
        check_vma=False,
    )
```

```python
import functools

import jax
import jax.numpy as jnp
from jax import lax
from jax.experimental import pallas as pl
from jax.experimental.pallas import tpu as pltpu
from jax.sharding import PartitionSpec

f32, bf = jnp.float32, jnp.bfloat16
EPS, NEG = 1e-12, -1e30
SL, D, HEADS, GROUPS, GW, GU = 512, 768, 12, 4, 192, 768
PAIRS = D // 128
R = 256
MESH = pl.DeviceIdType.MESH


def dg(a, b, ca, cb):
    return lax.dot_general(a, b, (((ca,), (cb,)), ((), ())), preferred_element_type=f32)


def nn(a, b):
    return dg(a, b, 1, 0)


def nt(a, b):
    return dg(a, b, 1, 1)


def tn(a, b):
    return dg(a, b, 0, 0)


def win(g):
    return 128 * ((GW * g) // 128)


def off(g):
    return 64 * (g % 2)


def halves(t):
    lane = lax.broadcasted_iota(jnp.int32, t.shape, 1)
    z = jnp.zeros_like(t)
    return jnp.where(lane < 64, t, z), jnp.where(lane < 64, z, t)


def rowsum(x):
    return jnp.sum(x, axis=1, keepdims=True)


def ln_fwd(r):
    c = r - rowsum(r) * (1.0 / D)
    inv = lax.rsqrt(rowsum(c * c) * (1.0 / D) + EPS)
    return c * inv, inv


def ln_bwd(gy, xh, inv, gamma):
    e = gy * gamma
    return inv * (e - rowsum(e) * (1.0 / D) - xh * (rowsum(e * xh) * (1.0 / D)))


def rows_of(i, size):
    return pl.ds(pl.multiple_of(i * size, size), size)


def project(tok, wq, bias, Q, K, V, s):
    rows = rows_of(s, SL)
    for S in range(2):
        b = 384 * S
        y0, y1 = nn(tok[rows, b:b + 256], wq[2 * S]), nn(tok[rows, b + 128:b + 384], wq[2 * S + 1])
        for part, (dst, brow) in enumerate(((Q, 4), (K, None), (V, 5))):
            c = 256 * part
            tiles = (y0[:, c:c + 128], y0[:, c + 128:c + 256] + y1[:, c:c + 128], y1[:, c + 128:c + 256])
            for i, t in enumerate(tiles):
                cols = slice(b + 128 * i, b + 128 * i + 128)
                if brow is not None:
                    t = t + bias[brow:brow + 1, cols]
                t = t.astype(bf)
                if part == 0:
                    t = t * jnp.asarray(0.125, bf)
                dst[rows, cols] = t


def attend(Q, K, V, P, CTX, LI, maskrow, s, p, T=256):
    r0 = pl.multiple_of(s * SL, SL)
    rows, cols = pl.ds(r0, SL), rows_of(p, 128)
    k = K[rows, cols]
    vcat = jnp.concatenate([jnp.concatenate([a, b], 1) for a, b in
                            zip(halves(V[rows, cols]), halves(jnp.ones((SL, 128), bf)))], 0)
    for t in range(SL // T):
        rt = pl.ds(r0 + t * T, T)
        pbs = []
        for h, q in enumerate(halves(Q[rt, cols])):
            sc = nt(q, k) + maskrow
            pb = jnp.exp(sc - jnp.max(sc, axis=1, keepdims=True)).astype(bf)
            P[h, t * T:(t + 1) * T] = pb
            pbs.append(pb)
        r = nn(jnp.concatenate(pbs, 1), vcat)
        li = 1.0 / r[:, 128:]
        CTX[rt, cols] = r[:, :128] * li
        LI[rt, cols] = li.astype(bf)


def attend_back(Q, K, V, P, CTX, DC, s, p, T=256):
    r0 = pl.multiple_of(s * SL, SL)
    rows, cols = pl.ds(r0, SL), rows_of(p, 128)
    q, k, v, dc = Q[rows, cols], K[rows, cols], V[rows, cols], DC[rows, cols]
    kcat = jnp.concatenate(halves(k), 0)
    dss, dq = [[], []], []
    for t in range(SL // T):
        rt = pl.ds(r0 + t * T, T)
        dct = dc[t * T:(t + 1) * T]
        dcs, prods = halves(dct), halves(dct.astype(f32) * CTX[rt, cols])
        row = []
        for h in range(2):
            dp = nt(dcs[h], v) - rowsum(prods[h])
            ds = (P[h, t * T:(t + 1) * T].astype(f32) * dp).astype(bf)
            dss[h].append(ds)
            row.append(ds)
        dq.append((nn(jnp.concatenate(row, 1), kcat) * 0.125).astype(bf))
    dk, dv = [], []
    for h in range(2):
        dk.append(tn(q, jnp.concatenate(dss[h], 0))[64 * h:64 * h + 64])
        dv.append(tn(dc, P[h])[64 * h:64 * h + 64])
    dk, dv = jnp.concatenate(dk, 0).astype(bf).T, jnp.concatenate(dv, 0).astype(bf).T

    def put():
        Q[rows, cols] = jnp.concatenate(dq, 0)
        K[rows, cols] = dk
        V[rows, cols] = dv

    return put


CH = 32


def fold(x):
    return jnp.sum(x.reshape(-1, 8, x.shape[-1]), axis=0)


def gelu_pair(u):
    c = 1.0 + lax.erf(u * 0.7071067811865476)
    return u * c, c + (0.7978845608028654 * u) * jnp.exp2((-0.7213475204444817 * u) * u)


def tile(i, tok, WO, WI, WT, bias, CTX, DC, DR, OB, GB, AB, SLP, H1B, DB, DA, XH, F, INV):
    r0 = pl.multiple_of(i * R, R)
    rows = pl.ds(r0, R)
    parts = [(slice(k, k + CH), pl.ds(r0 + k, CH)) for k in range(0, R, CH)]
    y = nn(CTX[rows, :].astype(bf), WO[...])
    for here, there in parts:
        xh1, inv1 = ln_fwd(y[here] + bias[6:7, :] + tok[there, :].astype(f32))
        XH[0, here, 0:D // 2] = xh1[:, :D // 2].astype(bf)
        XH[1, here, 0:D // 2] = xh1[:, D // 2:].astype(bf)
        INV[here, :] = jnp.broadcast_to(inv1, (CH, 128))
        h1 = xh1 * bias[10:11, :] + bias[7:8, :]
        H1B[here, :] = h1.astype(bf)
        F[here, :] = h1 + bias[8:9, :]
        yield 1
    for g in range(GROUPS):
        w = slice(win(g), win(g) + 256)
        AB[g], SLP[g] = gelu_pair((nn(H1B[:, w], WI[g]) + bias[g:g + 1, :]).astype(bf))
        F[:, w] += nt(AB[g], WT[g])
        yield 0
    sums = [0.0, 0.0, 0.0]
    for here, there in parts:
        xh2, inv2 = ln_fwd(F[here, :])
        y = (xh2 * bias[11:12, :] + bias[9:10, :]).astype(bf)
        OB[0, here, 0:D // 2] = y[:, :D // 2]
        OB[1, here, 0:D // 2] = y[:, D // 2:]
        gy = DC[there, :].astype(f32)
        dr2 = ln_bwd(gy, xh2, inv2, bias[11:12, :])
        F[here, :] = dr2
        DB[here, :] = dr2.astype(bf)
        sums = [s + fold(x) for s, x in zip(sums, (gy * xh2, gy, dr2))]
        yield 1
    for k, s in zip((11, 9, 8), sums):
        GB[k] += s
    for g in range(GROUPS):
        w = slice(win(g), win(g) + 256)
        SLP[g] = nn(DB[:, w], WT[g]).astype(bf) * SLP[g]
        F[:, w] += nt(SLP[g], WI[g])
        yield 0
    sums = [0.0, 0.0, 0.0]
    for here, there in parts:
        xh1 = jnp.concatenate([XH[0, here, 0:D // 2], XH[1, here, 0:D // 2]], 1).astype(f32)
        dh1 = F[here, :]
        dr1 = ln_bwd(dh1, xh1, INV[here, 0:1], bias[10:11, :])
        DA[here, :] = dr1.astype(bf)
        sums = [s + fold(x) for s, x in zip(sums, (dh1 * xh1, dh1, dr1))]
        yield 1
    for k, s in zip((10, 7, 6), sums):
        GB[k] += s
    y = nt(DA[...], WO[...])
    for here, there in parts:
        DC[there, :] = (y[here] * DR[there, :].astype(f32)).astype(bf)
    DR[rows, :] = DA[...]
    yield 0


def weights(i, CTX, G1, G2, G3, GB, AB, SLP, H1B, DB, DA):
    lane = lax.broadcasted_iota(jnp.int32, (R, 256), 1)
    rows = rows_of(i, R)
    for k in range(0, D, 256):
        G3[k:k + 256, :] += tn(CTX[rows, k:k + 256].astype(bf), DA[...])
        yield
    for g in range(GROUPS):
        w = slice(win(g), win(g) + 256)
        o, z = off(g), 0 if off(g) else GW
        mine = jnp.where((lane >= o) & (lane < o + GW), H1B[:, w], jnp.ones((R, 256), bf))
        t = tn(mine, SLP[g])
        G1[g] += t[o:o + GW]
        GB[g, 0:1, :] += t[z:z + 1]
        yield
        G2[g] += tn(DB[:, w], AB[g])[o:o + GW]
        yield


def beside(main, side, count):
    credit = 0.0
    for _ in range(8):
        next(main)
        credit += count / 8
        while credit >= 1:
            credit -= 1
            next(side, None)


def middle(i, tok, WO, WI, WT, bias, CTX, DC, DR, OB, G1, G2, G3, GB, AB, SLP, H1B, DB, DA, XH, F, INV):
    tiles, sides = [], []
    for u in range(2):
        v = 1 - u
        part = slice(u * R, (u + 1) * R)
        tiles.append(tile(2 * i + u, tok, WO, WI, WT, bias, CTX, DC, DR, OB.at[:, part], GB, AB.at[u], SLP.at[u], H1B.at[u],
                          DB.at[u], DA.at[u], XH.at[:, part], F.at[u], INV.at[u]))
        sides.append(weights(jnp.maximum(2 * i + u - 1, 0), CTX, G1, G2, G3, GB, AB.at[v], SLP.at[v], H1B.at[v], DB.at[v], DA.at[v]))
    (a, b), (before, between) = tiles, sides
    beside(a, before, SPLIT)
    for _ in range(4):
        next(a)
    beside(a, before, 11 - SPLIT)
    for _ in before:
        pass
    for _ in range(4):
        next(b)
        next(a)
        next(b)
    for _ in range(4):
        next(a)
        next(b)
        next(a)
    for _ in a:
        pass
    beside(b, between, SPLIT)
    for _ in range(4):
        next(b)
    beside(b, between, 11 - SPLIT)
    for _ in between:
        pass
    for _ in b:
        pass


SPLIT = 7


def qkv_grads(tok, Q, K, V, G1, GB):
    lane = lax.broadcasted_iota(jnp.int32, (tok.shape[0], 256), 1)
    for g in range(GROUPS):
        w = slice(win(g), win(g) + 256)
        o, z = off(g), 0 if off(g) else GW
        mine = jnp.where((lane >= o) & (lane < o + GW), tok[:, w], jnp.ones_like(tok[:, w]))
        t = tn(mine, jnp.concatenate([Q[:, w], K[:, w], V[:, w]], axis=1))
        G1[g] = t[o:o + GW]
        for k, c in ((4, o), (5, 512 + o)):
            GB[k, 0:1, GW * g:GW * (g + 1)] = t[z:z + 1, c:c + GW]


def token_grads(wq, Q, K, V, DR, s):
    rows = rows_of(s, SL)
    for S in range(2):
        b, ys = 384 * S, []
        for g in (2 * S, 2 * S + 1):
            w = slice(win(g), win(g) + 256)
            ys.append(nt(jnp.concatenate([Q[rows, w], K[rows, w], V[rows, w]], axis=1), wq[g]))
        tiles = (ys[0][:, :128], ys[0][:, 128:] + ys[1][:, :128], ys[1][:, 128:])
        for i, t in enumerate(tiles):
            cols = slice(b + 128 * i, b + 128 * i + 128)
            DR[rows, cols] = (t + DR[rows, cols].astype(f32)).astype(bf)


QA, QB, OW, FW = range(4)
GATHER = ("qf", "qf", "fq", "qf")
SCATTER = ("qf", "fq", "fq", "qf")


class Cut:
    def __init__(self, nq, nf):
        self.nq, self.nf = nq, nf
        self.n = 2 * nq * nf
        self.r = D // self.n
        self.a, self.b = GW // (2 * nq), GU // nf
        self.pairs = 3 if self.r % 8 == 0 else 2
        self.shapes = ((self.r, 2 * GW), (self.r, 256), (self.r, D), (2, self.a, GROUPS * self.b))

    def lead(self, i):
        return (self.nq, self.nf) if SCATTER[i] == "qf" else (self.nf, self.nq)

    def place(self, order, q, f):
        return q * self.nf + f if order == "qf" else f * self.nq + q

    def at(self, order, d):
        dp, f = divmod(d, self.nf)
        return dp % 2, self.place(order, dp // 2, f)


def put_pieces(cut, at, qkv, wo, wi, wt, biases, gains, SC, G):
    r = cut.r
    SC[...] = jnp.zeros_like(SC)
    SC[0:10, 0:r] = biases[...].astype(f32)
    SC[10:12, 0:r] = gains[...].astype(f32)
    rows = qkv[...].astype(f32)
    G[QA][at[QA]] = jnp.concatenate([rows[:r], rows[r:2 * r]], 1).astype(bf)
    G[QB][at[QB]] = jnp.concatenate([rows[2 * r:], SC[...].T[:r, :64]], 1).astype(bf)
    G[OW][at[OW]] = wo[...]
    for k, w in enumerate((wi, wt)):
        G[FW][at[FW] + (k,)] = jnp.concatenate([w[g].astype(f32) for g in range(GROUPS)], 1).astype(bf)


def unpack_q(cut, G, WQ, SM):
    WQ[...] = jnp.zeros_like(WQ)
    r = cut.r
    for p in range(3):
        for g in range(GROUPS):
            parts = []
            for i in range(GW // r):
                d, j = divmod((D * p + GW * g) // r + i, 3)
                if j < 2:
                    parts.append(G[QA][cut.at(GATHER[QA], d)].astype(f32)[:, GW * j:GW * (j + 1)])
                else:
                    parts.append(G[QB][cut.at(GATHER[QB], d)].astype(f32)[:, :GW])
            o = off(g)
            WQ[g, o:o + GW, 256 * p + o:256 * p + o + GW] = jnp.concatenate(parts, 0).astype(bf)
    small = jnp.concatenate([G[QB][cut.at(GATHER[QB], d)][:, 128:].astype(f32) for d in range(cut.n)], 0)
    SM[...] = small.T[64:80]


def unpack_o(cut, G, WO):
    per = GW // cut.r
    for i in range(D // GW):
        rows = [G[OW][cut.at(GATHER[OW], d)].astype(f32) for d in range(per * i, per * i + per)]
        WO[GW * i:GW * (i + 1), :] = jnp.concatenate(rows, 0).astype(bf)


def unpack_f(cut, G, WI, WT):
    b = cut.b
    for k, W in enumerate((WI, WT)):
        for g in range(GROUPS):
            o = off(g)
            z = 0 if o else GW
            W[g, z:z + 64] = jnp.zeros((64, GU), bf)
            cols = []
            for f in range(cut.nf):
                cols.append(jnp.concatenate(
                    [G[FW][cut.at(GATHER[FW], dp * cut.nf + f)][k].astype(f32)[:, g * b:(g + 1) * b] for dp in range(2 * cut.nq)], 0))
            w = jnp.concatenate(cols, 1)
            W[g, o:o + GW] = (0.5 * w if k else w).astype(bf)


def pack_o(cut, G3, G):
    for d in range(cut.n):
        G[OW][cut.at(SCATTER[OW], d)] = G3[cut.r * d:cut.r * (d + 1), :].astype(bf)


def pack_f(cut, G1, G2, G):
    a, b = cut.a, cut.b
    for k, grad in enumerate((G1, G2)):
        for dp in range(2 * cut.nq):
            for f in range(cut.nf):
                t = jnp.concatenate([grad[g, a * dp:a * (dp + 1), b * f:b * (f + 1)] for g in range(GROUPS)], 1)
                G[FW][cut.at(SCATTER[FW], dp * cut.nf + f) + (k,)] = (0.5 * t if k else t).astype(bf)


def pack_q(cut, G1, GB, G):
    r = cut.r
    small = jnp.concatenate([jnp.zeros((64, D), f32), jnp.sum(GB[...], axis=1), jnp.zeros((48, D), f32)], 0).T
    for d in range(cut.n):
        parts = []
        for j in range(3):
            p, rest = divmod(r * (3 * d + j), D)
            g, i = divmod(rest, GW)
            c = 256 * p + off(g)
            parts.append(G1[g, i:i + r, c:c + GW])
        G[QA][cut.at(SCATTER[QA], d)] = jnp.concatenate(parts[:2], 1).astype(bf)
        G[QB][cut.at(SCATTER[QB], d)] = jnp.concatenate([parts[2], small[r * d:r * (d + 1), 64:]], 1).astype(bf)


class Links:
    def __init__(self, cut, send_sem, recv_sem):
        self.cut, self.sems = cut, (send_sem, recv_sem)
        dp, self.f = lax.axis_index("dp"), lax.axis_index("ffn")
        self.c, self.q = lax.rem(dp, 2), lax.div(dp, 2)
        nq, nf = cut.nq, cut.nf
        fs = [lax.rem(self.f + k, nf) for k in range(1, nf)]
        qs = [lax.rem(self.q + k, nq) for k in range(1, nq)]
        to_f = [(2 * self.q + self.c, f) for f in fs]
        to_q = [(2 * q + self.c, self.f) for q in qs]
        self.twin = (2 * self.q + 1 - self.c, self.f)
        self.axis = {"q": (self.q, qs, to_q), "f": (self.f, fs, to_f)}
        self.per = nf + nq - 1

    def at(self, i):
        return self.c, self.cut.place(GATHER[i], self.q, self.f)

    def greet(self):
        barrier = pltpu.get_barrier_semaphore()
        everyone = self.axis["q"][2] + self.axis["f"][2] + [self.twin]
        for peer in everyone:
            pl.semaphore_signal(barrier, inc=1, device_id=peer, device_id_type=MESH)
        return lambda: pl.semaphore_wait(barrier, len(everyone))

    def copy(self, src, dst, slot, peer):
        return pltpu.make_async_remote_copy(
            src_ref=src, dst_ref=dst, send_sem=self.sems[0].at[slot], recv_sem=self.sems[1].at[slot],
            device_id=peer, device_id_type=MESH)

    def gather(self, stage, i, G):
        base, c = i * self.per, self.c
        (u, us, to_u), (v, vs, to_v) = (self.axis[x] for x in GATHER[i])
        size = len(vs) + 1
        if stage == 0:
            mine = G.at[c, u * size + v]
            return [self.copy(mine, mine, base + k, to_v[k]) for k in range(len(vs))]
        base += len(vs)
        if stage == 1:
            mine = G.at[c, pl.ds(u * size, size)]
            return [self.copy(mine, mine, base + k, to_u[k]) for k in range(len(us))]
        return [self.copy(G.at[c], G.at[c], base + len(us), self.twin)]

    def scatter(self, stage, i, G, RC, RU, Z, RV):
        base, c = (4 + i) * self.per, self.c
        (u, us, to_u), (v, vs, to_v) = (self.axis[x] for x in SCATTER[i])
        size = len(vs) + 1
        if stage == 0:
            return [self.copy(G.at[1 - c], RC, base, self.twin)]
        base += 1
        if stage == 1:
            return [self.copy(G.at[c, pl.ds(us[k] * size, size)], RU.at[k], base + k, to_u[k]) for k in range(len(us))]
        base += len(us)
        return [self.copy(Z.at[vs[k]], RV.at[k], base + k, to_v[k]) for k in range(len(vs))]

    def add_twin(self, i, G, RC, RU, Z, RV):
        for k in range(RC.shape[0]):
            G[self.c, k] = (G[self.c, k].astype(f32) + RC[k].astype(f32)).astype(bf)

    def add_u(self, i, G, RC, RU, Z, RV):
        size = Z.shape[0]
        total = G[self.c, pl.ds(self.axis[SCATTER[i][0]][0] * size, size)].astype(f32)
        for k in range(RU.shape[0]):
            total = total + RU[k].astype(f32)
        Z[...] = total.astype(bf)

    def add_v(self, i, G, RC, RU, Z, RV):
        total = Z[self.axis[SCATTER[i][1]][0]].astype(f32)
        for k in range(RV.shape[0]):
            total = total + RV[k].astype(f32)
        return total


def start(copies):
    for copy in copies:
        copy.start()


def arrive(copies):
    for copy in copies:
        copy.wait_recv()


def sent(copies):
    for copy in copies:
        copy.wait_send()


def layer(cut, remote, length, *refs):
    count = 6 if remote else 4
    pieces, refs = refs[:count], refs[count:]
    tok_in, cot_in, out, gx, phbm = refs[:5]
    results, refs = refs[5:9], refs[9:]
    tok, DC, Q, K, V, CTX, DR, WQ, WO, WI, WT, SM = refs[:12]
    G, refs = refs[12:16], refs[16:]
    if remote:
        parts, refs = [refs[4 * k:4 * k + 4] for k in range(4)], refs[16:]
        RC, RU, Z, RV = parts
    G1, G2, G3, GB, SC, AB, SLP, H1B, DB, DA, F, INV, PB, in_sem, p_sem, o_sem, x_sem = refs[:17]
    slots = tok.shape[0] // SL
    nmid = tok.shape[0] // (2 * R)
    links = Links(cut, *refs[17:]) if remote else None

    def gather(stage, which):
        return sum((links.gather(stage, i, G[i]) for i in which), [])

    def scatter(stage, which):
        return sum((links.scatter(stage, i, G[i], RC[i], RU[i], Z[i], RV[i]) for i in which), [])

    def add(step, which):
        return [step(i, G[i], RC[i], RU[i], Z[i], RV[i]) for i in which]

    early, late = (QA, QB), (OW, FW)
    if remote:
        met = links.greet()
    loads = [pltpu.make_async_copy(tok_in, tok, in_sem.at[0]), pltpu.make_async_copy(cot_in, DC, in_sem.at[1])]
    start(loads)
    if remote:
        put_pieces(cut, [links.at(i) for i in range(4)], *pieces, SC, G)
        met()
        start(gather(0, early))
    else:
        for src, dst in zip(pieces, G):
            pltpu.sync_copy(src, dst)
    for g in (G1, G2, G3, GB):
        g[...] = jnp.zeros_like(g)
    if remote:
        arrive(gather(0, early))
        start(gather(1, early))
        start(gather(0, (FW,)))
        arrive(gather(1, early))
        start(gather(2, early))
        start(gather(0, (OW,)))
        arrive(gather(2, early))
    unpack_q(cut, G, WQ, SM)
    if remote:
        arrive(gather(0, late))
        start(gather(1, late))
    loads[0].wait()
    for s in range(slots):
        project(tok, WQ, SM, Q, K, V, s)

    UP = cut.pairs
    steps = slots * PAIRS // UP

    def to_hbm(i, slot):
        return pltpu.make_async_copy(PB.at[slot], phbm.at[i], p_sem.at[slot])

    def forward(i, x):
        half = lax.rem(i, 2)

        @pl.when(i >= 2)
        def _():
            for u in range(UP):
                to_hbm(UP * i + u, UP * half + u).wait()

        if remote:
            @pl.when(i == steps * 5 // 6)
            def _():
                arrive(gather(1, late))
                start(gather(2, late))

        for u in range(UP):
            pair = UP * i + u
            s = lax.div(pair, PAIRS)
            lane = lax.broadcasted_iota(jnp.int32, (1, SL), 1)
            maskrow = jnp.where(lane < length[s], 0.0, NEG)
            attend(Q, K, V, PB.at[UP * half + u], CTX, DR, maskrow, s, lax.rem(pair, PAIRS))
        for u in range(UP):
            to_hbm(UP * i + u, UP * half + u).start()
        return x

    lax.fori_loop(0, steps, forward, 0)
    if remote:
        arrive(gather(2, late))
    unpack_o(cut, G, WO)
    unpack_f(cut, G, WI, WT)
    loads[1].wait()
    for i in range(max(0, steps - 2), steps):
        for u in range(UP):
            to_hbm(UP * i + u, UP * (i % 2) + u).wait()

    def from_hbm(i, slot):
        return pltpu.make_async_copy(phbm.at[i], PB.at[slot], p_sem.at[slot])

    for u in range(UP):
        from_hbm(u, u).start()

    OB, XH = PB.at[2 * UP - 1], PB.at[2 * UP - 2]

    def out_copy(i):
        return [pltpu.make_async_copy(OB.at[h, :, 0:D // 2], out.at[rows_of(i, 2 * R), h * (D // 2):(h + 1) * (D // 2)], o_sem.at[h])
                for h in range(2)]

    def mid(i, x):
        @pl.when(i >= 1)
        def _():
            for copy in out_copy(i):
                copy.wait()

        middle(i, tok, WO, WI, WT, SM, CTX, DC, DR, OB, G1, G2, G3, GB, AB, SLP, H1B, DB, DA, XH, F, INV)
        start(out_copy(i))
        return x

    for ref in (AB, SLP, H1B, DB, DA):
        ref[1] = jnp.zeros(ref.shape[1:], bf)
    lax.fori_loop(0, nmid, mid, 0)
    if remote:
        sent(sum((gather(stage, early + late) for stage in range(3)), []))
    rest = weights(2 * nmid - 1, CTX, G1, G2, G3, GB, AB.at[1], SLP.at[1], H1B.at[1], DB.at[1], DA.at[1])
    for _ in range(D // 256):
        next(rest)
    pack_o(cut, G3, G)
    if remote:
        start(scatter(0, (OW,)))
    for _ in rest:
        pass
    pack_f(cut, G1, G2, G)
    if remote:
        start(scatter(0, (FW,)))

    for copy in out_copy(nmid - 1):
        copy.wait()

    def backward(i, x):
        half = lax.rem(i, 2)

        @pl.when(i + 1 < steps)
        def _():
            for u in range(UP):
                from_hbm(UP * i + UP + u, UP - UP * half + u).start()

        if remote:
            @pl.when(i == steps // 4)
            def _():
                arrive(scatter(0, late))
                add(links.add_twin, late)
                start(scatter(1, late))

        for u in range(UP):
            from_hbm(UP * i + u, UP * half + u).wait()
        puts = []
        for u in range(UP):
            pair = UP * i + u
            puts.append(attend_back(Q, K, V, PB.at[UP * half + u], CTX, DC, lax.div(pair, PAIRS), lax.rem(pair, PAIRS)))
        for put in puts:
            put()
        return x

    lax.fori_loop(0, steps, backward, 0)
    if remote:
        arrive(scatter(1, late))
        add(links.add_u, late)
        start(scatter(2, late))
    qkv_grads(tok, Q, K, V, G1, GB)
    pack_q(cut, G1, GB, G)
    if remote:
        start(scatter(0, early))

    def gx_copy(s):
        return pltpu.make_async_copy(DR.at[rows_of(s, SL), :], gx.at[rows_of(s, SL), :], x_sem.at[s])

    def final(s, x):
        if remote:
            @pl.when(s == 1)
            def _():
                arrive(scatter(0, early))
                add(links.add_twin, early)
                start(scatter(1, early))
        token_grads(WQ, Q, K, V, DR, s)
        gx_copy(s).start()
        return x

    lax.fori_loop(0, slots, final, 0)
    if remote:
        arrive(scatter(2, late))
        for i, total in zip(late, add(links.add_v, late)):
            results[i][...] = total
        arrive(scatter(1, early))
        add(links.add_u, early)
        start(scatter(2, early))
        arrive(scatter(2, early))
        for i, total in zip(early, add(links.add_v, early)):
            results[i][...] = total
        sent(sum((scatter(stage, late + early) for stage in range(3)), []))
    else:
        for src, dst in zip(G, results):
            pltpu.sync_copy(src, dst)
    for s in range(slots):
        gx_copy(s).wait()


def run_layer(cut, remote, lengths, pieces, tokens, cotangent):
    rows = tokens.shape[0]
    slots = rows // SL
    vm, hbm = pl.BlockSpec(memory_space=pltpu.VMEM), pl.BlockSpec(memory_space=pl.ANY)
    sd, vmem, dma = jax.ShapeDtypeStruct, pltpu.VMEM, pltpu.SemaphoreType.DMA
    shapes, leads = cut.shapes, [cut.lead(i) for i in range(4)]
    scratch = [vmem((rows, D), bf)] * 5 + [vmem((rows, D), f32), vmem((rows, D), bf)]
    scratch += [vmem((GROUPS, 256, 768), bf), vmem((D, D), bf), vmem((GROUPS, 256, GU), bf), vmem((GROUPS, 256, GU), bf), vmem((16, D), f32)]
    scratch += [vmem((2, u[0] * u[1]) + s, bf) for u, s in zip(leads, shapes)]
    if remote:
        back = list(zip(leads, shapes))
        scratch += [vmem((u[0] * u[1],) + s, bf) for u, s in back]
        scratch += [vmem((u[0] - 1, u[1]) + s, bf) for u, s in back]
        scratch += [vmem(u[1:] + s, bf) for u, s in back]
        scratch += [vmem((u[1] - 1,) + s, bf) for u, s in back]
    scratch += [vmem((GROUPS, GW, GU), f32)] * 2 + [vmem((D, D), f32), vmem((16, 8, D), f32), vmem((128, 128), f32)]
    scratch += [vmem((2, GROUPS, R, GU), bf)] * 2 + [vmem((2, R, D), bf)] * 3 + [vmem((2, R, D), f32), vmem((2, R, 128), f32)]
    scratch += [vmem((2 * cut.pairs, 2, SL, SL), bf), dma((2,)), dma((2 * cut.pairs,)), dma((2,)), dma((slots,))]
    params = dict(vmem_limit_bytes=64 * 1024 * 1024 - 65536)
    if remote:
        count = 8 * (cut.nf + cut.nq - 1)
        scratch += [dma((count,)), dma((count,))]
        params.update(collective_id=0, has_side_effects=True)
    return pl.pallas_call(
        functools.partial(layer, cut, remote),
        out_shape=(sd((rows, D), bf), sd((rows, D), bf), sd((slots * PAIRS, 2, SL, SL), bf))
        + tuple(sd(s, f32) if remote else sd((2, u[0] * u[1]) + s, bf) for u, s in zip(leads, shapes)),
        in_specs=[pl.BlockSpec(memory_space=pltpu.SMEM)] + [vm if remote else hbm] * len(pieces) + [hbm, hbm],
        out_specs=(hbm, hbm, hbm) + (vm if remote else hbm,) * 4,
        scratch_shapes=scratch,
        compiler_params=pltpu.CompilerParams(**params),
    )(lengths, *pieces, tokens, cotangent)


def finish(cut, qa, qb, ow, fw, out, gx, g_qkv, g_in, g_out, g_bias, g_gain, g_wo, out2, gx2, SC):
    r, b = cut.r, cut.b
    out2[...] = out[...]
    gx2[...] = gx[...]

    @pl.when(pl.program_id(0) == 0)
    def _():
        g_qkv[...] = jnp.concatenate([qa[:, :GW], qa[:, GW:], qb[:, :GW]], 0)
        g_wo[...] = ow[...]
        for g in range(GROUPS):
            g_in[g] = fw[0, :, g * b:(g + 1) * b]
            g_out[g] = fw[1, :, g * b:(g + 1) * b]
        SC[...] = jnp.zeros_like(SC)
        SC[0:r, :] = qb[:, 128:]
        small = SC[...].T
        g_bias[...] = small[64:74, 0:r]
        g_gain[...] = small[74:76, 0:r]


def run_finish(cut, parts, out, gx):
    rows = out.shape[0]
    r, a, b = cut.r, cut.a, cut.b
    steps = 2
    sd = jax.ShapeDtypeStruct
    tile = pl.BlockSpec((rows // steps, D), lambda i: (i, 0))

    def whole(shape):
        return pl.BlockSpec(shape, lambda i: (0,) * len(shape))

    small = ((3 * r, GW), (GROUPS, a, b), (GROUPS, a, b), (10, r), (2, r), (r, D))
    return pl.pallas_call(
        functools.partial(finish, cut),
        grid=(steps,),
        out_shape=tuple(sd(s, f32) for s in small) + (sd((rows, D), bf),) * 2,
        in_specs=[whole(p.shape) for p in parts] + [tile, tile],
        out_specs=tuple(whole(s) for s in small) + (tile, tile),
        scratch_shapes=[pltpu.VMEM((128, 128), f32)],
    )(*parts, out, gx)


def on_device(cut, tokens, lengths, qkv_weight, out_weight, ffn_in_weight, ffn_out_weight, biases, gains, cotangent):
    pieces = (qkv_weight, out_weight, ffn_in_weight, jnp.swapaxes(ffn_out_weight, 1, 2), biases, gains)
    out, gx, _, *parts = run_layer(cut, True, lengths, pieces, tokens, cotangent)
    g_qkv, g_in, g_out, g_bias, g_gain, g_wo, out, gx = run_finish(cut, parts, out, gx)
    return out, gx, g_qkv, g_wo, g_in, jnp.swapaxes(g_out, 1, 2), g_bias, g_gain


def solution(mesh):
    both = ("dp", "ffn")
    P = PartitionSpec
    return jax.shard_map(
        functools.partial(on_device, Cut(mesh.shape["dp"] // 2, mesh.shape["ffn"])),
        mesh=mesh,
        in_specs=(P(both, None), P(both), P(both, None), P(both, None), P(None, "dp", "ffn"),
                  P(None, "ffn", "dp"), P(None, both), P(None, both), P(both, None)),
        out_specs=(P(both, None), P(both, None), P(both, None), P(both, None), P(None, "dp", "ffn"),
                   P(None, "ffn", "dp"), P(None, both), P(None, both)),
        check_vma=False,
    )
```
